32 devices in a mesh: rep: 4 (over x, core), shard: 8 (over z, y).
Axes of the slice: x: 2, y: 2, z: 4, core: 2. Of those that a mesh axis runs over, the one named last changes fastest.
Arguments:
- tokens: bfloat16 [20480, 1536], P(('rep', 'shard')), may hold values from -6 to 6
- norm_gains: bfloat16 [2, 1536], P(None, 'shard'), may hold values from 0.25 to 1.75
- qkv_weight: bfloat16 [1536, 2560], P('shard'), may hold values from -0.21875 to 0.21875
- out_weight: bfloat16 [1536, 1536], P('shard'), may hold values from -0.625 to 0.625
- router_weight: bfloat16 [1536, 16], P('shard'), may hold values from -0.078125 to 0.078125
- gate_up_weight: bfloat16 [16, 1536, 1024], P(None, 'shard'), may hold values from -0.15625 to 0.15625
- down_weight: bfloat16 [16, 512, 1536], P(None, 'shard'), may hold values from -1 to 1
- routes: int32 [20480, 8], P(('rep', 'shard')), may hold values from 0 to 15, all different within a row; in each aligned block of 640 rows (0 to 639, 640 to 1279, ...) at most 352 rows name the same one
- placement: int32 [160], replicated, may hold values from 0 to 19, as said below
- parents: int32 [8, 20], replicated, may hold values from 0 to 11, as said below
- cotangent: bfloat16 [20480, 1536], P(('rep', 'shard')), may hold values from -6 to 6
Outputs:
- block_out: bfloat16 [20480, 1536], P(('rep', 'shard'))
- token_grad: float32 [20480, 1536], P(('rep', 'shard'))
- gains_grad: float32 [2, 1536], P(None, 'shard')
- qkv_grad: float32 [1536, 2560], P('shard')
- out_grad: float32 [1536, 1536], P('shard')
- router_grad: float32 [1536, 16], P('shard')
- gate_up_grad: float32 [16, 1536, 1024], P(None, 'shard')
- down_grad: float32 [16, 512, 1536], P(None, 'shard')
The draws below stay inside these ranges and needn't reach their ends.
Inputs may be any that keep to these rules, and one draw needn't show every extreme that they name: `routes`: in the rows of one device no expert is named by more than 352 rows, a bound that some block reaches. `placement`: each aligned run of 20 entries holds every number of its range once. `parents`: in every row, segment 0 is its own parent, segments 1 to 7 have the parent one less, segments 8 to 11 have the parent 8 - 1, and every other segment has one of those branch segments as parent; every branch segment is some segment's parent.
All inputs are finite; a program needn't handle non-finite values.
Results may differ from the reference program's by a relative error of at most 0.019.
Values may be sent and summed in bfloat16 or wider, within the bound.
A program may use at most 448 MiB of HBM per device.

```python
import math
import jax
import jax.numpy as jnp
import numpy as np
from jax import lax

D = 1536
H = 24
KVH = 8
HD = 64
FF = 512
TOP = 8
E = 16
SEG = 128
TRUNK = 8
BRANCH = 4
TREE_DEVS = 4
TREE_SEGS = 20
SEG_DEV = 5
TOK_DEV = 640
CAP = 352
TOKENS = 20480
TREES = 8


def draw_placement(key, part):
    width = TREE_DEVS * SEG_DEV
    runs = TOKENS // (SEG * width)
    keys = jax.random.split(key, runs)
    orders = jax.vmap(lambda one_key: jax.random.permutation(one_key, width))(keys)
    return orders.reshape(-1).astype(jnp.int32)


def draw_parents(key, part):
    index = jnp.arange(TREE_SEGS, dtype=jnp.int32)
    trunk_part = jnp.maximum(index - 1, 0)
    fixed_part = jnp.where(index < TRUNK, trunk_part, TRUNK - 1)
    shift = jax.random.randint(jax.random.fold_in(key, 1), (TREES, 1), 0, BRANCH, dtype=jnp.int32)
    spread = jax.random.randint(jax.random.fold_in(key, 2), (TREES, TREE_SEGS), 0, BRANCH, dtype=jnp.int32)
    leaf_rank = index - TRUNK - BRANCH
    covered = TRUNK + (leaf_rank[None, :] + shift) % BRANCH
    leaf_part = jnp.where(leaf_rank[None, :] < BRANCH, covered, TRUNK + spread)
    return jnp.where(index[None, :] < TRUNK + BRANCH, fixed_part[None, :], leaf_part).astype(jnp.int32)


def levels(key, shape, cuts, least, high):
    def one(axis_at, blocks):
        steps = jax.random.uniform(jax.random.fold_in(jax.random.fold_in(key, 6), axis_at), (blocks,), jnp.float32, least / len(cuts), high / len(cuts))
        return jnp.repeat(jnp.exp(steps), shape[axis_at] // blocks).reshape((-1,) + (1,) * (len(shape) - axis_at - 1))

    factor_of = one(*cuts[0])
    for cut in cuts[1:]:
        factor_of = factor_of * one(*cut)
    return factor_of


def shared_out(key, own, number, rows, count, top, reach, skew):
    order = jax.random.permutation(key, count)
    heavy_load, ordinary = load_shares(count, rows * top, reach, skew, True), load_shares(count, rows * top, reach, skew, False)
    places = jnp.arange(count)

    def named(sizes, rotation):
        used = int((sizes > 0).sum())
        fixed = max(1, used // 4)
        moved = fixed + (places - fixed + rotation * (used - fixed)) % max(1, count - fixed)
        return jnp.zeros((count,), jnp.int32).at[order[jnp.where(places < fixed, places, moved)]].set(jnp.asarray(sizes, jnp.int32))

    sizes = jnp.where(number % 4 == 0, named(heavy_load, number // 4), named(ordinary, number - number // 4 - 1))
    mixed = jax.random.permutation(jax.random.fold_in(own, 3), count)
    donor, sink = mixed[0:count // 2 * 2:2], mixed[1:count // 2 * 2:2]
    slack = jnp.minimum(sizes[donor] - 1, reach - sizes[sink]) // 2
    slack = jnp.where((donor == order[0]) | (sink == order[0]) | (sizes[sink] == 0), 0, jnp.maximum(slack, 0))
    moved = jax.random.randint(jax.random.fold_in(own, 4), (count // 2,), 0, 1 << 20) % (slack + 1)
    sizes = sizes.at[donor].add(-moved).at[sink].add(moved)
    items = jnp.searchsorted(jnp.cumsum(sizes), jnp.arange(rows * top), side="right").astype(jnp.int32)
    listing = items.reshape(top, rows).T
    listing = listing[jax.random.permutation(jax.random.fold_in(own, 1), rows)]
    rotation = jax.random.randint(jax.random.fold_in(own, 2), (rows, 1), 0, top)
    return jnp.take_along_axis(listing, (jnp.arange(top)[None, :] + rotation) % top, axis=1)


def load_shares(count, total, limit, lean, full):
    loads = [(1 << 20) // math.isqrt(grade ** lean) + 1 for grade in range(1, count + 1)]
    largest = limit if full else min(limit, max(-(-total // count), total * loads[0] // sum(loads)))
    least = 1 if total - largest >= count - 1 else 0
    holding, surplus = [largest] + [least] * (count - 1), total - largest - least * (count - 1)
    while surplus > 0:
        movable = [i for i in range(1, count) if holding[i] < largest] or [i for i in range(1, count) if holding[i] < limit]
        pool, left = sum([loads[i] for i in movable]), surplus
        for i in movable:
            more = min(limit - holding[i], max(1, left * loads[i] // pool), surplus)
            holding[i] = holding[i] + more
            surplus = surplus - more
    return np.array(holding)


def bell_draw(own_key, shape, scale, bound, shards=(), kind=jnp.bfloat16):
    level = levels(own_key, shape, shards, -0.22, 0.18) if shards else 1.0
    values = jax.random.normal(own_key, shape, jnp.float32) * scale * level
    return jnp.minimum(jnp.maximum(values, -bound), bound).astype(kind)


def setup_inputs(seed: int = 0) -> dict:
    key_of = jax.random.split(jax.random.key(seed), 12)
    tokens = bell_draw(key_of[0], (TOKENS, D), 1.0, 6.0, ((0, 32),))
    norm_gains = jnp.clip(1.0 + 0.15 * jax.random.normal(key_of[1], (2, D), jnp.float32), 0.25, 1.75).astype(jnp.bfloat16)
    qkv_weight = bell_draw(key_of[2], (D, 2 * H * HD + 2 * KVH * HD - H * HD), (D // 2) ** -0.5, 0.21875, ((0, 8),))
    out_weight = bell_draw(key_of[3], (H * HD, D), (H * HD // 16) ** -0.5, 0.625, ((0, 8),))
    router_weight = bell_draw(key_of[4], (D, E), (4 * D) ** -0.5, 0.078125, ((0, 8),))
    gate_up_weight = bell_draw(key_of[5], (E, D, 2 * FF), D ** -0.5, 0.15625, ((1, 8),))
    down_weight = bell_draw(key_of[6], (E, FF, D), (FF // 16) ** -0.5, 1.0, ((1, 8),))
    routes_keys = jax.random.split(jax.random.fold_in(key_of[7], 1), TOKENS // TOK_DEV)
    routes_turns = jax.random.permutation(jax.random.fold_in(key_of[7], 3), TOKENS // TOK_DEV)
    routes = jax.vmap(lambda own, number: shared_out(jax.random.fold_in(key_of[7], 2), own, number, TOK_DEV, E, TOP, CAP, 1))(routes_keys, routes_turns).reshape((TOKENS, TOP))
    placement = draw_placement(jax.random.fold_in(key_of[11], 71), 0)
    parents = draw_parents(jax.random.fold_in(key_of[11], 71), 0)
    cotangent = bell_draw(key_of[10], (TOKENS, D), 1.0, 6.0, ((0, 32),))
    return {"tokens": tokens, "norm_gains": norm_gains, "qkv_weight": qkv_weight, "out_weight": out_weight, "router_weight": router_weight, "gate_up_weight": gate_up_weight, "down_weight": down_weight, "routes": routes, "placement": placement, "parents": parents, "cotangent": cotangent}


EPS = 1e-06
MASK_VALUE = -1e+30

@jax.custom_vjp
def low(v):
    return lax.optimization_barrier(v.astype(jnp.bfloat16)).astype(jnp.float32)

@jax.custom_vjp
def low_back(v):
    return v

def low_keep(v):
    return (low(v), None)

def low_pass(kept, grad):
    return (grad,)

def back_keep(v):
    return (v, None)

def back_low(kept, grad):
    return (low(grad),)
low.defvjp(low_keep, low_pass)
low_back.defvjp(back_keep, back_low)

def matmul(left, right):
    return jnp.dot(left, right, precision=lax.Precision.HIGHEST, preferred_element_type=jnp.float32)

def normed(values, gain):
    return values * lax.rsqrt(lax.optimization_barrier(jnp.mean(values * values, axis=-1, keepdims=True)) + EPS) * gain

def visible_slots(group_ids, group_parents):
    tree_index = group_ids // TREE_SEGS
    current = group_ids % TREE_SEGS
    alive = jnp.ones(group_ids.shape, dtype=bool)
    seen = jnp.zeros((group_ids.shape[0], group_ids.shape[0]), dtype=bool)
    for level in range(TRUNK + 2):
        wanted = tree_index * TREE_SEGS + current
        seen = seen | alive[:, None] & (wanted[:, None] == group_ids[None, :])
        parent_seg = group_parents[tree_index, current]
        alive = alive & (parent_seg != current)
        current = parent_seg
    return seen

def attend_block(query_block, start, keys, values, seen):
    block = query_block.shape[0]
    rows = keys.shape[0]
    groups_per = H // KVH
    key_row = jnp.arange(rows, dtype=jnp.int32)
    key_slot = key_row // SEG
    key_pos = key_row % SEG
    query_row = start + jnp.arange(block, dtype=jnp.int32)
    query_slot = query_row // SEG
    query_pos = query_row % SEG
    allowed = seen[query_slot][:, key_slot] & ((query_slot[:, None] != key_slot[None, :]) | (key_pos[None, :] <= query_pos[:, None]))
    heads = query_block.reshape(block, KVH, groups_per, HD)
    raw = jnp.einsum('qgrd,kgd->grqk', heads, keys, precision=lax.Precision.HIGHEST)
    scores = low_back(raw * HD ** (-0.5))
    scores = jnp.where(allowed[None, None], scores, MASK_VALUE)
    probs = jax.nn.softmax(scores, axis=-1)
    mixed = jnp.einsum('grqk,kgd->qgrd', low(probs), values, precision=lax.Precision.HIGHEST)
    return mixed.reshape(block, H * HD)

def group_attention(operands):
    queries, keys_flat, values_flat, group_ids, group_parents = operands
    rows = queries.shape[0]
    seen = visible_slots(group_ids, group_parents)
    block = 512 if rows % 512 == 0 else rows
    count = rows // block
    keys = keys_flat.reshape(rows, KVH, HD)
    values = values_flat.reshape(rows, KVH, HD)
    blocks = queries.reshape(count, block, H * HD)
    starts = jnp.arange(count, dtype=jnp.int32) * block
    outputs = lax.map(lambda pair: jax.checkpoint(attend_block)(pair[0], pair[1], keys, values, seen), (blocks, starts))
    return outputs.reshape(rows, H * HD)

def expert_rows(act_block, weight_block, gate_up_all, down_all):

    def one_expert(total, item):
        gate_up_one, down_one, column = item
        gate_up = low_back(matmul(act_block, gate_up_one))
        hidden = low(jax.nn.silu(gate_up[:, :FF]) * gate_up[:, FF:])
        expert_out = low_back(matmul(hidden, down_one))
        return (total + column[:, None] * expert_out, None)
    total, unused = lax.scan(one_expert, jnp.zeros(act_block.shape, jnp.float32), (gate_up_all, down_all, weight_block.T))
    return total

def forward(token_values, gains, qkv_w, out_w, router_w, gate_up_w, down_w, routes, placement, parents):
    count = token_values.shape[0]
    width_q = H * HD
    width_kv = KVH * HD
    act_first = low(normed(token_values, gains[0]))
    projected = matmul(act_first, qkv_w)
    queries = low(low_back(projected[:, :width_q]))
    keys = low(low_back(projected[:, width_q:width_q + width_kv]))
    values = low(low_back(projected[:, width_q + width_kv:]))
    slots_group = TREE_DEVS * SEG_DEV
    rows_group = slots_group * SEG
    groups = count // rows_group
    trees_group = slots_group // TREE_SEGS
    attended = lax.map(group_attention, (queries.reshape(groups, rows_group, width_q), keys.reshape(groups, rows_group, width_kv), values.reshape(groups, rows_group, width_kv), placement.reshape(groups, slots_group), parents.reshape(groups, trees_group, TREE_SEGS)))
    attended = low(low_back(attended.reshape(count, width_q)))
    residual = token_values + low_back(matmul(attended, out_w))
    act_second = low(normed(residual, gains[1]))
    logits = matmul(act_second, router_w)
    chosen = jnp.take_along_axis(logits, routes, axis=1)
    gates = jax.nn.softmax(chosen, axis=-1)
    picks = (routes[:, :, None] == jnp.arange(E, dtype=jnp.int32)[None, None, :]).astype(jnp.float32)
    gate_table = jnp.einsum('tk,tke->te', gates, picks, precision=lax.Precision.HIGHEST)
    block = 2048 if count % 2048 == 0 else count
    pieces = count // block
    mixture = lax.map(lambda pair: jax.checkpoint(expert_rows)(pair[0], pair[1], gate_up_w, down_w), (act_second.reshape(pieces, block, D), gate_table.reshape(pieces, block, E)))
    return residual + mixture.reshape(count, D)

def reference(tokens, norm_gains, qkv_weight, out_weight, router_weight, gate_up_weight, down_weight, routes, placement, parents, cotangent):
    floats = tuple((array.astype(jnp.float32) for array in (tokens, norm_gains, qkv_weight, out_weight, router_weight, gate_up_weight, down_weight)))

    def forward_floats(token_values, gains, qkv_w, out_w, router_w, gate_up_w, down_w):
        return forward(token_values, gains, qkv_w, out_w, router_w, gate_up_w, down_w, routes, placement, parents)
    result, pullback = jax.vjp(forward_floats, *floats)
    grads = pullback(cotangent.astype(jnp.float32))
    return (result.astype(jnp.bfloat16), grads[0], grads[1], grads[2], grads[3], grads[4], grads[5], grads[6])
```

```python
import jax
import jax.numpy as jnp
from jax import lax
from jax.sharding import PartitionSpec as P

D = 1536
H = 24
KVH = 8
HD = 64
FF = 512
TOP = 8
E = 16
SEG = 128
TRUNK = 8
TREE_DEVS = 4
TREE_SEGS = 20
CAP = 352


EPS = 1e-06
MASK_VALUE = -1e30


def partner(block, axis, stride):
    count = lax.axis_size(axis)
    route = []
    for low in range(count):
        high = low | 1 << stride
        if high != low and high < count:
            route += [(low, high), (high, low)]
    return lax.ppermute(block, axis, route)


def norm_rows(values, gain):
    scale_rows = lax.rsqrt(jnp.mean(values * values, axis=-1, keepdims=True) + EPS)
    return (values * scale_rows * gain, scale_rows)


def norm_back(values, scale_rows, gain, upstream):
    scaled = upstream * gain
    inner = jnp.mean(scaled * values, axis=-1, keepdims=True)
    through = scale_rows * scaled - values * (scale_rows * scale_rows * scale_rows) * inner
    gain_grad = jnp.sum(upstream * values * scale_rows, axis=0)
    return (through, gain_grad)


def table_lookup(table, index):
    positions = jnp.arange(table.shape[0], dtype=jnp.int32)
    return jnp.sum(jnp.where(index[:, None] == positions[None, :], table[None, :], 0), axis=1)


def find_slot(group_ids, wanted):
    positions = jnp.arange(group_ids.shape[0], dtype=jnp.int32)
    return jnp.sum(jnp.where(group_ids[None, :] == wanted[:, None], positions[None, :], 0), axis=1)


def ancestor_slots(local_ids, group_ids, group_parents, depth):
    flat_parents = group_parents.reshape(-1)
    tree_index = local_ids // TREE_SEGS
    current = local_ids % TREE_SEGS
    alive = jnp.ones(local_ids.shape, dtype=bool)
    slot_list = []
    alive_list = []
    for level in range(depth):
        wanted = tree_index * TREE_SEGS + current
        slot_list.append(find_slot(group_ids, wanted))
        alive_list.append(alive)
        parent_seg = table_lookup(flat_parents, wanted)
        alive = alive & (parent_seg != current)
        current = parent_seg
    return (jnp.stack(slot_list, axis=1), jnp.stack(alive_list, axis=1))


def head_scores(queries, keys, mask, scale):
    scores = jnp.einsum("sgqd,skd->sgqk", queries, keys, preferred_element_type=jnp.float32) * scale
    return jnp.where(mask[:, None], scores, MASK_VALUE)


def head_forward(operands, mask, scale):
    queries, keys, values = operands
    scores = head_scores(queries, keys, mask, scale)
    highest = jnp.max(scores, axis=-1, keepdims=True)
    weights = jnp.exp(scores - highest)
    totals = jnp.sum(weights, axis=-1, keepdims=True)
    probs = (weights / totals).astype(jnp.bfloat16)
    mixed = jnp.einsum("sgqk,skd->sgqd", probs, values, preferred_element_type=jnp.float32)
    return (mixed.astype(jnp.bfloat16), highest + jnp.log(totals))


def head_backward(operands, mask, scale):
    queries, keys, values, upstream, log_totals = operands
    scores = head_scores(queries, keys, mask, scale)
    probs = jnp.exp(scores - log_totals)
    value_grad = jnp.einsum(
        "sgqk,sgqd->skd", probs.astype(jnp.bfloat16), upstream, preferred_element_type=jnp.float32
    )
    prob_grad = jnp.einsum("sgqd,skd->sgqk", upstream, values, preferred_element_type=jnp.float32)
    inner = jnp.sum(probs * prob_grad, axis=-1, keepdims=True)
    score_grad = (probs * (prob_grad - inner)).astype(jnp.bfloat16)
    query_grad = (
        jnp.einsum("sgqk,skd->sgqd", score_grad, keys, preferred_element_type=jnp.float32) * scale
    )
    key_grad = (
        jnp.einsum("sgqk,sgqd->skd", score_grad, queries, preferred_element_type=jnp.float32)
        * scale
    )
    return (query_grad.astype(jnp.bfloat16), key_grad, value_grad)


def gather_columns(weight, rep_index, rep_count):
    width = weight.shape[1] // rep_count
    own = lax.dynamic_slice_in_dim(weight, rep_index * width, width, axis=1)
    part = lax.all_gather(own, "shard", axis=0, tiled=True)
    return lax.all_gather(part, "rep", axis=0)


def spread_experts(grad):
    share = lax.psum_scatter(grad.astype(jnp.bfloat16), "shard", scatter_dimension=1, tiled=True)
    return lax.all_gather(share, "rep", axis=0, tiled=True).astype(jnp.float32)


def spread_columns(grad, rep_count):
    rows, width = grad.shape
    pieces = grad.astype(jnp.bfloat16).reshape(rows, rep_count, width // rep_count).transpose(1, 0, 2)
    part = lax.psum_scatter(pieces, "rep", scatter_dimension=0, tiled=True)[0]
    share = lax.psum_scatter(part, "shard", scatter_dimension=0, tiled=True)
    whole = lax.all_gather(share, "rep", axis=1, tiled=True)
    return whole.astype(jnp.float32)


def shards(
    tokens,
    norm_gains,
    qkv_weight,
    out_weight,
    router_weight,
    gate_up_weight,
    down_weight,
    routes,
    placement,
    parents,
    cotangent,
):
    shard_index = lax.axis_index("shard")
    rep_index = lax.axis_index("rep")
    shard_count = lax.axis_size("shard")
    token_count = tokens.shape[0]
    seg_dev = token_count // SEG
    depth = TRUNK + 2
    key_count = depth * SEG
    width_q = H * HD
    width_kv = KVH * HD
    groups_per = H // KVH
    scale = HD ** (-0.5)
    group_size = TREE_DEVS * seg_dev
    tree_count = group_size // TREE_SEGS
    member = shard_index % TREE_DEVS
    group = (rep_index * shard_count + shard_index) // TREE_DEVS
    group_ids = lax.dynamic_slice_in_dim(placement, group * group_size, group_size)
    group_parents = lax.dynamic_slice_in_dim(parents, group * tree_count, tree_count)
    local_ids = lax.dynamic_slice_in_dim(group_ids, member * seg_dev, seg_dev)
    path_slots, path_alive = ancestor_slots(local_ids, group_ids, group_parents, depth)
    key_level = jnp.arange(key_count, dtype=jnp.int32) // SEG
    key_pos = jnp.arange(key_count, dtype=jnp.int32) % SEG
    query_pos = jnp.arange(SEG, dtype=jnp.int32)
    level_alive = jnp.repeat(path_alive, SEG, axis=1)
    mask = level_alive[:, None, :] & (
        (key_level[None, None, :] > 0) | (key_pos[None, None, :] <= query_pos[None, :, None])
    )
    rep_count = lax.axis_size("rep")
    own_experts = E // rep_count
    first_expert = rep_index * own_experts
    gains = lax.all_gather(norm_gains, "shard", axis=1, tiled=True)
    w_router = lax.all_gather(router_weight, "shard", axis=0, tiled=True)
    w_qkv = gather_columns(qkv_weight, rep_index, rep_count)
    w_out = gather_columns(out_weight, rep_index, rep_count)
    w_gate_up = lax.all_gather(
        lax.dynamic_slice_in_dim(gate_up_weight, first_expert, own_experts), "shard", axis=1, tiled=True
    )
    w_down = lax.all_gather(
        lax.dynamic_slice_in_dim(down_weight, first_expert, own_experts), "shard", axis=1, tiled=True
    )
    cot_all = lax.all_gather(cotangent, "rep", axis=0, tiled=True)
    gain_first = gains[0].astype(jnp.float32)
    gain_second = gains[1].astype(jnp.float32)
    token_values = tokens.astype(jnp.float32)
    normed_first, scale_first = norm_rows(token_values, gain_first)
    act_first = normed_first.astype(jnp.bfloat16)
    projected = jnp.einsum("td,rdc->trc", act_first, w_qkv, preferred_element_type=jnp.float32)
    projected = projected.reshape(token_count, width_q + 2 * width_kv)
    queries = projected[:, :width_q].astype(jnp.bfloat16)
    own_kv = projected[:, width_q:].astype(jnp.bfloat16).reshape(seg_dev, SEG, 2 * width_kv)
    low_first = member % 2 == 0
    pair_first = member // 2 == 0
    near_kv = partner(own_kv, "shard", 0)
    pair_kv = jnp.where(
        low_first,
        jnp.concatenate([own_kv, near_kv], axis=0),
        jnp.concatenate([near_kv, own_kv], axis=0),
    )
    far_kv = partner(pair_kv, "shard", 1)
    group_kv = jnp.where(
        pair_first,
        jnp.concatenate([pair_kv, far_kv], axis=0),
        jnp.concatenate([far_kv, pair_kv], axis=0),
    )
    chosen_kv = group_kv[path_slots].reshape(seg_dev, key_count, 2, KVH, HD)
    head_kv = chosen_kv.transpose(3, 2, 0, 1, 4)
    head_keys = head_kv[:, 0]
    head_values = head_kv[:, 1]
    head_queries = queries.reshape(seg_dev, SEG, KVH, groups_per, HD).transpose(2, 0, 3, 1, 4)
    mixed, log_totals = lax.map(
        lambda operands: head_forward(operands, mask, scale), (head_queries, head_keys, head_values)
    )
    attended = mixed.transpose(1, 3, 0, 2, 4).reshape(token_count, width_q)
    mixed_out = jnp.einsum("td,rdc->trc", attended, w_out, preferred_element_type=jnp.float32)
    residual = token_values + mixed_out.reshape(token_count, D)
    normed_second, scale_second = norm_rows(residual, gain_second)
    act_second = normed_second.astype(jnp.bfloat16)
    logits = jnp.dot(act_second, w_router, preferred_element_type=jnp.float32)
    expert_ids = jnp.arange(E, dtype=jnp.int32)
    picks = routes[:, :, None] == expert_ids[None, None, :]
    chosen = jnp.sum(jnp.where(picks, logits[:, None, :], 0.0), axis=-1)
    gates = jax.nn.softmax(chosen, axis=-1)
    upstream = cotangent.astype(jnp.float32)
    gate_table = jnp.sum(jnp.where(picks, gates[:, :, None], 0.0), axis=1)
    act_all = lax.all_gather(act_second, "rep", axis=0, tiled=True)
    gate_all = lax.all_gather(gate_table, "rep", axis=0, tiled=True)
    own_gate = lax.dynamic_slice_in_dim(gate_all, first_expert, own_experts, axis=1).T[:, :, None]
    gate_up = jnp.einsum("td,edf->etf", act_all, w_gate_up, preferred_element_type=jnp.float32)
    gate_part = gate_up[..., :FF]
    up_part = gate_up[..., FF:]
    sig_gate = jax.nn.sigmoid(gate_part)
    hidden = gate_part * sig_gate * up_part
    gated = (hidden * own_gate).astype(jnp.bfloat16)
    mix_part = jnp.einsum("etf,efd->td", gated, w_down, preferred_element_type=jnp.float32)
    mixture = lax.psum_scatter(mix_part.astype(jnp.bfloat16), "rep", scatter_dimension=0, tiled=True)
    block_out = (residual + mixture.astype(jnp.float32)).astype(jnp.bfloat16)
    raw_grad = jnp.einsum("td,efd->etf", cot_all, w_down, preferred_element_type=jnp.float32)
    gate_grad_own = jnp.sum(hidden * raw_grad, axis=-1)
    gate_grad_all = lax.all_gather(gate_grad_own, "rep", axis=0, tiled=True)
    gate_grad_table = lax.dynamic_slice_in_dim(
        gate_grad_all, rep_index * token_count, token_count, axis=1
    ).T
    inner_gate = jnp.sum(gate_table * gate_grad_table, axis=-1, keepdims=True)
    logit_grad = gate_table * (gate_grad_table - inner_gate)
    router_grad = jnp.dot(
        act_second.astype(jnp.float32).T,
        logit_grad,
        precision=lax.Precision.HIGHEST,
        preferred_element_type=jnp.float32,
    )
    hidden_grad = raw_grad * own_gate
    gate_grad_part = hidden_grad * up_part * sig_gate * (1.0 + gate_part * (1.0 - sig_gate))
    up_grad_part = hidden_grad * gate_part * sig_gate
    gate_up_grad_rows = jnp.concatenate([gate_grad_part, up_grad_part], axis=-1).astype(
        jnp.bfloat16
    )
    down_grad = jnp.einsum("etf,td->efd", gated, cot_all, preferred_element_type=jnp.float32)
    gate_up_grad = jnp.einsum(
        "td,etf->edf", act_all, gate_up_grad_rows, preferred_element_type=jnp.float32
    )
    down_grad = spread_experts(down_grad)
    gate_up_grad = spread_experts(gate_up_grad)
    act_part = jnp.einsum(
        "etf,edf->td", gate_up_grad_rows, w_gate_up, preferred_element_type=jnp.float32
    )
    act_second_grad = lax.psum_scatter(
        act_part.astype(jnp.bfloat16), "rep", scatter_dimension=0, tiled=True
    ).astype(jnp.float32)
    act_second_grad = act_second_grad + jnp.dot(
        logit_grad,
        w_router.astype(jnp.float32).T,
        precision=lax.Precision.HIGHEST,
        preferred_element_type=jnp.float32,
    )
    through_second, gain_grad_second = norm_back(
        residual, scale_second, gains[1].astype(jnp.float32), act_second_grad
    )
    residual_grad = upstream + through_second
    branch_grad = residual_grad.astype(jnp.bfloat16)
    out_grad = jnp.dot(attended.T, branch_grad, preferred_element_type=jnp.float32)
    attended_grad = jnp.einsum(
        "trc,rdc->td",
        branch_grad.reshape(token_count, rep_count, D // rep_count),
        w_out,
        preferred_element_type=jnp.float32,
    ).astype(jnp.bfloat16)
    head_upstream = attended_grad.reshape(seg_dev, SEG, KVH, groups_per, HD).transpose(
        2, 0, 3, 1, 4
    )
    query_grad, key_grad, value_grad = lax.map(
        lambda operands: head_backward(operands, mask, scale),
        (head_queries, head_keys, head_values, head_upstream, log_totals),
    )
    query_grad = query_grad.transpose(1, 3, 0, 2, 4).reshape(token_count, width_q)
    path_grad = (
        jnp.stack([key_grad, value_grad], axis=1)
        .transpose(2, 3, 1, 0, 4)
        .reshape(seg_dev, depth, SEG, 2 * width_kv)
    )
    group_grad = (
        jnp.zeros((group_size, SEG, 2 * width_kv), jnp.float32).at[path_slots].add(path_grad)
    )
    pair_part = jnp.where(pair_first, group_grad[: 2 * seg_dev], group_grad[2 * seg_dev :])
    far_part = jnp.where(pair_first, group_grad[2 * seg_dev :], group_grad[: 2 * seg_dev])
    pair_sum = pair_part + partner(far_part.astype(jnp.bfloat16), "shard", 1).astype(far_part.dtype)
    own_part = jnp.where(low_first, pair_sum[:seg_dev], pair_sum[seg_dev:])
    near_part = jnp.where(low_first, pair_sum[seg_dev:], pair_sum[:seg_dev])
    own_grad = own_part + partner(near_part.astype(jnp.bfloat16), "shard", 0).astype(
        near_part.dtype
    )
    projected_grad = jnp.concatenate(
        [query_grad, own_grad.reshape(token_count, 2 * width_kv).astype(jnp.bfloat16)], axis=1
    )
    qkv_grad = jnp.dot(act_first.T, projected_grad, preferred_element_type=jnp.float32)
    act_first_grad = jnp.einsum(
        "trc,rdc->td",
        projected_grad.reshape(token_count, rep_count, -1),
        w_qkv,
        preferred_element_type=jnp.float32,
    )
    through_first, gain_grad_first = norm_back(
        token_values, scale_first, gains[0].astype(jnp.float32), act_first_grad
    )
    token_grad = residual_grad + through_first
    gains_grad = jnp.stack([gain_grad_first, gain_grad_second], axis=1)
    small = jnp.concatenate([gains_grad, router_grad], axis=1)
    small = lax.psum_scatter(small, "shard", scatter_dimension=0, tiled=True)
    small = lax.psum(small, "rep")
    qkv_grad = spread_columns(qkv_grad, rep_count)
    out_grad = spread_columns(out_grad, rep_count)
    return (block_out, token_grad, small[:, :2].T, qkv_grad, out_grad, small[:, 2:], gate_up_grad, down_grad)


def solution(mesh):
    in_specs = (
        P(("rep", "shard"), None),
        P(None, "shard"),
        P("shard", None),
        P("shard", None),
        P("shard", None),
        P(None, "shard", None),
        P(None, "shard", None),
        P(("rep", "shard"), None),
        P(),
        P(),
        P(("rep", "shard"), None),
    )
    out_specs = (
        P(("rep", "shard"), None),
        P(("rep", "shard"), None),
        P(None, "shard"),
        P("shard", None),
        P("shard", None),
        P("shard", None),
        P(None, "shard", None),
        P(None, "shard", None),
    )
    return jax.shard_map(shards, mesh=mesh, in_specs=in_specs, out_specs=out_specs, check_vma=False)
```

```python
import functools

import jax
import jax.experimental.pallas as pl
import jax.experimental.pallas.tpu as pltpu
import jax.numpy as jnp
from jax import lax
from jax.sharding import PartitionSpec as P

D = 1536
H = 24
KVH = 8
HD = 64
FF = 512
TOP = 8
E = 16
SEG = 128
TRUNK = 8
TREE_DEVS = 4
TREE_SEGS = 20
CAP = 352


EPS = 1e-06


PAIRS = KVH // 2
LANES = 2 * HD
NEG=-1e30
def low_half(): return lax.broadcasted_iota(jnp.int32,(SEG,LANES),1)<HD
def stack_heads(ref, row, pair, factor=None):
    low=low_half()
    t=[ref[pl.ds(row,SEG), pl.ds(pl.multiple_of((3*pair+i)*LANES,LANES),LANES)].astype(jnp.float32) for i in range(3)]
    if factor is not None: t=[x*factor for x in t]
    z=jnp.zeros_like(t[0])
    r0=pltpu.roll(t[0],HD,1); r2=pltpu.roll(t[2],HD,1)
    parts=[jnp.where(low,t[0],z),jnp.where(low,r0,z),jnp.where(low,t[1],z),
           jnp.where(low,z,t[1]),jnp.where(low,z,r2),jnp.where(low,z,t[2])]
    return jnp.concatenate(parts,axis=0)
def unstack_heads(rows):
    low=low_half()
    a=[rows[i*SEG:(i+1)*SEG] for i in range(6)]
    return [jnp.where(low,a[0],pltpu.roll(a[1],HD,1)), jnp.where(low,a[2],a[3]), jnp.where(low,pltpu.roll(a[4],HD,1),a[5])]
def kv_path(kv_ref, slots, seg, depth, col):
    return jnp.concatenate([kv_ref[slots[seg,lev],:,pl.ds(pl.multiple_of(col,LANES),LANES)] for lev in range(depth)],axis=0)
NT=(((1,),(1,)),((),())); NN=(((1,),(0,)),((),())); TN=(((0,),(0,)),((),()))
def dot(a,b,dims): return lax.dot_general(a,b,dims,preferred_element_type=jnp.float32)
def causal_bias(width):
    key=lax.broadcasted_iota(jnp.int32,(SEG,width),0); qry=lax.broadcasted_iota(jnp.int32,(SEG,width),1)%SEG
    return jnp.where(key<=qry,0.0,NEG)
def fwd_step(depth, slots, bias, q_ref, kv_ref, o_ref, lse_ref, s_scr, p_scr, i, c):
    width=6*SEG
    seg=i//PAIRS; pair=i%PAIRS
    row=pl.multiple_of(seg*SEG,SEG)
    q6=stack_heads(q_ref,row,pair,HD**-0.5).astype(jnp.bfloat16)
    top=jnp.full((8,width),NEG,jnp.float32)
    for lev in range(depth):
        k=kv_ref[slots[seg,lev],:,pl.ds(pl.multiple_of(pair*LANES,LANES),LANES)]
        s=dot(k,q6,NT)
        s=s+(causal_bias(width) if lev==0 else bias[seg,lev])
        s_scr[lev*SEG:(lev+1)*SEG,:]=s
        top=jnp.maximum(top,jnp.max(s.reshape(SEG//8,8,width),axis=0))
    top=jnp.max(top,axis=0,keepdims=True)
    tot=jnp.zeros((8,width),jnp.float32)
    acc=jnp.zeros((LANES,width),jnp.float32)
    for lev in range(depth):
        p=jnp.exp(s_scr[lev*SEG:(lev+1)*SEG,:]-top)
        tot=tot+jnp.sum(p.reshape(SEG//8,8,width),axis=0)
        p_scr[lev*SEG:(lev+1)*SEG,:]=p.astype(jnp.bfloat16)
    v=kv_path(kv_ref,slots,seg,depth,KVH*HD+pair*LANES)
    acc=dot(v,p_scr[...],TN)
    tot=jnp.sum(tot,axis=0,keepdims=True)
    lse_ref[i]=jnp.broadcast_to(top+jnp.log(tot),(8,width))
    o6=(acc/tot).T
    for j,t in enumerate(unstack_heads(o6)):
        o_ref[pl.ds(row,SEG),pl.ds(pl.multiple_of((3*pair+j)*LANES,LANES),LANES)]=t.astype(o_ref.dtype)
    return c
def bwd_kernel(depth, slots, bias, inv, q_ref, kv_ref, o_ref, do_ref, lse_ref, dq_ref, dkv_ref, path, p_scr, d_scr):
    width=6*SEG
    segs=q_ref.shape[0]//SEG
    path[:,depth]=jnp.zeros((segs,)+path.shape[2:],path.dtype)
    def step(i,c):
        seg=i//PAIRS; pair=i%PAIRS
        row=pl.multiple_of(seg*SEG,SEG)
        q6=stack_heads(q_ref,row,pair,HD**-0.5).astype(jnp.bfloat16)
        do6f=stack_heads(do_ref,row,pair)
        do6=do6f.astype(jnp.bfloat16)
        prod=do6f*stack_heads(o_ref,row,pair)
        hi=prod.astype(jnp.bfloat16); lo=(prod-hi.astype(jnp.float32)).astype(jnp.bfloat16)
        ones=jnp.ones((8,LANES),jnp.bfloat16)
        delta=(dot(ones,hi,NT)+dot(ones,lo,NT))[:1]
        lse=lse_ref[i][:1]
        kcol=pl.multiple_of(pair*LANES,LANES); vcol=pl.multiple_of(KVH*HD+pair*LANES,LANES)
        for lev in range(depth):
            k=kv_ref[slots[seg,lev],:,pl.ds(kcol,LANES)]
            v=kv_ref[slots[seg,lev],:,pl.ds(vcol,LANES)]
            s=dot(k,q6,NT)
            s=s+(causal_bias(width) if lev==0 else bias[seg,lev])
            p=jnp.exp(s-lse)
            dp=dot(v,do6,NT)
            ds=(p*(dp-delta)).astype(jnp.bfloat16)
            p_scr[lev*SEG:(lev+1)*SEG,:]=p.astype(jnp.bfloat16)
            d_scr[lev*SEG:(lev+1)*SEG,:]=ds
        dv=dot(p_scr[...],do6,NN)
        dk=dot(d_scr[...],q6,NN)
        for lev in range(depth):
            path[seg,lev,:,pl.ds(kcol,LANES)]=dk[lev*SEG:(lev+1)*SEG].astype(path.dtype)
            path[seg,lev,:,pl.ds(vcol,LANES)]=dv[lev*SEG:(lev+1)*SEG].astype(path.dtype)
        k=kv_path(kv_ref,slots,seg,depth,pair*LANES)
        dq6=(dot(k,d_scr[...],TN)*(HD**-0.5)).T
        for j,t in enumerate(unstack_heads(dq6)):
            dq_ref[pl.ds(row,SEG),pl.ds(pl.multiple_of((3*pair+j)*LANES,LANES),LANES)]=t.astype(dq_ref.dtype)
        return c
    lax.fori_loop(0,segs*PAIRS,step,0)
    def collect(slot,c):
        for col in range(0,2*KVH*HD,256):
            tot=path[0,inv[slot,0],:,col:col+256].astype(jnp.float32)
            for seg in range(1,segs): tot=tot+path[seg,inv[slot,seg],:,col:col+256].astype(jnp.float32)
            dkv_ref[slot,:,col:col+256]=tot.astype(dkv_ref.dtype)
        return c
    lax.fori_loop(0,dkv_ref.shape[0],collect,0)
def attn_bwd(slots,bias,inv,q,kv,o,do,lse,depth):
    T=q.shape[0]; segs=T//SEG
    V=pl.BlockSpec(memory_space=pltpu.VMEM); S=pl.BlockSpec(memory_space=pltpu.SMEM)
    return pl.pallas_call(functools.partial(bwd_kernel,depth),
        out_shape=(jax.ShapeDtypeStruct(q.shape,jnp.bfloat16),jax.ShapeDtypeStruct(kv.shape,jnp.bfloat16)),
        in_specs=[S,S,S,V,V,V,V,V],out_specs=(V,V),
        scratch_shapes=[pltpu.VMEM((segs,depth+1,SEG,2*KVH*HD),jnp.bfloat16),pltpu.VMEM((depth*SEG,6*SEG),jnp.bfloat16),pltpu.VMEM((depth*SEG,6*SEG),jnp.bfloat16)],
        compiler_params=pltpu.CompilerParams(vmem_limit_bytes=60*2**20))(slots,bias,inv,q,kv,o,do,lse)


MESH = pl.DeviceIdType.MESH
ANY = pl.BlockSpec(memory_space=pl.ANY)
VMEM = pl.BlockSpec(memory_space=pltpu.VMEM)
SMEM = pl.BlockSpec(memory_space=pltpu.SMEM)


class Sends:
    def __init__(self):
        self.open = []

    def start(self, cond, src, dst, send_sem, recv_sem, device):
        copy = pltpu.make_async_remote_copy(
            src_ref=src, dst_ref=dst, send_sem=send_sem, recv_sem=recv_sem, device_id=device, device_id_type=MESH
        )
        when(cond, copy.start)
        self.open.append((cond, copy.wait_send))

    def local(self, src, dst, sem):
        copy = pltpu.make_async_copy(src, dst, sem)
        copy.start()
        self.open.append((None, copy.wait))

    def drain(self):
        for cond, wait in self.open:
            when(cond, wait)
        self.open = []


def when(cond, body):
    if cond is None:
        body()
    else:
        pl.when(cond)(body)


def received(cond, region, send_sem, recv_sem, device):
    copy = pltpu.make_async_remote_copy(
        src_ref=region, dst_ref=region, send_sem=send_sem, recv_sem=recv_sem, device_id=device, device_id_type=MESH
    )
    when(cond, copy.wait_recv)


def line_place(shards):
    me = lax.axis_index("shard")
    return me, me // 2, shards // 2


def greet(devices):
    barrier = pltpu.get_barrier_semaphore()
    count = 0
    for cond, device in devices:
        when(
            cond,
            lambda device=device: pl.semaphore_signal(barrier, inc=1, device_id=device, device_id_type=MESH),
        )
        count = count + (1 if cond is None else cond.astype(jnp.int32))
    pl.semaphore_wait(barrier, count)


def line_neighbours(shards):
    me, spot, length = line_place(shards)
    return [
        (None, {"shard": me + 1 - 2 * (me % 2)}),
        (spot > 0, {"shard": me - 2}),
        (spot + 1 < length, {"shard": me + 2}),
    ]


class LineGather:
    def __init__(self, shards, sources, region, up, down, pair, local_sem, arrived=None):
        self.shards, self.sources, self.region = shards, sources, region
        self.up, self.down, self.pair, self.local_sem = up, down, pair, local_sem
        self.arrived = arrived or (lambda cond, block, index: None)
        self.sends = Sends()
        self.me, self.spot, self.length = line_place(shards)
        self.twin = self.me + 1 - 2 * (self.me % 2)

    def forward(self, cond, block, step, rising, falling, src=None):
        place = step if rising else self.length - 1 + step
        for n in range(len(self.sources)):
            here = self.region(n, block)
            out = here if src is None else src[n]
            ways = []
            if rising:
                ways.append((both(cond, self.spot + 1 < self.length), self.up, step + 1, self.me + 2))
            if falling:
                ways.append((both(cond, self.spot > 0), self.down, step + 1, self.me - 2))
            for where, sems, index, device in ways:
                if index < self.length:
                    self.sends.start(where, out, here, sems.at[0, index, n], sems.at[1, index, n], {"shard": device})
            self.sends.start(
                cond, out, here, self.pair.at[0, place, n], self.pair.at[1, place, n], {"shard": self.twin}
            )

    def begin(self):
        for n, src in enumerate(self.sources):
            self.sends.local(src, self.region(n, self.me), self.local_sem.at[n])
        self.forward(None, self.me, 0, True, True, self.sources)

    def finish_local(self):
        for cond, wait in self.sends.open[: len(self.sources)]:
            wait()
        self.sends.open = self.sends.open[len(self.sources) :]

    def step(self, step):
        for sems, cond, block, rising in (
            (self.up, self.spot - step >= 0, self.me - 2 * step, True),
            (self.down, self.spot + step < self.length, self.me + 2 * step, False),
        ):
            for n in range(len(self.sources)):
                received(cond, self.region(n, block), sems.at[0, step, n], sems.at[1, step, n], {"shard": self.twin})
            self.forward(cond, block, step, rising, not rising)
            self.arrived(cond, block, step if rising else self.length - 1 + step)

    def pair_step(self, step):
        turns = [(None, self.twin, 0)] if step == 0 else [
            (self.spot - step >= 0, self.twin - 2 * step, step),
            (self.spot + step < self.length, self.twin + 2 * step, self.length - 1 + step),
        ]
        for cond, block, place in turns:
            for n in range(len(self.sources)):
                received(
                    cond, self.region(n, block), self.pair.at[0, place, n], self.pair.at[1, place, n], {"shard": self.twin}
                )
            self.arrived(cond, block, 2 * self.length - 1 + place)


def both(first, second):
    return second if first is None else jnp.logical_and(first, second)


def line_sems(shards, arrays):
    length = shards // 2
    return [
        pltpu.SemaphoreType.DMA((2, length, arrays)),
        pltpu.SemaphoreType.DMA((2, length, arrays)),
        pltpu.SemaphoreType.DMA((2, 2 * length - 1, arrays)),
        pltpu.SemaphoreType.DMA((arrays,)),
    ]


class RepSpread:
    def __init__(self, arrays, region, cross, core, relay):
        self.arrays, self.region = arrays, region
        self.cross, self.core, self.relay = cross, core, relay
        rep = lax.axis_index("rep")
        self.rep = rep
        self.near = rep + 1 - 2 * (rep % 2)
        self.far = lax.rem(rep + 2, 4)
        self.diagonal = lax.rem(self.near + 2, 4)
        self.sends = Sends()
        self.blocks = []

    def arrived(self, cond, block, index):
        for n in self.arrays:
            here = self.region(n, self.rep, block)
            self.sends.start(
                cond, here, here, self.cross.at[0, block, n], self.cross.at[1, block, n], {"rep": self.far}
            )
            self.sends.start(
                cond, here, here, self.core.at[0, block, n], self.core.at[1, block, n], {"rep": self.near}
            )
        self.blocks.append((cond, block))

    def pass_on(self):
        for cond, block in self.blocks:
            for n in self.arrays:
                here = self.region(n, self.far, block)
                received(cond, here, self.cross.at[0, block, n], self.cross.at[1, block, n], {"rep": self.far})
                self.sends.start(
                    cond, here, here, self.relay.at[0, block, n], self.relay.at[1, block, n], {"rep": self.near}
                )
        self.passed = getattr(self, "passed", []) + self.blocks
        self.blocks = []

    def end(self):
        self.pass_on()
        for cond, block in self.passed:
            for n in self.arrays:
                for sems, part in ((self.core, self.near), (self.relay, self.diagonal)):
                    here = self.region(n, part, block)
                    received(cond, here, sems.at[0, block, n], sems.at[1, block, n], {"rep": self.near})
        self.sends.drain()


def rep_neighbours():
    rep = lax.axis_index("rep")
    return [(None, {"rep": rep + 1 - 2 * (rep % 2)}), (None, {"rep": lax.rem(rep + 2, 4)})]


def rep_sems(shards, arrays):
    return [pltpu.SemaphoreType.DMA((2, shards, arrays)) for unused in range(3)]


def weights_kernel(shards, qkv, out, small, qkv_all, out_all, small_all, up, down, pair, local_sem, cross, core, relay):
    rep = lax.axis_index("rep")
    greet(line_neighbours(shards) + rep_neighbours())
    refs = (qkv_all, out_all, small_all)

    def part(n, owner, block):
        return refs[n].at[block] if n == 2 else refs[n].at[owner, block]

    def columns(ref, width):
        return ref.at[:, pl.ds(pl.multiple_of(rep * width, LANES), width)]

    spread = RepSpread((0, 1), part, cross, core, relay)
    sources = (columns(qkv, qkv_all.shape[-1]), columns(out, out_all.shape[-1]), small)
    gather = LineGather(
        shards, sources, lambda n, block: part(n, rep, block), up, down, pair, local_sem, spread.arrived
    )
    gather.begin()
    gather.finish_local()
    spread.arrived(None, gather.me, 0)
    for step in range(gather.length):
        if step:
            gather.step(step)
        spread.pass_on()
        gather.pair_step(step)
    spread.end()
    gather.sends.drain()


def gather_weights(qkv_weight, out_weight, small, shards, reps):
    rows = qkv_weight.shape[0]
    shapes = [
        (reps, shards, rows, qkv_weight.shape[1] // reps),
        (reps, shards, rows, out_weight.shape[1] // reps),
        (shards,) + small.shape,
    ]
    return pl.pallas_call(
        functools.partial(weights_kernel, shards),
        out_shape=[jax.ShapeDtypeStruct(shape, jnp.bfloat16) for shape in shapes],
        in_specs=[ANY] * 3,
        out_specs=[ANY] * 3,
        scratch_shapes=line_sems(shards, 3) + rep_sems(shards, 2),
        compiler_params=pltpu.CompilerParams(collective_id=1, has_side_effects=True),
    )(qkv_weight, out_weight, small)


def attend_gather_kernel(
    depth,
    shards,
    slots,
    bias,
    q_ref,
    kv_ref,
    gu_ref,
    dn_ref,
    o_ref,
    lse_ref,
    kv_all,
    gu_all,
    dn_all,
    s_scr,
    p_scr,
    kv_sems,
    up,
    down,
    pair,
    local_sem,
):
    me = lax.axis_index("shard")
    first = me // TREE_DEVS * TREE_DEVS
    member = me % TREE_DEVS
    seg_dev = kv_ref.shape[0]
    others = [first + lax.rem(member + away, TREE_DEVS) for away in range(1, TREE_DEVS)]
    greet(line_neighbours(shards) + [(None, {"shard": other}) for other in others])
    sends = Sends()
    own = kv_all.at[pl.ds(member * seg_dev, seg_dev)]
    for away, other in enumerate(others):
        sends.start(None, kv_ref, own, kv_sems.at[0, away], kv_sems.at[1, away], {"shard": other})
    gather = LineGather(
        shards,
        (gu_ref, dn_ref),
        lambda n, block: (gu_all, dn_all)[n].at[:, block],
        up,
        down,
        pair,
        local_sem,
    )
    gather.begin()
    kv_all[pl.ds(member * seg_dev, seg_dev)] = kv_ref[...]
    for away in range(TREE_DEVS - 1):
        source = lax.rem(member + TREE_DEVS - 1 - away, TREE_DEVS)
        block = kv_all.at[pl.ds(source * seg_dev, seg_dev)]
        received(None, block, kv_sems.at[0, away], kv_sems.at[1, away], {"shard": first + source})
    count = seg_dev * PAIRS
    attend = functools.partial(fwd_step, depth, slots, bias, q_ref, kv_all, o_ref, lse_ref, s_scr, p_scr)
    done = 0
    for step in range(1, gather.length):
        upto = count * step // (gather.length - 1)
        lax.fori_loop(done, upto, attend, 0)
        done = upto
        gather.step(step)
    for step in range(gather.length):
        gather.pair_step(step)
    gather.sends.drain()
    sends.drain()


def attend_gather(slots, bias, q, kv, gate_up, down, depth, shards):
    tokens = q.shape[0]
    count = tokens // SEG * PAIRS
    experts, rows = gate_up.shape[:2]
    return pl.pallas_call(
        functools.partial(attend_gather_kernel, depth, shards),
        out_shape=(
            jax.ShapeDtypeStruct(q.shape, jnp.bfloat16),
            jax.ShapeDtypeStruct((count, 8, 6 * SEG), jnp.float32),
            jax.ShapeDtypeStruct((TREE_DEVS * kv.shape[0],) + kv.shape[1:], jnp.bfloat16),
            jax.ShapeDtypeStruct((experts, shards, rows) + gate_up.shape[2:], jnp.bfloat16),
            jax.ShapeDtypeStruct((experts, shards) + down.shape[1:], jnp.bfloat16),
        ),
        in_specs=[SMEM, SMEM, VMEM, VMEM, ANY, ANY],
        out_specs=(VMEM, VMEM, VMEM, ANY, ANY),
        scratch_shapes=[
            pltpu.VMEM((depth * SEG, 6 * SEG), jnp.float32),
            pltpu.VMEM((depth * SEG, 6 * SEG), jnp.bfloat16),
            pltpu.SemaphoreType.DMA((2, TREE_DEVS - 1)),
        ]
        + line_sems(shards, 2),
        compiler_params=pltpu.CompilerParams(
            collective_id=2, has_side_effects=True, vmem_limit_bytes=48 * 2**20
        ),
    )(slots, bias, q, kv, gate_up, down)


def partner(block, axis, stride):
    count = lax.axis_size(axis)
    route = []
    for low in range(count):
        high = low | 1 << stride
        if high != low and high < count:
            route += [(low, high), (high, low)]
    return lax.ppermute(block, axis, route)


def norm_rows(values, gain):
    scale_rows = lax.rsqrt(jnp.mean(values * values, axis=-1, keepdims=True) + EPS)
    return (values * scale_rows * gain, scale_rows)


def norm_back(values, scale_rows, gain, upstream):
    scaled = upstream * gain
    inner = jnp.mean(scaled * values, axis=-1, keepdims=True)
    through = scale_rows * scaled - values * (scale_rows * scale_rows * scale_rows) * inner
    gain_grad = jnp.sum(upstream * values * scale_rows, axis=0)
    return (through, gain_grad)


def table_lookup(table, index):
    positions = jnp.arange(table.shape[0], dtype=jnp.int32)
    return jnp.sum(jnp.where(index[:, None] == positions[None, :], table[None, :], 0), axis=1)


def find_slot(group_ids, wanted):
    positions = jnp.arange(group_ids.shape[0], dtype=jnp.int32)
    return jnp.sum(jnp.where(group_ids[None, :] == wanted[:, None], positions[None, :], 0), axis=1)


def ancestor_slots(local_ids, group_ids, group_parents, depth):
    flat_parents = group_parents.reshape(-1)
    tree_index = local_ids // TREE_SEGS
    current = local_ids % TREE_SEGS
    alive = jnp.ones(local_ids.shape, dtype=bool)
    slot_list = []
    alive_list = []
    for level in range(depth):
        wanted = tree_index * TREE_SEGS + current
        slot_list.append(find_slot(group_ids, wanted))
        alive_list.append(alive)
        parent_seg = table_lookup(flat_parents, wanted)
        alive = alive & (parent_seg != current)
        current = parent_seg
    return (jnp.stack(slot_list, axis=1), jnp.stack(alive_list, axis=1))


def path_levels(path_slots, path_alive, slot_count):
    depth = path_slots.shape[1]
    slots = jnp.arange(slot_count, dtype=jnp.int32)
    hit = path_alive[None] & (path_slots[None] == slots[:, None, None])
    levels = jnp.arange(depth, dtype=jnp.int32)
    return depth - jnp.sum(jnp.where(hit, depth - levels, 0), axis=2)


def spread_experts(grad):
    share = lax.psum_scatter(grad.astype(jnp.bfloat16), "shard", scatter_dimension=1, tiled=True)
    return lax.all_gather(share, "rep", axis=0, tiled=True).astype(jnp.float32)


def spread_columns(grad, rep_count):
    rows, width = grad.shape
    pieces = grad.astype(jnp.bfloat16).reshape(rows, rep_count, width // rep_count).transpose(1, 0, 2)
    part = lax.psum_scatter(pieces, "rep", scatter_dimension=0, tiled=True)[0]
    share = lax.psum_scatter(part, "shard", scatter_dimension=0, tiled=True)
    whole = lax.all_gather(share, "rep", axis=1, tiled=True)
    return whole.astype(jnp.float32)


def shards(
    tokens,
    norm_gains,
    qkv_weight,
    out_weight,
    router_weight,
    gate_up_weight,
    down_weight,
    routes,
    placement,
    parents,
    cotangent,
):
    shard_index = lax.axis_index("shard")
    rep_index = lax.axis_index("rep")
    shard_count = lax.axis_size("shard")
    token_count = tokens.shape[0]
    seg_dev = token_count // SEG
    depth = TRUNK + 2
    width_q = H * HD
    width_kv = KVH * HD
    group_size = TREE_DEVS * seg_dev
    tree_count = group_size // TREE_SEGS
    member = shard_index % TREE_DEVS
    group = (rep_index * shard_count + shard_index) // TREE_DEVS
    group_ids = lax.dynamic_slice_in_dim(placement, group * group_size, group_size)
    group_parents = lax.dynamic_slice_in_dim(parents, group * tree_count, tree_count)
    local_ids = lax.dynamic_slice_in_dim(group_ids, member * seg_dev, seg_dev)
    path_slots, path_alive = ancestor_slots(local_ids, group_ids, group_parents, depth)
    rep_count = lax.axis_size("rep")
    own_experts = E // rep_count
    first_expert = rep_index * own_experts
    padding = jnp.zeros((norm_gains.shape[1], LANES - E - 2), jnp.bfloat16)
    small = jnp.concatenate([router_weight, norm_gains.T, padding], axis=1)
    w_qkv, w_out, small = gather_weights(qkv_weight, out_weight, small, shard_count, rep_count)
    w_qkv = w_qkv.reshape(rep_count, D, -1)
    w_out = w_out.reshape(rep_count, D, -1)
    small = small.reshape(D, LANES)
    w_router = small[:, :E]
    gains = small[:, E : E + 2].T
    gate_up_own = lax.dynamic_slice_in_dim(gate_up_weight, first_expert, own_experts)
    down_own = lax.dynamic_slice_in_dim(down_weight, first_expert, own_experts)
    cot_all = lax.all_gather(cotangent, "rep", axis=0, tiled=True)
    gain_first = gains[0].astype(jnp.float32)
    gain_second = gains[1].astype(jnp.float32)
    token_values = tokens.astype(jnp.float32)
    normed_first, scale_first = norm_rows(token_values, gain_first)
    act_first = normed_first.astype(jnp.bfloat16)
    projected = jnp.einsum("td,rdc->trc", act_first, w_qkv, preferred_element_type=jnp.float32)
    projected = projected.reshape(token_count, width_q + 2 * width_kv)
    queries = projected[:, :width_q].astype(jnp.bfloat16)
    own_kv = projected[:, width_q:].astype(jnp.bfloat16).reshape(seg_dev, SEG, 2 * width_kv)
    low_first = member % 2 == 0
    pair_first = member // 2 == 0
    bias = jnp.where(path_alive, 0.0, NEG).astype(jnp.float32)
    attended, log_totals, group_kv, w_gate_up, w_down = attend_gather(
        path_slots, bias, queries, own_kv, gate_up_own, down_own, depth, shard_count
    )
    w_gate_up = w_gate_up.reshape(own_experts, D, -1)
    w_down = w_down.reshape(own_experts, FF, D)
    mixed_out = jnp.einsum("td,rdc->trc", attended, w_out, preferred_element_type=jnp.float32)
    residual = token_values + mixed_out.reshape(token_count, D)
    normed_second, scale_second = norm_rows(residual, gain_second)
    act_second = normed_second.astype(jnp.bfloat16)
    logits = jnp.dot(act_second, w_router, preferred_element_type=jnp.float32)
    expert_ids = jnp.arange(E, dtype=jnp.int32)
    picks = routes[:, :, None] == expert_ids[None, None, :]
    chosen = jnp.sum(jnp.where(picks, logits[:, None, :], 0.0), axis=-1)
    gates = jax.nn.softmax(chosen, axis=-1)
    upstream = cotangent.astype(jnp.float32)
    gate_table = jnp.sum(jnp.where(picks, gates[:, :, None], 0.0), axis=1)
    act_all = lax.all_gather(act_second, "rep", axis=0, tiled=True)
    gate_all = lax.all_gather(gate_table, "rep", axis=0, tiled=True)
    own_gate = lax.dynamic_slice_in_dim(gate_all, first_expert, own_experts, axis=1).T[:, :, None]
    gate_up = jnp.einsum("td,edf->etf", act_all, w_gate_up, preferred_element_type=jnp.float32)
    gate_part = gate_up[..., :FF]
    up_part = gate_up[..., FF:]
    sig_gate = jax.nn.sigmoid(gate_part)
    hidden = gate_part * sig_gate * up_part
    gated = (hidden * own_gate).astype(jnp.bfloat16)
    mix_part = jnp.einsum("etf,efd->td", gated, w_down, preferred_element_type=jnp.float32)
    mixture = lax.psum_scatter(mix_part.astype(jnp.bfloat16), "rep", scatter_dimension=0, tiled=True)
    block_out = (residual + mixture.astype(jnp.float32)).astype(jnp.bfloat16)
    raw_grad = jnp.einsum("td,efd->etf", cot_all, w_down, preferred_element_type=jnp.float32)
    gate_grad_own = jnp.sum(hidden * raw_grad, axis=-1)
    gate_grad_all = lax.all_gather(gate_grad_own, "rep", axis=0, tiled=True)
    gate_grad_table = lax.dynamic_slice_in_dim(
        gate_grad_all, rep_index * token_count, token_count, axis=1
    ).T
    inner_gate = jnp.sum(gate_table * gate_grad_table, axis=-1, keepdims=True)
    logit_grad = gate_table * (gate_grad_table - inner_gate)
    router_grad = jnp.dot(
        act_second.astype(jnp.float32).T,
        logit_grad,
        precision=lax.Precision.HIGHEST,
        preferred_element_type=jnp.float32,
    )
    hidden_grad = raw_grad * own_gate
    gate_grad_part = hidden_grad * up_part * sig_gate * (1.0 + gate_part * (1.0 - sig_gate))
    up_grad_part = hidden_grad * gate_part * sig_gate
    gate_up_grad_rows = jnp.concatenate([gate_grad_part, up_grad_part], axis=-1).astype(
        jnp.bfloat16
    )
    down_grad = jnp.einsum("etf,td->efd", gated, cot_all, preferred_element_type=jnp.float32)
    gate_up_grad = jnp.einsum(
        "td,etf->edf", act_all, gate_up_grad_rows, preferred_element_type=jnp.float32
    )
    down_grad = spread_experts(down_grad)
    gate_up_grad = spread_experts(gate_up_grad)
    act_part = jnp.einsum(
        "etf,edf->td", gate_up_grad_rows, w_gate_up, preferred_element_type=jnp.float32
    )
    act_second_grad = lax.psum_scatter(
        act_part.astype(jnp.bfloat16), "rep", scatter_dimension=0, tiled=True
    ).astype(jnp.float32)
    act_second_grad = act_second_grad + jnp.dot(
        logit_grad,
        w_router.astype(jnp.float32).T,
        precision=lax.Precision.HIGHEST,
        preferred_element_type=jnp.float32,
    )
    through_second, gain_grad_second = norm_back(
        residual, scale_second, gains[1].astype(jnp.float32), act_second_grad
    )
    residual_grad = upstream + through_second
    branch_grad = residual_grad.astype(jnp.bfloat16)
    out_grad = jnp.dot(attended.T, branch_grad, preferred_element_type=jnp.float32)
    attended_grad = jnp.einsum(
        "trc,rdc->td",
        branch_grad.reshape(token_count, rep_count, D // rep_count),
        w_out,
        preferred_element_type=jnp.float32,
    ).astype(jnp.bfloat16)
    query_grad, group_grad = attn_bwd(
        path_slots,
        bias,
        path_levels(path_slots, path_alive, group_size),
        queries,
        group_kv,
        attended,
        attended_grad,
        log_totals,
        depth,
    )
    pair_part = jnp.where(pair_first, group_grad[: 2 * seg_dev], group_grad[2 * seg_dev :])
    far_part = jnp.where(pair_first, group_grad[2 * seg_dev :], group_grad[: 2 * seg_dev])
    pair_sum = pair_part.astype(jnp.float32) + partner(far_part, "shard", 1).astype(jnp.float32)
    own_part = jnp.where(low_first, pair_sum[:seg_dev], pair_sum[seg_dev:])
    near_part = jnp.where(low_first, pair_sum[seg_dev:], pair_sum[:seg_dev])
    own_grad = own_part + partner(near_part.astype(jnp.bfloat16), "shard", 0).astype(
        near_part.dtype
    )
    projected_grad = jnp.concatenate(
        [query_grad, own_grad.reshape(token_count, 2 * width_kv).astype(jnp.bfloat16)], axis=1
    )
    qkv_grad = jnp.dot(act_first.T, projected_grad, preferred_element_type=jnp.float32)
    act_first_grad = jnp.einsum(
        "trc,rdc->td",
        projected_grad.reshape(token_count, rep_count, -1),
        w_qkv,
        preferred_element_type=jnp.float32,
    )
    through_first, gain_grad_first = norm_back(
        token_values, scale_first, gains[0].astype(jnp.float32), act_first_grad
    )
    token_grad = residual_grad + through_first
    gains_grad = jnp.stack([gain_grad_first, gain_grad_second], axis=1)
    small = jnp.concatenate([gains_grad, router_grad], axis=1)
    small = lax.psum_scatter(small, "shard", scatter_dimension=0, tiled=True)
    small = lax.psum(small, "rep")
    qkv_grad = spread_columns(qkv_grad, rep_count)
    out_grad = spread_columns(out_grad, rep_count)
    return (block_out, token_grad, small[:, :2].T, qkv_grad, out_grad, small[:, 2:], gate_up_grad, down_grad)


def solution(mesh):
    in_specs = (
        P(("rep", "shard"), None),
        P(None, "shard"),
        P("shard", None),
        P("shard", None),
        P("shard", None),
        P(None, "shard", None),
        P(None, "shard", None),
        P(("rep", "shard"), None),
        P(),
        P(),
        P(("rep", "shard"), None),
    )
    out_specs = (
        P(("rep", "shard"), None),
        P(("rep", "shard"), None),
        P(None, "shard"),
        P("shard", None),
        P("shard", None),
        P("shard", None),
        P(None, "shard", None),
        P(None, "shard", None),
    )
    return jax.shard_map(shards, mesh=mesh, in_specs=in_specs, out_specs=out_specs, check_vma=False)
```

```python
import functools

import jax
import jax.experimental.pallas as pl
import jax.experimental.pallas.tpu as pltpu
import jax.numpy as jnp
from jax import lax
from jax.sharding import PartitionSpec as P

D = 1536
H = 24
KVH = 8
HD = 64
FF = 512
TOP = 8
E = 16
SEG = 128
TRUNK = 8
TREE_DEVS = 4
TREE_SEGS = 20
CAP = 352


EPS = 1e-06


PAIRS = KVH // 2
LANES = 2 * HD
NEG=-1e30
def low_half(): return lax.broadcasted_iota(jnp.int32,(SEG,LANES),1)<HD
def stack_heads(ref, row, pair, factor=None):
    low=low_half()
    t=[ref[pl.ds(row,SEG), pl.ds(pl.multiple_of((3*pair+i)*LANES,LANES),LANES)].astype(jnp.float32) for i in range(3)]
    if factor is not None: t=[x*factor for x in t]
    z=jnp.zeros_like(t[0])
    r0=pltpu.roll(t[0],HD,1); r2=pltpu.roll(t[2],HD,1)
    parts=[jnp.where(low,t[0],z),jnp.where(low,r0,z),jnp.where(low,t[1],z),
           jnp.where(low,z,t[1]),jnp.where(low,z,r2),jnp.where(low,z,t[2])]
    return jnp.concatenate(parts,axis=0)
def unstack_heads(rows):
    low=low_half()
    a=[rows[i*SEG:(i+1)*SEG] for i in range(6)]
    return [jnp.where(low,a[0],pltpu.roll(a[1],HD,1)), jnp.where(low,a[2],a[3]), jnp.where(low,pltpu.roll(a[4],HD,1),a[5])]
def kv_path(kv_ref, slots, seg, depth, col):
    return jnp.concatenate([kv_ref[slots[seg,lev],:,pl.ds(pl.multiple_of(col,LANES),LANES)] for lev in range(depth)],axis=0)
NT=(((1,),(1,)),((),())); NN=(((1,),(0,)),((),())); TN=(((0,),(0,)),((),()))
def dot(a,b,dims): return lax.dot_general(a,b,dims,preferred_element_type=jnp.float32)
def causal_bias(width):
    key=lax.broadcasted_iota(jnp.int32,(SEG,width),0); qry=lax.broadcasted_iota(jnp.int32,(SEG,width),1)%SEG
    return jnp.where(key<=qry,0.0,NEG)
def fwd_step(depth, slots, bias, q_ref, kv_ref, o_ref, lse_ref, s_scr, p_scr, i, c):
    width=6*SEG
    seg=i//PAIRS; pair=i%PAIRS
    row=pl.multiple_of(seg*SEG,SEG)
    q6=stack_heads(q_ref,row,pair,HD**-0.5).astype(jnp.bfloat16)
    top=jnp.full((8,width),NEG,jnp.float32)
    for lev in range(depth):
        k=kv_ref[slots[seg,lev],:,pl.ds(pl.multiple_of(pair*LANES,LANES),LANES)]
        s=dot(k,q6,NT)
        s=s+(causal_bias(width) if lev==0 else bias[seg,lev])
        s_scr[lev*SEG:(lev+1)*SEG,:]=s
        top=jnp.maximum(top,jnp.max(s.reshape(SEG//8,8,width),axis=0))
    top=jnp.max(top,axis=0,keepdims=True)
    tot=jnp.zeros((8,width),jnp.float32)
    acc=jnp.zeros((LANES,width),jnp.float32)
    for lev in range(depth):
        p=jnp.exp(s_scr[lev*SEG:(lev+1)*SEG,:]-top)
        tot=tot+jnp.sum(p.reshape(SEG//8,8,width),axis=0)
        p_scr[lev*SEG:(lev+1)*SEG,:]=p.astype(jnp.bfloat16)
    v=kv_path(kv_ref,slots,seg,depth,KVH*HD+pair*LANES)
    acc=dot(v,p_scr[...],TN)
    tot=jnp.sum(tot,axis=0,keepdims=True)
    lse_ref[i]=jnp.broadcast_to(top+jnp.log(tot),(8,width))
    o6=(acc/tot).T
    for j,t in enumerate(unstack_heads(o6)):
        o_ref[pl.ds(row,SEG),pl.ds(pl.multiple_of((3*pair+j)*LANES,LANES),LANES)]=t.astype(o_ref.dtype)
    return c
def bwd_step(depth, slots, bias, q_ref, kv_ref, o_ref, do_ref, lse_ref, dq_ref, path, p_scr, d_scr, i, c):
    width=6*SEG
    seg=i//PAIRS; pair=i%PAIRS
    row=pl.multiple_of(seg*SEG,SEG)
    q6=stack_heads(q_ref,row,pair,HD**-0.5).astype(jnp.bfloat16)
    do6f=stack_heads(do_ref,row,pair)
    do6=do6f.astype(jnp.bfloat16)
    prod=do6f*stack_heads(o_ref,row,pair)
    hi=prod.astype(jnp.bfloat16); lo=(prod-hi.astype(jnp.float32)).astype(jnp.bfloat16)
    ones=jnp.ones((8,LANES),jnp.bfloat16)
    delta=(dot(ones,hi,NT)+dot(ones,lo,NT))[:1]
    lse=lse_ref[i][:1]
    kcol=pl.multiple_of(pair*LANES,LANES); vcol=pl.multiple_of(KVH*HD+pair*LANES,LANES)
    for lev in range(depth):
        k=kv_ref[slots[seg,lev],:,pl.ds(kcol,LANES)]
        v=kv_ref[slots[seg,lev],:,pl.ds(vcol,LANES)]
        s=dot(k,q6,NT)
        s=s+(causal_bias(width) if lev==0 else bias[seg,lev])
        p=jnp.exp(s-lse)
        dp=dot(v,do6,NT)
        ds=(p*(dp-delta)).astype(jnp.bfloat16)
        p_scr[lev*SEG:(lev+1)*SEG,:]=p.astype(jnp.bfloat16)
        d_scr[lev*SEG:(lev+1)*SEG,:]=ds
    dv=dot(p_scr[...],do6,NN)
    dk=dot(d_scr[...],q6,NN)
    for lev in range(depth):
        path[seg,lev,:,pl.ds(kcol,LANES)]=dk[lev*SEG:(lev+1)*SEG].astype(path.dtype)
        path[seg,lev,:,pl.ds(vcol,LANES)]=dv[lev*SEG:(lev+1)*SEG].astype(path.dtype)
    k=kv_path(kv_ref,slots,seg,depth,pair*LANES)
    dq6=(dot(k,d_scr[...],TN)*(HD**-0.5)).T
    for j,t in enumerate(unstack_heads(dq6)):
        dq_ref[pl.ds(row,SEG),pl.ds(pl.multiple_of((3*pair+j)*LANES,LANES),LANES)]=t.astype(dq_ref.dtype)
    return c
def bwd_collect(inv, path, group, slot, c):
    for col in range(0,2*KVH*HD,256):
        tot=path[0,inv[slot,0],:,col:col+256].astype(jnp.float32)
        for seg in range(1,path.shape[0]): tot=tot+path[seg,inv[slot,seg],:,col:col+256].astype(jnp.float32)
        group[slot,:,col:col+256]=tot.astype(group.dtype)
    return c
MESH = pl.DeviceIdType.MESH
ANY = pl.BlockSpec(memory_space=pl.ANY)
VMEM = pl.BlockSpec(memory_space=pltpu.VMEM)
SMEM = pl.BlockSpec(memory_space=pltpu.SMEM)


class Sends:
    def __init__(self):
        self.open = []

    def start(self, cond, src, dst, send_sem, recv_sem, device):
        copy = pltpu.make_async_remote_copy(
            src_ref=src, dst_ref=dst, send_sem=send_sem, recv_sem=recv_sem, device_id=device, device_id_type=MESH
        )
        when(cond, copy.start)
        self.open.append((cond, copy.wait_send))

    def local(self, src, dst, sem):
        copy = pltpu.make_async_copy(src, dst, sem)
        copy.start()
        self.open.append((None, copy.wait))

    def drain(self):
        for cond, wait in self.open:
            when(cond, wait)
        self.open = []


def when(cond, body):
    if cond is None:
        body()
    else:
        pl.when(cond)(body)


def received(cond, region, send_sem, recv_sem, device):
    copy = pltpu.make_async_remote_copy(
        src_ref=region, dst_ref=region, send_sem=send_sem, recv_sem=recv_sem, device_id=device, device_id_type=MESH
    )
    when(cond, copy.wait_recv)


def line_place(shards):
    me = lax.axis_index("shard")
    return me, me // 2, shards // 2


def greet(devices):
    barrier = pltpu.get_barrier_semaphore()
    count = 0
    for cond, device in devices:
        when(
            cond,
            lambda device=device: pl.semaphore_signal(barrier, inc=1, device_id=device, device_id_type=MESH),
        )
        count = count + (1 if cond is None else cond.astype(jnp.int32))
    pl.semaphore_wait(barrier, count)


def line_neighbours(shards):
    me, spot, length = line_place(shards)
    return [
        (None, {"shard": me + 1 - 2 * (me % 2)}),
        (spot > 0, {"shard": me - 2}),
        (spot + 1 < length, {"shard": me + 2}),
    ]


class LineGather:
    def __init__(self, shards, sources, region, up, down, pair, local_sem, arrived=None):
        self.shards, self.sources, self.region = shards, sources, region
        self.up, self.down, self.pair, self.local_sem = up, down, pair, local_sem
        self.arrived = arrived or (lambda cond, block, index: None)
        self.sends = Sends()
        self.me, self.spot, self.length = line_place(shards)
        self.twin = self.me + 1 - 2 * (self.me % 2)

    def forward(self, cond, block, step, rising, falling, src=None):
        place = step if rising else self.length - 1 + step
        for n in range(len(self.sources)):
            here = self.region(n, block)
            out = here if src is None else src[n]
            ways = []
            if rising:
                ways.append((both(cond, self.spot + 1 < self.length), self.up, step + 1, self.me + 2))
            if falling:
                ways.append((both(cond, self.spot > 0), self.down, step + 1, self.me - 2))
            for where, sems, index, device in ways:
                if index < self.length:
                    self.sends.start(where, out, here, sems.at[0, index, n], sems.at[1, index, n], {"shard": device})
            self.sends.start(
                cond, out, here, self.pair.at[0, place, n], self.pair.at[1, place, n], {"shard": self.twin}
            )

    def begin(self):
        for n, src in enumerate(self.sources):
            self.sends.local(src, self.region(n, self.me), self.local_sem.at[n])
        self.forward(None, self.me, 0, True, True, self.sources)

    def finish_local(self):
        for cond, wait in self.sends.open[: len(self.sources)]:
            wait()
        self.sends.open = self.sends.open[len(self.sources) :]

    def step(self, step):
        for sems, cond, block, rising in (
            (self.up, self.spot - step >= 0, self.me - 2 * step, True),
            (self.down, self.spot + step < self.length, self.me + 2 * step, False),
        ):
            for n in range(len(self.sources)):
                received(cond, self.region(n, block), sems.at[0, step, n], sems.at[1, step, n], {"shard": self.twin})
            self.forward(cond, block, step, rising, not rising)
            self.arrived(cond, block, step if rising else self.length - 1 + step)

    def pair_step(self, step):
        turns = [(None, self.twin, 0)] if step == 0 else [
            (self.spot - step >= 0, self.twin - 2 * step, step),
            (self.spot + step < self.length, self.twin + 2 * step, self.length - 1 + step),
        ]
        for cond, block, place in turns:
            for n in range(len(self.sources)):
                received(
                    cond, self.region(n, block), self.pair.at[0, place, n], self.pair.at[1, place, n], {"shard": self.twin}
                )
            self.arrived(cond, block, 2 * self.length - 1 + place)


def both(first, second):
    return second if first is None else jnp.logical_and(first, second)


def line_sems(shards, arrays):
    length = shards // 2
    return [
        pltpu.SemaphoreType.DMA((2, length, arrays)),
        pltpu.SemaphoreType.DMA((2, length, arrays)),
        pltpu.SemaphoreType.DMA((2, 2 * length - 1, arrays)),
        pltpu.SemaphoreType.DMA((arrays,)),
    ]


class RepSpread:
    def __init__(self, arrays, region, cross, core, relay):
        self.arrays, self.region = arrays, region
        self.cross, self.core, self.relay = cross, core, relay
        rep = lax.axis_index("rep")
        self.rep = rep
        self.near = rep + 1 - 2 * (rep % 2)
        self.far = lax.rem(rep + 2, 4)
        self.diagonal = lax.rem(self.near + 2, 4)
        self.sends = Sends()
        self.blocks = []
        self.passed = []
        self.sources = None

    def arrived(self, cond, block, index):
        for n in self.arrays:
            here = self.region(n, self.rep, block)
            src = here if self.sources is None else self.sources[n]
            self.sends.start(
                cond, src, here, self.cross.at[0, block, n], self.cross.at[1, block, n], {"rep": self.far}
            )
            self.sends.start(
                cond, src, here, self.core.at[0, block, n], self.core.at[1, block, n], {"rep": self.near}
            )
        self.blocks.append((cond, block))

    def pass_on(self):
        for cond, block in self.blocks:
            for n in self.arrays:
                here = self.region(n, self.far, block)
                received(cond, here, self.cross.at[0, block, n], self.cross.at[1, block, n], {"rep": self.far})
                self.sends.start(
                    cond, here, here, self.relay.at[0, block, n], self.relay.at[1, block, n], {"rep": self.near}
                )
        self.passed = self.passed + self.blocks
        self.blocks = []

    def end(self):
        self.pass_on()
        for cond, block in self.passed:
            for n in self.arrays:
                for sems, part in ((self.core, self.near), (self.relay, self.diagonal)):
                    here = self.region(n, part, block)
                    received(cond, here, sems.at[0, block, n], sems.at[1, block, n], {"rep": self.near})
        self.sends.drain()


def rep_neighbours():
    rep = lax.axis_index("rep")
    return [(None, {"rep": rep + 1 - 2 * (rep % 2)}), (None, {"rep": lax.rem(rep + 2, 4)})]


def rep_sems(shards, arrays):
    return [pltpu.SemaphoreType.DMA((2, shards, arrays)) for unused in range(3)]


def weights_kernel(shards, qkv, out, small, qkv_all, out_all, small_all, up, down, pair, local_sem, cross, core, relay):
    rep = lax.axis_index("rep")
    greet(line_neighbours(shards) + rep_neighbours())
    refs = (qkv_all, out_all, small_all)

    def part(n, owner, block):
        return refs[n].at[block] if n == 2 else refs[n].at[owner, block]

    def columns(ref, width):
        return ref.at[:, pl.ds(pl.multiple_of(rep * width, LANES), width)]

    spread = RepSpread((0, 1), part, cross, core, relay)
    sources = (columns(qkv, qkv_all.shape[-1]), columns(out, out_all.shape[-1]), small)
    gather = LineGather(
        shards, sources, lambda n, block: part(n, rep, block), up, down, pair, local_sem, spread.arrived
    )
    gather.begin()
    gather.finish_local()
    spread.arrived(None, gather.me, 0)
    for step in range(gather.length):
        if step:
            gather.step(step)
        spread.pass_on()
        gather.pair_step(step)
    spread.end()
    gather.sends.drain()


def gather_weights(qkv_weight, out_weight, small, shards, reps):
    rows = qkv_weight.shape[0]
    shapes = [
        (reps, shards, rows, qkv_weight.shape[1] // reps),
        (reps, shards, rows, out_weight.shape[1] // reps),
        (shards,) + small.shape,
    ]
    return pl.pallas_call(
        functools.partial(weights_kernel, shards),
        out_shape=[jax.ShapeDtypeStruct(shape, jnp.bfloat16) for shape in shapes],
        in_specs=[ANY] * 3,
        out_specs=[ANY] * 3,
        scratch_shapes=line_sems(shards, 3) + rep_sems(shards, 2),
        compiler_params=pltpu.CompilerParams(collective_id=1, has_side_effects=True),
    )(qkv_weight, out_weight, small)


def attend_gather_kernel(
    depth,
    shards,
    slots,
    bias,
    q_ref,
    kv_ref,
    gu_ref,
    dn_ref,
    o_ref,
    lse_ref,
    kv_all,
    gu_all,
    dn_all,
    s_scr,
    p_scr,
    kv_sems,
    up,
    down,
    pair,
    local_sem,
):
    me = lax.axis_index("shard")
    first = me // TREE_DEVS * TREE_DEVS
    member = me % TREE_DEVS
    seg_dev = kv_ref.shape[0]
    others = [first + lax.rem(member + away, TREE_DEVS) for away in range(1, TREE_DEVS)]
    greet(line_neighbours(shards) + [(None, {"shard": other}) for other in others])
    sends = Sends()
    own = kv_all.at[pl.ds(member * seg_dev, seg_dev)]
    for away, other in enumerate(others):
        sends.start(None, kv_ref, own, kv_sems.at[0, away], kv_sems.at[1, away], {"shard": other})
    gather = LineGather(
        shards,
        (gu_ref, dn_ref),
        lambda n, block: (gu_all, dn_all)[n].at[:, block],
        up,
        down,
        pair,
        local_sem,
    )
    gather.begin()
    kv_all[pl.ds(member * seg_dev, seg_dev)] = kv_ref[...]
    for away in range(TREE_DEVS - 1):
        source = lax.rem(member + TREE_DEVS - 1 - away, TREE_DEVS)
        block = kv_all.at[pl.ds(source * seg_dev, seg_dev)]
        received(None, block, kv_sems.at[0, away], kv_sems.at[1, away], {"shard": first + source})
    count = seg_dev * PAIRS
    attend = functools.partial(fwd_step, depth, slots, bias, q_ref, kv_all, o_ref, lse_ref, s_scr, p_scr)
    done = 0
    for step in range(1, gather.length):
        upto = count * step // (gather.length - 1)
        lax.fori_loop(done, upto, attend, 0)
        done = upto
        gather.step(step)
    for step in range(gather.length):
        gather.pair_step(step)
    gather.sends.drain()
    sends.drain()


def attend_gather(slots, bias, q, kv, gate_up, down, depth, shards):
    tokens = q.shape[0]
    count = tokens // SEG * PAIRS
    experts, rows = gate_up.shape[:2]
    return pl.pallas_call(
        functools.partial(attend_gather_kernel, depth, shards),
        out_shape=(
            jax.ShapeDtypeStruct(q.shape, jnp.bfloat16),
            jax.ShapeDtypeStruct((count, 8, 6 * SEG), jnp.float32),
            jax.ShapeDtypeStruct((TREE_DEVS * kv.shape[0],) + kv.shape[1:], jnp.bfloat16),
            jax.ShapeDtypeStruct((experts, shards, rows) + gate_up.shape[2:], jnp.bfloat16),
            jax.ShapeDtypeStruct((experts, shards) + down.shape[1:], jnp.bfloat16),
        ),
        in_specs=[SMEM, SMEM, VMEM, VMEM, ANY, ANY],
        out_specs=(VMEM, VMEM, VMEM, ANY, ANY),
        scratch_shapes=[
            pltpu.VMEM((depth * SEG, 6 * SEG), jnp.float32),
            pltpu.VMEM((depth * SEG, 6 * SEG), jnp.bfloat16),
            pltpu.SemaphoreType.DMA((2, TREE_DEVS - 1)),
        ]
        + line_sems(shards, 2),
        compiler_params=pltpu.CompilerParams(
            collective_id=2, has_side_effects=True, vmem_limit_bytes=48 * 2**20
        ),
    )(slots, bias, q, kv, gate_up, down)


class LineScatter:
    def __init__(self, shards, arrays, local, pair_buf, line_buf, temp, stages, outs, pair, line, loads, ready=None):
        self.shards, self.arrays, self.local = shards, arrays, local
        self.pair_buf, self.line_buf, self.temp = pair_buf, line_buf, temp
        self.stages, self.outs = stages, outs
        self.pair, self.line, self.loads = pair, line, loads
        self.ready = ready or (lambda block: None)
        self.sends = Sends()
        self.me, self.spot, self.length = line_place(shards)
        self.side = self.me % 2
        self.twin = self.me + 1 - 2 * self.side

    def add(self, n, sources, target):
        stage, out = self.stages[n], self.outs[n]
        copies = []
        for k, (cond, ref) in enumerate(sources):
            copy = pltpu.make_async_copy(ref, stage.at[k], self.loads.at[k])
            copies.append((cond, copy))
            when(cond, copy.start)
        outer, rows, width = out.shape
        chunk = 32 if rows % 32 == 0 else rows
        pieces = rows // chunk

        def clear(k):
            def one(i, c):
                row = pl.multiple_of(i % pieces * chunk, chunk)
                stage[k, i // pieces, pl.ds(row, chunk)] = jnp.zeros((chunk, width), stage.dtype)
                return c

            lax.fori_loop(0, outer * pieces, one, 0)

        for k, (cond, copy) in enumerate(copies):
            when(cond, copy.wait)
            if cond is not None:
                pl.when(jnp.logical_not(cond))(functools.partial(clear, k))

        def one(i, c):
            row = pl.multiple_of(i % pieces * chunk, chunk)
            total = stage[0, i // pieces, pl.ds(row, chunk)].astype(jnp.float32)
            for k in range(1, len(sources)):
                total = total + stage[k, i // pieces, pl.ds(row, chunk)].astype(jnp.float32)
            out[i // pieces, pl.ds(row, chunk)] = total.astype(out.dtype)
            return c

        lax.fori_loop(0, outer * pieces, one, 0)
        store = pltpu.make_async_copy(out, target, self.loads.at[self.loads.shape[0] - 1])
        store.start()
        store.wait()

    def begin(self):
        order = []
        for step in range(self.length):
            for target in (self.length - 1 - step, step):
                if target not in order:
                    order.append(target)
        for target in order:
            block = 2 * target + 1 - self.side
            self.ready(block)
            for n in range(self.arrays):
                sources = self.local(n, block)
                src = sources[0]
                if len(sources) > 1:
                    src = self.temp[n].at[target]
                    self.add(n, [(None, ref) for ref in sources], src)
                self.sends.start(
                    None,
                    src,
                    self.pair_buf[n].at[target],
                    self.pair.at[0, target, n],
                    self.pair.at[1, target, n],
                    {"shard": self.twin},
                )

    def got_pair(self, target, n):
        received(
            None,
            self.pair_buf[n].at[target],
            self.pair.at[0, target, n],
            self.pair.at[1, target, n],
            {"shard": self.twin},
        )

    def got_line(self, cond, slot, n, device):
        received(cond, self.line_buf[n].at[slot], self.line.at[0, slot, n], self.line.at[1, slot, n], {"shard": device})

    def step(self, step):
        below, above = self.spot > 0, self.spot + 1 < self.length
        turns = (
            (self.length - 1 - step, True, below, self.me - 2, self.me + 2),
            (step, False, above, self.me + 2, self.me - 2),
        )
        for target, rising, has, source, device in turns:
            cond = self.spot < target if rising else self.spot > target
            block = 2 * target + self.side
            slot = target if rising else jnp.where(self.spot == target + 1, self.length, target)
            for n in range(self.arrays):
                copy = pltpu.make_async_remote_copy(
                    src_ref=self.pair_buf[n].at[target],
                    dst_ref=self.line_buf[n].at[slot],
                    send_sem=self.line.at[0, slot, n],
                    recv_sem=self.line.at[1, slot, n],
                    device_id={"shard": device},
                    device_id_type=MESH,
                )

                def body(n=n, copy=copy, target=target, has=has, source=source, block=block):
                    self.got_pair(target, n)
                    self.got_line(has, target, n, source)
                    if n == 0:
                        self.ready(block)
                    sources = [(None, ref) for ref in self.local(n, block)]
                    sources += [(None, self.pair_buf[n].at[target]), (has, self.line_buf[n].at[target])]
                    self.add(n, sources, self.pair_buf[n].at[target])
                    copy.start()

                pl.when(cond)(body)
                self.sends.open.append((cond, copy.wait_send))

    def finish(self, targets):
        below, above = self.spot > 0, self.spot + 1 < self.length
        self.ready(self.me)
        for n in range(self.arrays):
            self.got_pair(self.spot, n)
            self.got_line(below, self.spot, n, self.me - 2)
            self.got_line(above, self.length, n, self.me + 2)
            sources = [(None, ref) for ref in self.local(n, self.me)]
            sources += [
                (None, self.pair_buf[n].at[self.spot]),
                (below, self.line_buf[n].at[self.spot]),
                (above, self.line_buf[n].at[self.length]),
            ]
            self.add(n, sources, targets[n])


def scatter_sems(shards, arrays, loads):
    length = shards // 2
    return [
        pltpu.SemaphoreType.DMA((2, length, arrays)),
        pltpu.SemaphoreType.DMA((2, length + 1, arrays)),
        pltpu.SemaphoreType.DMA((loads + 1,)),
    ]


def scatter_buffers(shards, block):
    length = shards // 2
    return [
        jax.ShapeDtypeStruct((length,) + block, jnp.bfloat16),
        jax.ShapeDtypeStruct((length + 1,) + block, jnp.bfloat16),
    ]


def back_kernel(
    depth,
    shards,
    slots,
    bias,
    inv,
    q_ref,
    kv_ref,
    o_ref,
    do_ref,
    lse_ref,
    gu_ref,
    dn_ref,
    dq_ref,
    dkv_ref,
    gu_out,
    dn_out,
    gu_pair,
    gu_line,
    dn_pair,
    dn_line,
    path,
    p_scr,
    d_scr,
    group,
    guest,
    gu_stage,
    dn_stage,
    gu_sum,
    dn_sum,
    kv_sems,
    pair,
    line,
    loads,
):
    me = lax.axis_index("shard")
    first = me // TREE_DEVS * TREE_DEVS
    member = me % TREE_DEVS
    segs = q_ref.shape[0] // SEG
    others = [first + lax.rem(member + away, TREE_DEVS) for away in range(1, TREE_DEVS)]
    greet(line_neighbours(shards) + [(None, {"shard": other}) for other in others])
    scatter = LineScatter(
        shards,
        2,
        lambda n, block: [(gu_ref, dn_ref)[n].at[:, block]],
        (gu_pair, dn_pair),
        (gu_line, dn_line),
        None,
        (gu_stage, dn_stage),
        (gu_sum, dn_sum),
        pair,
        line,
        loads,
    )
    scatter.begin()
    path[:, depth] = jnp.zeros((segs,) + path.shape[2:], path.dtype)
    step = functools.partial(
        bwd_step, depth, slots, bias, q_ref, kv_ref, o_ref, do_ref, lse_ref, dq_ref, path, p_scr, d_scr
    )
    lax.fori_loop(0, segs * PAIRS, step, 0)
    lax.fori_loop(0, group.shape[0], functools.partial(bwd_collect, inv, path, group), 0)
    sends = Sends()
    for away, other in enumerate(others):
        target = lax.rem(member + away + 1, TREE_DEVS)
        sends.start(
            None,
            group.at[pl.ds(target * segs, segs)],
            guest.at[away],
            kv_sems.at[0, away],
            kv_sems.at[1, away],
            {"shard": other},
        )
    for turn in range(scatter.length):
        scatter.step(turn)
    for away in range(TREE_DEVS - 1):
        source = first + lax.rem(member + TREE_DEVS - 1 - away, TREE_DEVS)
        received(None, guest.at[away], kv_sems.at[0, away], kv_sems.at[1, away], {"shard": source})

    def join(seg, c):
        for col in range(0, 2 * KVH * HD, 256):
            total = group[member * segs + seg, :, col : col + 256].astype(jnp.float32)
            for away in range(TREE_DEVS - 1):
                total = total + guest[away, seg, :, col : col + 256].astype(jnp.float32)
            dkv_ref[seg, :, col : col + 256] = total.astype(dkv_ref.dtype)
        return c

    lax.fori_loop(0, segs, join, 0)
    scatter.finish((gu_out, dn_out))
    sends.drain()
    scatter.sends.drain()


def attend_back(slots, bias, inv, q, kv, o, do, lse, gate_up_grad, down_grad, depth, shards):
    segs = q.shape[0] // SEG
    own_kv = (segs,) + kv.shape[1:]
    gu_block = (gate_up_grad.shape[0],) + gate_up_grad.shape[2:]
    dn_block = (down_grad.shape[0],) + down_grad.shape[2:]
    outs = [
        jax.ShapeDtypeStruct(q.shape, jnp.bfloat16),
        jax.ShapeDtypeStruct(own_kv, jnp.bfloat16),
        jax.ShapeDtypeStruct(gu_block, jnp.bfloat16),
        jax.ShapeDtypeStruct(dn_block, jnp.bfloat16),
    ]
    outs += scatter_buffers(shards, gu_block) + scatter_buffers(shards, dn_block)
    return pl.pallas_call(
        functools.partial(back_kernel, depth, shards),
        out_shape=outs,
        in_specs=[SMEM] * 3 + [VMEM] * 5 + [ANY] * 2,
        out_specs=[VMEM] * 2 + [ANY] * 6,
        scratch_shapes=[
            pltpu.VMEM((segs, depth + 1, SEG, 2 * KVH * HD), jnp.bfloat16),
            pltpu.VMEM((depth * SEG, 6 * SEG), jnp.bfloat16),
            pltpu.VMEM((depth * SEG, 6 * SEG), jnp.bfloat16),
            pltpu.VMEM(kv.shape, jnp.bfloat16),
            pltpu.VMEM((TREE_DEVS - 1,) + own_kv, jnp.bfloat16),
            pltpu.VMEM((4,) + gu_block, jnp.bfloat16),
            pltpu.VMEM((4,) + dn_block, jnp.bfloat16),
            pltpu.VMEM(gu_block, jnp.bfloat16),
            pltpu.VMEM(dn_block, jnp.bfloat16),
            pltpu.SemaphoreType.DMA((2, TREE_DEVS - 1)),
        ]
        + scatter_sems(shards, 2, 4),
        compiler_params=pltpu.CompilerParams(
            collective_id=3, has_side_effects=True, vmem_limit_bytes=60 * 2**20
        ),
    )(slots, bias, inv, q, kv, o, do, lse, gate_up_grad, down_grad)[:4]


def finish_kernel(
    shards,
    grad_ref,
    gu_ref,
    dn_ref,
    grad_out,
    gu_out,
    dn_out,
    core_buf,
    share_buf,
    cross_buf,
    pair_buf,
    line_buf,
    temp_buf,
    stage,
    total,
    core_sems,
    swap_sems,
    own_sems,
    cross,
    core,
    relay,
    pair,
    line,
    loads,
):
    rep = lax.axis_index("rep")
    near = rep + 1 - 2 * (rep % 2)
    far = lax.rem(rep + 2, 4)
    half = rep % 2
    greet(line_neighbours(shards) + rep_neighbours())
    sends = Sends()
    length = shards // 2
    order = []
    for step in range(length):
        for target in (length - 1 - step, step):
            if target not in order:
                order.append(target)
    side = lax.axis_index("shard") % 2
    for turn in (1 - side, side):
        for target in order:
            block = 2 * target + turn
            sends.start(
                None,
                grad_ref.at[1 - half, block],
                core_buf.at[block],
                core_sems.at[0, block],
                core_sems.at[1, block],
                {"rep": near},
            )
    experts = (gu_out, dn_out)
    for n, src in enumerate((gu_ref, dn_ref)):
        sends.local(src, experts[n].at[rep], own_sems.at[n])
    spread = RepSpread((0, 1), lambda n, part, block: experts[n].at[part], cross, core, relay)
    spread.sources = (gu_ref, dn_ref)
    spread.arrived(None, 0, 0)

    def ready(block):
        received(None, core_buf.at[block], core_sems.at[0, block], core_sems.at[1, block], {"rep": near})

    scatter = LineScatter(
        shards,
        1,
        lambda n, block: [grad_ref.at[half, block], core_buf.at[block]],
        (pair_buf,),
        (line_buf,),
        (temp_buf,),
        (stage,),
        (total,),
        pair,
        line,
        loads,
        ready,
    )
    scatter.begin()
    for turn in range(scatter.length):
        scatter.step(turn)
    scatter.finish((share_buf,))
    sends.start(None, share_buf, cross_buf, swap_sems.at[0, 0], swap_sems.at[1, 0], {"rep": far})
    spread.end()
    received(None, cross_buf, swap_sems.at[0, 0], swap_sems.at[1, 0], {"rep": far})
    scatter.add(0, [(None, share_buf), (None, cross_buf)], grad_out.at[half])
    sends.start(None, grad_out.at[half], grad_out.at[half], swap_sems.at[0, 1], swap_sems.at[1, 1], {"rep": near})
    received(None, grad_out.at[1 - half], swap_sems.at[0, 1], swap_sems.at[1, 1], {"rep": near})
    sends.drain()
    scatter.sends.drain()


def finish_grads(grad, gate_up_share, down_share, reps):
    halves, shards = grad.shape[:2]
    block = grad.shape[2:]

    def shape(*dims):
        return jax.ShapeDtypeStruct(dims, jnp.bfloat16)

    outs = [
        shape(halves, *block),
        shape(reps, *gate_up_share.shape),
        shape(reps, *down_share.shape),
        shape(shards, *block),
        shape(*block),
        shape(*block),
    ]
    outs += scatter_buffers(shards, block) + [shape(shards // 2, *block)]
    return pl.pallas_call(
        functools.partial(finish_kernel, shards),
        out_shape=outs,
        in_specs=[ANY] * 3,
        out_specs=[ANY] * len(outs),
        scratch_shapes=[
            pltpu.VMEM((5,) + block, jnp.bfloat16),
            pltpu.VMEM(block, jnp.bfloat16),
            pltpu.SemaphoreType.DMA((2, shards)),
            pltpu.SemaphoreType.DMA((2, 2)),
            pltpu.SemaphoreType.DMA((2,)),
        ]
        + rep_sems(1, 2)
        + scatter_sems(shards, 1, 5),
        compiler_params=pltpu.CompilerParams(
            collective_id=4, has_side_effects=True, vmem_limit_bytes=32 * 2**20
        ),
    )(grad, gate_up_share, down_share)[:3]


def norm_rows(values, gain):
    scale_rows = lax.rsqrt(jnp.mean(values * values, axis=-1, keepdims=True) + EPS)
    return (values * scale_rows * gain, scale_rows)


def norm_back(values, scale_rows, gain, upstream):
    scaled = upstream * gain
    inner = jnp.mean(scaled * values, axis=-1, keepdims=True)
    through = scale_rows * scaled - values * (scale_rows * scale_rows * scale_rows) * inner
    gain_grad = jnp.sum(upstream * values * scale_rows, axis=0)
    return (through, gain_grad)


def table_lookup(table, index):
    positions = jnp.arange(table.shape[0], dtype=jnp.int32)
    return jnp.sum(jnp.where(index[:, None] == positions[None, :], table[None, :], 0), axis=1)


def find_slot(group_ids, wanted):
    positions = jnp.arange(group_ids.shape[0], dtype=jnp.int32)
    return jnp.sum(jnp.where(group_ids[None, :] == wanted[:, None], positions[None, :], 0), axis=1)


def ancestor_slots(local_ids, group_ids, group_parents, depth):
    flat_parents = group_parents.reshape(-1)
    tree_index = local_ids // TREE_SEGS
    current = local_ids % TREE_SEGS
    alive = jnp.ones(local_ids.shape, dtype=bool)
    slot_list = []
    alive_list = []
    for level in range(depth):
        wanted = tree_index * TREE_SEGS + current
        slot_list.append(find_slot(group_ids, wanted))
        alive_list.append(alive)
        parent_seg = table_lookup(flat_parents, wanted)
        alive = alive & (parent_seg != current)
        current = parent_seg
    return (jnp.stack(slot_list, axis=1), jnp.stack(alive_list, axis=1))


def path_levels(path_slots, path_alive, slot_count):
    depth = path_slots.shape[1]
    slots = jnp.arange(slot_count, dtype=jnp.int32)
    hit = path_alive[None] & (path_slots[None] == slots[:, None, None])
    levels = jnp.arange(depth, dtype=jnp.int32)
    return depth - jnp.sum(jnp.where(hit, depth - levels, 0), axis=2)


def w_total(width_q, width_kv):
    return width_q + 2 * width_kv + D


def shards(
    tokens,
    norm_gains,
    qkv_weight,
    out_weight,
    router_weight,
    gate_up_weight,
    down_weight,
    routes,
    placement,
    parents,
    cotangent,
):
    shard_index = lax.axis_index("shard")
    rep_index = lax.axis_index("rep")
    shard_count = lax.axis_size("shard")
    token_count = tokens.shape[0]
    seg_dev = token_count // SEG
    depth = TRUNK + 2
    width_q = H * HD
    width_kv = KVH * HD
    group_size = TREE_DEVS * seg_dev
    tree_count = group_size // TREE_SEGS
    member = shard_index % TREE_DEVS
    group = (rep_index * shard_count + shard_index) // TREE_DEVS
    group_ids = lax.dynamic_slice_in_dim(placement, group * group_size, group_size)
    group_parents = lax.dynamic_slice_in_dim(parents, group * tree_count, tree_count)
    local_ids = lax.dynamic_slice_in_dim(group_ids, member * seg_dev, seg_dev)
    path_slots, path_alive = ancestor_slots(local_ids, group_ids, group_parents, depth)
    rep_count = lax.axis_size("rep")
    own_experts = E // rep_count
    first_expert = rep_index * own_experts
    padding = jnp.zeros((norm_gains.shape[1], LANES - E - 2), jnp.bfloat16)
    small = jnp.concatenate([router_weight, norm_gains.T, padding], axis=1)
    w_qkv, w_out, small = gather_weights(qkv_weight, out_weight, small, shard_count, rep_count)
    w_qkv = w_qkv.reshape(rep_count, D, -1)
    w_out = w_out.reshape(rep_count, D, -1)
    small = small.reshape(D, LANES)
    w_router = small[:, :E]
    gains = small[:, E : E + 2].T
    gate_up_own = lax.dynamic_slice_in_dim(gate_up_weight, first_expert, own_experts)
    down_own = lax.dynamic_slice_in_dim(down_weight, first_expert, own_experts)
    cot_all = lax.all_gather(cotangent, "rep", axis=0, tiled=True)
    gain_first = gains[0].astype(jnp.float32)
    gain_second = gains[1].astype(jnp.float32)
    token_values = tokens.astype(jnp.float32)
    normed_first, scale_first = norm_rows(token_values, gain_first)
    act_first = normed_first.astype(jnp.bfloat16)
    projected = jnp.einsum("td,rdc->trc", act_first, w_qkv, preferred_element_type=jnp.float32)
    projected = projected.reshape(token_count, width_q + 2 * width_kv)
    queries = projected[:, :width_q].astype(jnp.bfloat16)
    own_kv = projected[:, width_q:].astype(jnp.bfloat16).reshape(seg_dev, SEG, 2 * width_kv)
    bias = jnp.where(path_alive, 0.0, NEG).astype(jnp.float32)
    attended, log_totals, group_kv, w_gate_up, w_down = attend_gather(
        path_slots, bias, queries, own_kv, gate_up_own, down_own, depth, shard_count
    )
    w_gate_up = w_gate_up.reshape(own_experts, D, -1)
    w_down = w_down.reshape(own_experts, FF, D)
    mixed_out = jnp.einsum("td,rdc->trc", attended, w_out, preferred_element_type=jnp.float32)
    residual = token_values + mixed_out.reshape(token_count, D)
    normed_second, scale_second = norm_rows(residual, gain_second)
    act_second = normed_second.astype(jnp.bfloat16)
    logits = jnp.dot(act_second, w_router, preferred_element_type=jnp.float32)
    expert_ids = jnp.arange(E, dtype=jnp.int32)
    picks = routes[:, :, None] == expert_ids[None, None, :]
    chosen = jnp.sum(jnp.where(picks, logits[:, None, :], 0.0), axis=-1)
    gates = jax.nn.softmax(chosen, axis=-1)
    upstream = cotangent.astype(jnp.float32)
    gate_table = jnp.sum(jnp.where(picks, gates[:, :, None], 0.0), axis=1)
    act_all = lax.all_gather(act_second, "rep", axis=0, tiled=True)
    gate_all = lax.all_gather(gate_table, "rep", axis=0, tiled=True)
    own_gate = lax.dynamic_slice_in_dim(gate_all, first_expert, own_experts, axis=1).T[:, :, None]
    gate_up = jnp.einsum("td,edf->etf", act_all, w_gate_up, preferred_element_type=jnp.float32)
    gate_part = gate_up[..., :FF]
    up_part = gate_up[..., FF:]
    sig_gate = jax.nn.sigmoid(gate_part)
    hidden = gate_part * sig_gate * up_part
    gated = (hidden * own_gate).astype(jnp.bfloat16)
    mix_part = jnp.einsum("etf,efd->td", gated, w_down, preferred_element_type=jnp.float32)
    mixture = lax.psum_scatter(mix_part.astype(jnp.bfloat16), "rep", scatter_dimension=0, tiled=True)
    block_out = (residual + mixture.astype(jnp.float32)).astype(jnp.bfloat16)
    raw_grad = jnp.einsum("td,efd->etf", cot_all, w_down, preferred_element_type=jnp.float32)
    gate_grad_own = jnp.sum(hidden * raw_grad, axis=-1)
    gate_grad_all = lax.all_gather(gate_grad_own, "rep", axis=0, tiled=True)
    gate_grad_table = lax.dynamic_slice_in_dim(
        gate_grad_all, rep_index * token_count, token_count, axis=1
    ).T
    inner_gate = jnp.sum(gate_table * gate_grad_table, axis=-1, keepdims=True)
    logit_grad = gate_table * (gate_grad_table - inner_gate)
    router_grad = jnp.dot(
        act_second.astype(jnp.float32).T,
        logit_grad,
        precision=lax.Precision.HIGHEST,
        preferred_element_type=jnp.float32,
    )
    hidden_grad = raw_grad * own_gate
    gate_grad_part = hidden_grad * up_part * sig_gate * (1.0 + gate_part * (1.0 - sig_gate))
    up_grad_part = hidden_grad * gate_part * sig_gate
    gate_up_grad_rows = jnp.concatenate([gate_grad_part, up_grad_part], axis=-1).astype(
        jnp.bfloat16
    )
    down_grad = jnp.einsum("etf,td->efd", gated, cot_all, preferred_element_type=jnp.float32)
    gate_up_grad = jnp.einsum(
        "td,etf->edf", act_all, gate_up_grad_rows, preferred_element_type=jnp.float32
    )
    act_part = jnp.einsum(
        "etf,edf->td", gate_up_grad_rows, w_gate_up, preferred_element_type=jnp.float32
    )
    act_second_grad = lax.psum_scatter(
        act_part.astype(jnp.bfloat16), "rep", scatter_dimension=0, tiled=True
    ).astype(jnp.float32)
    act_second_grad = act_second_grad + jnp.dot(
        logit_grad,
        w_router.astype(jnp.float32).T,
        precision=lax.Precision.HIGHEST,
        preferred_element_type=jnp.float32,
    )
    through_second, gain_grad_second = norm_back(
        residual, scale_second, gains[1].astype(jnp.float32), act_second_grad
    )
    residual_grad = upstream + through_second
    branch_grad = residual_grad.astype(jnp.bfloat16)
    out_grad = jnp.dot(attended.T, branch_grad, preferred_element_type=jnp.float32)
    attended_grad = jnp.einsum(
        "trc,rdc->td",
        branch_grad.reshape(token_count, rep_count, D // rep_count),
        w_out,
        preferred_element_type=jnp.float32,
    ).astype(jnp.bfloat16)
    query_grad, own_grad, gate_up_share, down_share = attend_back(
        path_slots,
        bias,
        path_levels(path_slots, path_alive, group_size),
        queries,
        group_kv,
        attended,
        attended_grad,
        log_totals,
        gate_up_grad.astype(jnp.bfloat16).reshape(own_experts, shard_count, -1, 2 * FF),
        down_grad.astype(jnp.bfloat16).reshape(own_experts, shard_count, -1, D),
        depth,
        shard_count,
    )
    projected_grad = jnp.concatenate(
        [query_grad, own_grad.reshape(token_count, 2 * width_kv)], axis=1
    )
    qkv_grad = jnp.dot(act_first.T, projected_grad, preferred_element_type=jnp.float32)
    act_first_grad = jnp.einsum(
        "trc,rdc->td",
        projected_grad.reshape(token_count, rep_count, -1),
        w_qkv,
        preferred_element_type=jnp.float32,
    )
    through_first, gain_grad_first = norm_back(
        token_values, scale_first, gains[0].astype(jnp.float32), act_first_grad
    )
    token_grad = residual_grad + through_first
    width = 2 * LANES * -(-(w_total(width_q, width_kv) + E + 2) // (2 * LANES))
    padding = jnp.zeros((D, width - w_total(width_q, width_kv) - E - 2), jnp.float32)
    joined = jnp.concatenate(
        [
            qkv_grad,
            out_grad,
            gain_grad_first[:, None],
            gain_grad_second[:, None],
            router_grad,
            padding,
        ],
        axis=1,
    ).astype(jnp.bfloat16)
    joined = joined.reshape(shard_count, 1, D // shard_count, 2, width // 2).transpose(3, 0, 1, 2, 4)
    joined, gate_up_grad, down_grad = finish_grads(joined, gate_up_share, down_share, rep_count)
    joined = joined.transpose(1, 2, 0, 3).reshape(D // shard_count, width).astype(jnp.float32)
    at_out = width_q + 2 * width_kv
    at_small = at_out + D
    return (
        block_out,
        token_grad,
        joined[:, at_small : at_small + 2].T,
        joined[:, :at_out],
        joined[:, at_out:at_small],
        joined[:, at_small + 2 : at_small + 2 + E],
        gate_up_grad.reshape((E,) + gate_up_grad.shape[2:]).astype(jnp.float32),
        down_grad.reshape((E,) + down_grad.shape[2:]).astype(jnp.float32),
    )


def solution(mesh):
    in_specs = (
        P(("rep", "shard"), None),
        P(None, "shard"),
        P("shard", None),
        P("shard", None),
        P("shard", None),
        P(None, "shard", None),
        P(None, "shard", None),
        P(("rep", "shard"), None),
        P(),
        P(),
        P(("rep", "shard"), None),
    )
    out_specs = (
        P(("rep", "shard"), None),
        P(("rep", "shard"), None),
        P(None, "shard"),
        P("shard", None),
        P("shard", None),
        P("shard", None),
        P(None, "shard", None),
        P(None, "shard", None),
    )
    return jax.shard_map(shards, mesh=mesh, in_specs=in_specs, out_specs=out_specs, check_vma=False)
```

```python
import functools

import jax
import jax.experimental.pallas as pl
import jax.experimental.pallas.tpu as pltpu
import jax.numpy as jnp
from jax import lax
from jax.sharding import PartitionSpec as P

D = 1536
H = 24
KVH = 8
HD = 64
FF = 512
TOP = 8
E = 16
SEG = 128
TRUNK = 8
TREE_DEVS = 4
TREE_SEGS = 20
CAP = 352


EPS = 1e-06


PAIRS = KVH // 2
LANES = 2 * HD
NEG=-1e30
def low_half(): return lax.broadcasted_iota(jnp.int32,(SEG,LANES),1)<HD
def stack_heads(ref, row, pair, factor=None):
    low=low_half()
    t=[ref[pl.ds(row,SEG), pl.ds(pl.multiple_of((3*pair+i)*LANES,LANES),LANES)].astype(jnp.float32) for i in range(3)]
    if factor is not None: t=[x*factor for x in t]
    z=jnp.zeros_like(t[0])
    r0=pltpu.roll(t[0],HD,1); r2=pltpu.roll(t[2],HD,1)
    parts=[jnp.where(low,t[0],z),jnp.where(low,r0,z),jnp.where(low,t[1],z),
           jnp.where(low,z,t[1]),jnp.where(low,z,r2),jnp.where(low,z,t[2])]
    return jnp.concatenate(parts,axis=0)
def unstack_heads(rows):
    low=low_half()
    a=[rows[i*SEG:(i+1)*SEG] for i in range(6)]
    return [jnp.where(low,a[0],pltpu.roll(a[1],HD,1)), jnp.where(low,a[2],a[3]), jnp.where(low,pltpu.roll(a[4],HD,1),a[5])]
def kv_path(kv_ref, slots, seg, depth, col):
    return jnp.concatenate([kv_ref[slots[seg,lev],:,pl.ds(pl.multiple_of(col,LANES),LANES)] for lev in range(depth)],axis=0)
NT=(((1,),(1,)),((),())); NN=(((1,),(0,)),((),())); TN=(((0,),(0,)),((),()))
def dot(a,b,dims): return lax.dot_general(a,b,dims,preferred_element_type=jnp.float32)
def causal_bias(width):
    key=lax.broadcasted_iota(jnp.int32,(SEG,width),0); qry=lax.broadcasted_iota(jnp.int32,(SEG,width),1)%SEG
    return jnp.where(key<=qry,0.0,NEG)
def fwd_step(depth, slots, bias, q_ref, kv_ref, o_ref, lse_ref, s_scr, p_scr, i, c):
    width=6*SEG
    seg=i//PAIRS; pair=i%PAIRS
    row=pl.multiple_of(seg*SEG,SEG)
    q6=stack_heads(q_ref,row,pair,HD**-0.5).astype(jnp.bfloat16)
    top=jnp.full((8,width),NEG,jnp.float32)
    for lev in range(depth):
        k=kv_ref[slots[seg,lev],:,pl.ds(pl.multiple_of(pair*LANES,LANES),LANES)]
        s=dot(k,q6,NT)
        s=s+(causal_bias(width) if lev==0 else bias[seg,lev])
        s_scr[lev*SEG:(lev+1)*SEG,:]=s
        top=jnp.maximum(top,jnp.max(s.reshape(SEG//8,8,width),axis=0))
    top=jnp.max(top,axis=0,keepdims=True)
    tot=jnp.zeros((8,width),jnp.float32)
    acc=jnp.zeros((LANES,width),jnp.float32)
    for lev in range(depth):
        p=jnp.exp(s_scr[lev*SEG:(lev+1)*SEG,:]-top)
        tot=tot+jnp.sum(p.reshape(SEG//8,8,width),axis=0)
        p_scr[lev*SEG:(lev+1)*SEG,:]=p.astype(jnp.bfloat16)
    v=kv_path(kv_ref,slots,seg,depth,KVH*HD+pair*LANES)
    acc=dot(v,p_scr[...],TN)
    tot=jnp.sum(tot,axis=0,keepdims=True)
    lse_ref[i]=jnp.broadcast_to(top+jnp.log(tot),(8,width))
    o6=(acc/tot).T
    for j,t in enumerate(unstack_heads(o6)):
        o_ref[pl.ds(row,SEG),pl.ds(pl.multiple_of((3*pair+j)*LANES,LANES),LANES)]=t.astype(o_ref.dtype)
    return c
def bwd_step(depth, slots, bias, q_ref, kv_ref, o_ref, do_ref, lse_ref, dq_ref, path, p_scr, d_scr, i, c):
    width=6*SEG
    seg=i//PAIRS; pair=i%PAIRS
    row=pl.multiple_of(seg*SEG,SEG)
    q6=stack_heads(q_ref,row,pair,HD**-0.5).astype(jnp.bfloat16)
    do6f=stack_heads(do_ref,row,pair)
    do6=do6f.astype(jnp.bfloat16)
    prod=do6f*stack_heads(o_ref,row,pair)
    hi=prod.astype(jnp.bfloat16); lo=(prod-hi.astype(jnp.float32)).astype(jnp.bfloat16)
    ones=jnp.ones((8,LANES),jnp.bfloat16)
    delta=(dot(ones,hi,NT)+dot(ones,lo,NT))[:1]
    lse=lse_ref[i][:1]
    kcol=pl.multiple_of(pair*LANES,LANES); vcol=pl.multiple_of(KVH*HD+pair*LANES,LANES)
    for lev in range(depth):
        k=kv_ref[slots[seg,lev],:,pl.ds(kcol,LANES)]
        v=kv_ref[slots[seg,lev],:,pl.ds(vcol,LANES)]
        s=dot(k,q6,NT)
        s=s+(causal_bias(width) if lev==0 else bias[seg,lev])
        p=jnp.exp(s-lse)
        dp=dot(v,do6,NT)
        ds=(p*(dp-delta)).astype(jnp.bfloat16)
        p_scr[lev*SEG:(lev+1)*SEG,:]=p.astype(jnp.bfloat16)
        d_scr[lev*SEG:(lev+1)*SEG,:]=ds
    dv=dot(p_scr[...],do6,NN)
    dk=dot(d_scr[...],q6,NN)
    for lev in range(depth):
        path[seg,lev,:,pl.ds(kcol,LANES)]=dk[lev*SEG:(lev+1)*SEG].astype(path.dtype)
        path[seg,lev,:,pl.ds(vcol,LANES)]=dv[lev*SEG:(lev+1)*SEG].astype(path.dtype)
    k=kv_path(kv_ref,slots,seg,depth,pair*LANES)
    dq6=(dot(k,d_scr[...],TN)*(HD**-0.5)).T
    for j,t in enumerate(unstack_heads(dq6)):
        dq_ref[pl.ds(row,SEG),pl.ds(pl.multiple_of((3*pair+j)*LANES,LANES),LANES)]=t.astype(dq_ref.dtype)
    return c
def bwd_collect(inv, path, group, slot, c):
    for col in range(0,2*KVH*HD,256):
        tot=path[0,inv[slot,0],:,col:col+256].astype(jnp.float32)
        for seg in range(1,path.shape[0]): tot=tot+path[seg,inv[slot,seg],:,col:col+256].astype(jnp.float32)
        group[slot,:,col:col+256]=tot.astype(group.dtype)
    return c
MESH = pl.DeviceIdType.MESH
ANY = pl.BlockSpec(memory_space=pl.ANY)
VMEM = pl.BlockSpec(memory_space=pltpu.VMEM)
SMEM = pl.BlockSpec(memory_space=pltpu.SMEM)


def work(flops, moved):
    return pl.CostEstimate(flops=int(flops), bytes_accessed=int(moved), transcendentals=0)


class Sends:
    def __init__(self):
        self.open = []

    def start(self, cond, src, dst, send_sem, recv_sem, device):
        copy = pltpu.make_async_remote_copy(
            src_ref=src, dst_ref=dst, send_sem=send_sem, recv_sem=recv_sem, device_id=device, device_id_type=MESH
        )
        when(cond, copy.start)
        self.open.append((cond, copy.wait_send))

    def local(self, src, dst, sem):
        copy = pltpu.make_async_copy(src, dst, sem)
        copy.start()
        self.open.append((None, copy.wait))

    def drain(self):
        for cond, wait in self.open:
            when(cond, wait)
        self.open = []


def when(cond, body):
    if cond is None:
        body()
    else:
        pl.when(cond)(body)


def received(cond, region, send_sem, recv_sem, device):
    copy = pltpu.make_async_remote_copy(
        src_ref=region, dst_ref=region, send_sem=send_sem, recv_sem=recv_sem, device_id=device, device_id_type=MESH
    )
    when(cond, copy.wait_recv)


def line_place(shards):
    me = lax.axis_index("shard")
    return me, me // 2, shards // 2


def greet(devices):
    barrier = pltpu.get_barrier_semaphore()
    count = 0
    for cond, device in devices:
        when(
            cond,
            lambda device=device: pl.semaphore_signal(barrier, inc=1, device_id=device, device_id_type=MESH),
        )
        count = count + (1 if cond is None else cond.astype(jnp.int32))
    pl.semaphore_wait(barrier, count)


def line_neighbours(shards):
    me, spot, length = line_place(shards)
    return [
        (None, {"shard": me + 1 - 2 * (me % 2)}),
        (spot > 0, {"shard": me - 2}),
        (spot + 1 < length, {"shard": me + 2}),
    ]


class LineGather:
    def __init__(self, shards, sources, region, up, down, pair, local_sem, arrived=None):
        self.shards, self.sources, self.region = shards, sources, region
        self.up, self.down, self.pair, self.local_sem = up, down, pair, local_sem
        self.arrived = arrived or (lambda cond, block, index: None)
        self.sends = Sends()
        self.me, self.spot, self.length = line_place(shards)
        self.twin = self.me + 1 - 2 * (self.me % 2)

    def forward(self, cond, block, step, rising, falling, src=None):
        place = step if rising else self.length - 1 + step
        for n in range(len(self.sources)):
            here = self.region(n, block)
            out = here if src is None else src[n]
            ways = []
            if rising:
                ways.append((both(cond, self.spot + 1 < self.length), self.up, step + 1, self.me + 2))
            if falling:
                ways.append((both(cond, self.spot > 0), self.down, step + 1, self.me - 2))
            for where, sems, index, device in ways:
                if index < self.length:
                    self.sends.start(where, out, here, sems.at[0, index, n], sems.at[1, index, n], {"shard": device})
            self.sends.start(
                cond, out, here, self.pair.at[0, place, n], self.pair.at[1, place, n], {"shard": self.twin}
            )

    def begin(self):
        for n, src in enumerate(self.sources):
            self.sends.local(src, self.region(n, self.me), self.local_sem.at[n])
        self.forward(None, self.me, 0, True, True, self.sources)

    def finish_local(self):
        for cond, wait in self.sends.open[: len(self.sources)]:
            wait()
        self.sends.open = self.sends.open[len(self.sources) :]

    def step(self, step):
        for sems, cond, block, rising in (
            (self.up, self.spot - step >= 0, self.me - 2 * step, True),
            (self.down, self.spot + step < self.length, self.me + 2 * step, False),
        ):
            for n in range(len(self.sources)):
                received(cond, self.region(n, block), sems.at[0, step, n], sems.at[1, step, n], {"shard": self.twin})
            self.forward(cond, block, step, rising, not rising)
            self.arrived(cond, block, step if rising else self.length - 1 + step)

    def pair_step(self, step):
        turns = [(None, self.twin, 0)] if step == 0 else [
            (self.spot - step >= 0, self.twin - 2 * step, step),
            (self.spot + step < self.length, self.twin + 2 * step, self.length - 1 + step),
        ]
        for cond, block, place in turns:
            for n in range(len(self.sources)):
                received(
                    cond, self.region(n, block), self.pair.at[0, place, n], self.pair.at[1, place, n], {"shard": self.twin}
                )
            self.arrived(cond, block, 2 * self.length - 1 + place)


def both(first, second):
    return second if first is None else jnp.logical_and(first, second)


def line_sems(shards, arrays):
    length = shards // 2
    return [
        pltpu.SemaphoreType.DMA((2, length, arrays)),
        pltpu.SemaphoreType.DMA((2, length, arrays)),
        pltpu.SemaphoreType.DMA((2, 2 * length - 1, arrays)),
        pltpu.SemaphoreType.DMA((arrays,)),
    ]


class RepSpread:
    def __init__(self, arrays, region, cross, core, relay):
        self.arrays, self.region = arrays, region
        self.cross, self.core, self.relay = cross, core, relay
        rep = lax.axis_index("rep")
        self.rep = rep
        self.near = rep + 1 - 2 * (rep % 2)
        self.far = lax.rem(rep + 2, 4)
        self.diagonal = lax.rem(self.near + 2, 4)
        self.sends = Sends()
        self.blocks = []
        self.passed = []
        self.sources = None

    def arrived(self, cond, block, index):
        for n in self.arrays:
            here = self.region(n, self.rep, block)
            src = here if self.sources is None else self.sources[n]
            self.sends.start(
                cond, src, here, self.cross.at[0, block, n], self.cross.at[1, block, n], {"rep": self.far}
            )
            self.sends.start(
                cond, src, here, self.core.at[0, block, n], self.core.at[1, block, n], {"rep": self.near}
            )
        self.blocks.append((cond, block))

    def pass_on(self):
        for cond, block in self.blocks:
            for n in self.arrays:
                here = self.region(n, self.far, block)
                received(cond, here, self.cross.at[0, block, n], self.cross.at[1, block, n], {"rep": self.far})
                self.sends.start(
                    cond, here, here, self.relay.at[0, block, n], self.relay.at[1, block, n], {"rep": self.near}
                )
        self.passed = self.passed + self.blocks
        self.blocks = []

    def end(self):
        self.pass_on()
        for cond, block in self.passed:
            for n in self.arrays:
                for sems, part in ((self.core, self.near), (self.relay, self.diagonal)):
                    here = self.region(n, part, block)
                    received(cond, here, sems.at[0, block, n], sems.at[1, block, n], {"rep": self.near})
        self.sends.drain()


def rep_neighbours():
    rep = lax.axis_index("rep")
    return [(None, {"rep": rep + 1 - 2 * (rep % 2)}), (None, {"rep": lax.rem(rep + 2, 4)})]


def rep_sems(shards, arrays):
    return [pltpu.SemaphoreType.DMA((2, shards, arrays)) for unused in range(3)]


def part_columns(ref, part, width):
    return ref.at[:, pl.ds(pl.multiple_of(part * width, LANES), width)]


def weights_kernel(shards, qkv, small, qkv_all, small_all, up, down, pair, local_sem, cross, core, relay):
    rep = lax.axis_index("rep")
    greet(line_neighbours(shards) + rep_neighbours())
    width = qkv.shape[1] // lax.axis_size("rep")

    def part(n, owner, block):
        return small_all.at[block] if n == 1 else part_columns(qkv_all.at[block], owner, width)

    spread = RepSpread((0,), part, cross, core, relay)
    spread.sources = None
    gather = LineGather(
        shards,
        (part_columns(qkv, rep, width), small),
        lambda n, block: part(n, rep, block),
        up,
        down,
        pair,
        local_sem,
        spread.arrived,
    )
    gather.begin()
    gather.finish_local()
    spread.arrived(None, gather.me, 0)
    for step in range(gather.length):
        if step:
            gather.step(step)
        spread.pass_on()
        gather.pair_step(step)
    spread.end()
    gather.sends.drain()


def gather_weights(qkv_weight, small, shards):
    shapes = [(shards,) + qkv_weight.shape, (shards,) + small.shape]
    return pl.pallas_call(
        functools.partial(weights_kernel, shards),
        out_shape=[jax.ShapeDtypeStruct(shape, jnp.bfloat16) for shape in shapes],
        in_specs=[ANY] * 2,
        out_specs=[ANY] * 2,
        scratch_shapes=line_sems(shards, 2) + rep_sems(shards, 1),
        cost_estimate=work(0, 2e8),
        compiler_params=pltpu.CompilerParams(collective_id=1, has_side_effects=True),
    )(qkv_weight, small)


def attend_gather_kernel(
    depth,
    shards,
    experts,
    slots,
    bias,
    q_ref,
    kv_ref,
    gu_ref,
    dn_ref,
    out_ref,
    cot_ref,
    o_ref,
    lse_ref,
    kv_all,
    gu_all,
    dn_all,
    out_all,
    cot_all,
    s_scr,
    p_scr,
    kv_sems,
    cot_sem,
    up,
    down,
    pair,
    local_sem,
    cross,
    core,
    relay,
    cot_cross,
    cot_core,
    cot_relay,
):
    me = lax.axis_index("shard")
    rep = lax.axis_index("rep")
    first = me // TREE_DEVS * TREE_DEVS
    member = me % TREE_DEVS
    seg_dev = kv_ref.shape[0]
    others = [first + lax.rem(member + away, TREE_DEVS) for away in range(1, TREE_DEVS)]
    greet(line_neighbours(shards) + rep_neighbours() + [(None, {"shard": other}) for other in others])
    sends = Sends()
    own = kv_all.at[pl.ds(member * seg_dev, seg_dev)]
    for away, other in enumerate(others):
        sends.start(None, kv_ref, own, kv_sems.at[0, away], kv_sems.at[1, away], {"shard": other})
    width = out_ref.shape[1] // lax.axis_size("rep")
    own_experts = gu_ref.shape[0] // lax.axis_size("rep")

    def part(n, owner, block):
        if n == 2:
            return part_columns(out_all.at[block], owner, width)
        return (gu_all, dn_all)[n].at[:, block]

    spread = RepSpread((2,), part, cross, core, relay)
    gather = LineGather(
        shards,
        (
            gu_ref.at[pl.ds(rep * own_experts, experts)],
            dn_ref.at[pl.ds(rep * own_experts, experts)],
            part_columns(out_ref, rep, width),
        ),
        lambda n, block: part(n, rep, block),
        up,
        down,
        pair,
        local_sem,
        spread.arrived,
    )
    gather.begin()
    sends.local(cot_ref, cot_all.at[rep], cot_sem)
    cot_spread = RepSpread((0,), lambda n, owner, block: cot_all.at[owner], cot_cross, cot_core, cot_relay)
    cot_spread.sources = (cot_ref,)
    cot_spread.arrived(None, 0, 0)
    gather.finish_local()
    spread.arrived(None, me, 0)
    kv_all[pl.ds(member * seg_dev, seg_dev)] = kv_ref[...]
    for away in range(TREE_DEVS - 1):
        source = lax.rem(member + TREE_DEVS - 1 - away, TREE_DEVS)
        block = kv_all.at[pl.ds(source * seg_dev, seg_dev)]
        received(None, block, kv_sems.at[0, away], kv_sems.at[1, away], {"shard": first + source})
    count = seg_dev * PAIRS
    attend = functools.partial(fwd_step, depth, slots, bias, q_ref, kv_all, o_ref, lse_ref, s_scr, p_scr)
    done = 0
    for step in range(1, gather.length):
        upto = count * step // (gather.length - 1)
        lax.fori_loop(done, upto, attend, 0)
        done = upto
        gather.step(step)
        gather.pair_step(step - 1)
        spread.pass_on()
    cot_spread.end()
    gather.pair_step(gather.length - 1)
    spread.end()
    gather.sends.drain()
    sends.drain()


def attend_gather(slots, bias, q, kv, gate_up, down, out, cotangent, depth, shards, reps, experts):
    tokens = q.shape[0]
    count = tokens // SEG * PAIRS
    shapes = [
        q.shape,
        (TREE_DEVS * kv.shape[0],) + kv.shape[1:],
        (experts, shards) + gate_up.shape[1:],
        (experts, shards) + down.shape[1:],
        (shards,) + out.shape,
        (reps,) + cotangent.shape,
    ]
    outs = [jax.ShapeDtypeStruct(shape, jnp.bfloat16) for shape in shapes]
    return pl.pallas_call(
        functools.partial(attend_gather_kernel, depth, shards, experts),
        out_shape=outs[:1] + [jax.ShapeDtypeStruct((count, 8, 6 * SEG), jnp.float32)] + outs[1:],
        in_specs=[SMEM, SMEM, VMEM, VMEM] + [ANY] * 4,
        out_specs=[VMEM] * 3 + [ANY] * 4,
        scratch_shapes=[
            pltpu.VMEM((depth * SEG, 6 * SEG), jnp.float32),
            pltpu.VMEM((depth * SEG, 6 * SEG), jnp.bfloat16),
            pltpu.SemaphoreType.DMA((2, TREE_DEVS - 1)),
            pltpu.SemaphoreType.DMA,
        ]
        + line_sems(shards, 3)
        + rep_sems(shards, 3)
        + rep_sems(1, 1),
        cost_estimate=work(2e10, 7e8),
        compiler_params=pltpu.CompilerParams(
            collective_id=2, has_side_effects=True, vmem_limit_bytes=48 * 2**20
        ),
    )(slots, bias, q, kv, gate_up, down, out, cotangent)


def share_kernel(chunks, rows_ref, gate_ref, rows_all, gate_all, own_sems, cross, core, relay):
    rep = lax.axis_index("rep")
    greet(rep_neighbours())
    size = rows_ref.shape[0] // chunks

    def piece(n, part, block):
        return gate_all.at[part] if n == chunks else rows_all.at[part, pl.ds(n * size, size)]

    spread = RepSpread(tuple(range(chunks + 1)), piece, cross, core, relay)
    spread.sources = [rows_ref.at[pl.ds(n * size, size)] for n in range(chunks)] + [gate_ref]
    spread.arrived(None, 0, 0)
    for n in range(chunks + 1):
        spread.sends.local(spread.sources[n], piece(n, rep, 0), own_sems.at[n])
    spread.end()


def share_rows(rows, gates, reps):
    chunks = 4
    return pl.pallas_call(
        functools.partial(share_kernel, chunks),
        out_shape=[
            jax.ShapeDtypeStruct((reps,) + rows.shape, rows.dtype),
            jax.ShapeDtypeStruct((reps,) + gates.shape, gates.dtype),
        ],
        in_specs=[ANY] * 2,
        out_specs=[ANY] * 2,
        scratch_shapes=[pltpu.SemaphoreType.DMA((chunks + 1,))] + rep_sems(1, chunks + 1),
        cost_estimate=work(0, 1.6e8),
        compiler_params=pltpu.CompilerParams(collective_id=6, has_side_effects=True),
    )(rows, gates)


def join_kernel(part, total, near_buf, cross_out, cross_buf, near_sems, cross_sems):
    rep = lax.axis_index("rep")
    near = rep + 1 - 2 * (rep % 2)
    far = lax.rem(rep + 2, 4)
    diagonal = lax.rem(near + 2, 4)
    greet(rep_neighbours())
    sends = Sends()
    chunks = near_sems.shape[2]
    size = total.shape[0] // chunks
    for slot, owner in ((1, diagonal), (0, near)):
        for c in range(chunks):
            rows = pl.ds(c * size, size)
            sends.start(
                None,
                part.at[owner, rows],
                near_buf.at[slot, rows],
                near_sems.at[0, slot, c],
                near_sems.at[1, slot, c],
                {"rep": near},
            )

    def got(slot, c):
        here = near_buf.at[slot, pl.ds(c * size, size)]
        received(None, here, near_sems.at[0, slot, c], near_sems.at[1, slot, c], {"rep": near})

    step = 32 if size % 32 == 0 else size
    for c in range(chunks):
        got(1, c)

        def first(i, carry, c=c):
            rows = pl.ds(pl.multiple_of(c * size + i * step, step), step)
            value = part[far, rows].astype(jnp.float32) + near_buf[1, rows].astype(jnp.float32)
            cross_out[rows] = value.astype(cross_out.dtype)
            return carry

        lax.fori_loop(0, size // step, first, 0)
        rows = pl.ds(c * size, size)
        sends.start(
            None, cross_out.at[rows], cross_buf.at[rows], cross_sems.at[0, c], cross_sems.at[1, c], {"rep": far}
        )
    for c in range(chunks):
        got(0, c)
        here = cross_buf.at[pl.ds(c * size, size)]
        received(None, here, cross_sems.at[0, c], cross_sems.at[1, c], {"rep": far})

        def second(i, carry, c=c):
            rows = pl.ds(pl.multiple_of(c * size + i * step, step), step)
            value = part[rep, rows].astype(jnp.float32) + near_buf[0, rows].astype(jnp.float32)
            total[rows] = value + cross_buf[rows].astype(jnp.float32)
            return carry

        lax.fori_loop(0, size // step, second, 0)
    sends.drain()


def join_reps(part):
    block = part.shape[1:]
    chunks = 4
    return pl.pallas_call(
        join_kernel,
        out_shape=jax.ShapeDtypeStruct(block, jnp.float32),
        in_specs=[VMEM],
        out_specs=VMEM,
        scratch_shapes=[
            pltpu.VMEM((2,) + block, jnp.bfloat16),
            pltpu.VMEM(block, jnp.bfloat16),
            pltpu.VMEM(block, jnp.bfloat16),
            pltpu.SemaphoreType.DMA((2, 2, chunks)),
            pltpu.SemaphoreType.DMA((2, chunks)),
        ],
        cost_estimate=work(0, 1.6e8),
        compiler_params=pltpu.CompilerParams(
            collective_id=5, has_side_effects=True, vmem_limit_bytes=40 * 2**20
        ),
    )(part)


class LineScatter:
    def __init__(self, shards, arrays, local, pair_buf, line_buf, temp, stages, outs, pair, line, loads, ready=None):
        self.shards, self.arrays, self.local = shards, arrays, local
        self.pair_buf, self.line_buf, self.temp = pair_buf, line_buf, temp
        self.stages, self.outs = stages, outs
        self.pair, self.line, self.loads = pair, line, loads
        self.ready = ready or (lambda block: None)
        self.sends = Sends()
        self.me, self.spot, self.length = line_place(shards)
        self.side = self.me % 2
        self.twin = self.me + 1 - 2 * self.side

    def add(self, n, sources, target):
        stage, out = self.stages[n], self.outs[n]
        copies = []
        for k, (cond, ref) in enumerate(sources):
            copy = pltpu.make_async_copy(ref, stage.at[k], self.loads.at[k])
            copies.append((cond, copy))
            when(cond, copy.start)
        outer, rows, width = out.shape
        chunk = 32 if rows % 32 == 0 else rows
        pieces = rows // chunk

        def clear(k):
            def one(i, c):
                row = pl.multiple_of(i % pieces * chunk, chunk)
                stage[k, i // pieces, pl.ds(row, chunk)] = jnp.zeros((chunk, width), stage.dtype)
                return c

            lax.fori_loop(0, outer * pieces, one, 0)

        for k, (cond, copy) in enumerate(copies):
            when(cond, copy.wait)
            if cond is not None:
                pl.when(jnp.logical_not(cond))(functools.partial(clear, k))

        def one(i, c):
            row = pl.multiple_of(i % pieces * chunk, chunk)
            total = stage[0, i // pieces, pl.ds(row, chunk)].astype(jnp.float32)
            for k in range(1, len(sources)):
                total = total + stage[k, i // pieces, pl.ds(row, chunk)].astype(jnp.float32)
            out[i // pieces, pl.ds(row, chunk)] = total.astype(out.dtype)
            return c

        lax.fori_loop(0, outer * pieces, one, 0)
        store = pltpu.make_async_copy(out, target, self.loads.at[self.loads.shape[0] - 1])
        store.start()
        store.wait()

    def begin(self):
        order = []
        for step in range(self.length):
            for target in (self.length - 1 - step, step):
                if target not in order:
                    order.append(target)
        for target in order:
            block = 2 * target + 1 - self.side
            self.ready(block)
            for n in range(self.arrays):
                sources = self.local(n, block)
                src = sources[0]
                if len(sources) > 1:
                    src = self.temp[n].at[target]
                    self.add(n, [(None, ref) for ref in sources], src)
                self.sends.start(
                    None,
                    src,
                    self.pair_buf[n].at[target],
                    self.pair.at[0, target, n],
                    self.pair.at[1, target, n],
                    {"shard": self.twin},
                )

    def got_pair(self, target, n):
        received(
            None,
            self.pair_buf[n].at[target],
            self.pair.at[0, target, n],
            self.pair.at[1, target, n],
            {"shard": self.twin},
        )

    def got_line(self, cond, slot, n, device):
        received(cond, self.line_buf[n].at[slot], self.line.at[0, slot, n], self.line.at[1, slot, n], {"shard": device})

    def step(self, step):
        below, above = self.spot > 0, self.spot + 1 < self.length
        turns = (
            (self.length - 1 - step, True, below, self.me - 2, self.me + 2),
            (step, False, above, self.me + 2, self.me - 2),
        )
        for target, rising, has, source, device in turns:
            cond = self.spot < target if rising else self.spot > target
            block = 2 * target + self.side
            slot = target if rising else jnp.where(self.spot == target + 1, self.length, target)
            for n in range(self.arrays):
                copy = pltpu.make_async_remote_copy(
                    src_ref=self.pair_buf[n].at[target],
                    dst_ref=self.line_buf[n].at[slot],
                    send_sem=self.line.at[0, slot, n],
                    recv_sem=self.line.at[1, slot, n],
                    device_id={"shard": device},
                    device_id_type=MESH,
                )

                def body(n=n, copy=copy, target=target, has=has, source=source, block=block):
                    self.got_pair(target, n)
                    self.got_line(has, target, n, source)
                    if n == 0:
                        self.ready(block)
                    sources = [(None, ref) for ref in self.local(n, block)]
                    sources += [(None, self.pair_buf[n].at[target]), (has, self.line_buf[n].at[target])]
                    self.add(n, sources, self.pair_buf[n].at[target])
                    copy.start()

                pl.when(cond)(body)
                self.sends.open.append((cond, copy.wait_send))

    def finish(self, targets):
        below, above = self.spot > 0, self.spot + 1 < self.length
        self.ready(self.me)
        for n in range(self.arrays):
            self.got_pair(self.spot, n)
            self.got_line(below, self.spot, n, self.me - 2)
            self.got_line(above, self.length, n, self.me + 2)
            sources = [(None, ref) for ref in self.local(n, self.me)]
            sources += [
                (None, self.pair_buf[n].at[self.spot]),
                (below, self.line_buf[n].at[self.spot]),
                (above, self.line_buf[n].at[self.length]),
            ]
            self.add(n, sources, targets[n])


def scatter_sems(shards, arrays, loads):
    length = shards // 2
    return [
        pltpu.SemaphoreType.DMA((2, length, arrays)),
        pltpu.SemaphoreType.DMA((2, length + 1, arrays)),
        pltpu.SemaphoreType.DMA((loads + 1,)),
    ]


def scatter_buffers(shards, block):
    length = shards // 2
    return [
        jax.ShapeDtypeStruct((length,) + block, jnp.bfloat16),
        jax.ShapeDtypeStruct((length + 1,) + block, jnp.bfloat16),
    ]


def back_kernel(
    depth,
    shards,
    slots,
    bias,
    inv,
    q_ref,
    kv_ref,
    o_ref,
    do_ref,
    lse_ref,
    gu_ref,
    dn_ref,
    dq_ref,
    dkv_ref,
    gu_out,
    dn_out,
    gu_pair,
    gu_line,
    dn_pair,
    dn_line,
    path,
    p_scr,
    d_scr,
    group,
    guest,
    gu_stage,
    dn_stage,
    gu_sum,
    dn_sum,
    kv_sems,
    pair,
    line,
    loads,
):
    me = lax.axis_index("shard")
    first = me // TREE_DEVS * TREE_DEVS
    member = me % TREE_DEVS
    segs = q_ref.shape[0] // SEG
    others = [first + lax.rem(member + away, TREE_DEVS) for away in range(1, TREE_DEVS)]
    greet(line_neighbours(shards) + [(None, {"shard": other}) for other in others])
    scatter = LineScatter(
        shards,
        2,
        lambda n, block: [(gu_ref, dn_ref)[n].at[:, block]],
        (gu_pair, dn_pair),
        (gu_line, dn_line),
        None,
        (gu_stage, dn_stage),
        (gu_sum, dn_sum),
        pair,
        line,
        loads,
    )
    scatter.begin()
    path[:, depth] = jnp.zeros((segs,) + path.shape[2:], path.dtype)
    step = functools.partial(
        bwd_step, depth, slots, bias, q_ref, kv_ref, o_ref, do_ref, lse_ref, dq_ref, path, p_scr, d_scr
    )
    early = segs * PAIRS * 3 // 5
    lax.fori_loop(0, early, step, 0)
    scatter.step(0)
    lax.fori_loop(early, segs * PAIRS, step, 0)
    lax.fori_loop(0, group.shape[0], functools.partial(bwd_collect, inv, path, group), 0)
    sends = Sends()
    for away, other in enumerate(others):
        target = lax.rem(member + away + 1, TREE_DEVS)
        sends.start(
            None,
            group.at[pl.ds(target * segs, segs)],
            guest.at[away],
            kv_sems.at[0, away],
            kv_sems.at[1, away],
            {"shard": other},
        )
    for turn in range(1, scatter.length):
        scatter.step(turn)
    for away in range(TREE_DEVS - 1):
        source = first + lax.rem(member + TREE_DEVS - 1 - away, TREE_DEVS)
        received(None, guest.at[away], kv_sems.at[0, away], kv_sems.at[1, away], {"shard": source})

    def join(seg, c):
        for col in range(0, 2 * KVH * HD, 256):
            total = group[member * segs + seg, :, col : col + 256].astype(jnp.float32)
            for away in range(TREE_DEVS - 1):
                total = total + guest[away, seg, :, col : col + 256].astype(jnp.float32)
            dkv_ref[seg, :, col : col + 256] = total.astype(dkv_ref.dtype)
        return c

    lax.fori_loop(0, segs, join, 0)
    scatter.finish((gu_out, dn_out))
    sends.drain()
    scatter.sends.drain()


def attend_back(slots, bias, inv, q, kv, o, do, lse, gate_up_grad, down_grad, depth, shards):
    segs = q.shape[0] // SEG
    own_kv = (segs,) + kv.shape[1:]
    gu_block = (gate_up_grad.shape[0],) + gate_up_grad.shape[2:]
    dn_block = (down_grad.shape[0],) + down_grad.shape[2:]
    outs = [
        jax.ShapeDtypeStruct(q.shape, jnp.bfloat16),
        jax.ShapeDtypeStruct(own_kv, jnp.bfloat16),
        jax.ShapeDtypeStruct(gu_block, jnp.bfloat16),
        jax.ShapeDtypeStruct(dn_block, jnp.bfloat16),
    ]
    outs += scatter_buffers(shards, gu_block) + scatter_buffers(shards, dn_block)
    return pl.pallas_call(
        functools.partial(back_kernel, depth, shards),
        out_shape=outs,
        in_specs=[SMEM] * 3 + [VMEM] * 5 + [ANY] * 2,
        out_specs=[VMEM] * 2 + [ANY] * 6,
        scratch_shapes=[
            pltpu.VMEM((segs, depth + 1, SEG, 2 * KVH * HD), jnp.bfloat16),
            pltpu.VMEM((depth * SEG, 6 * SEG), jnp.bfloat16),
            pltpu.VMEM((depth * SEG, 6 * SEG), jnp.bfloat16),
            pltpu.VMEM(kv.shape, jnp.bfloat16),
            pltpu.VMEM((TREE_DEVS - 1,) + own_kv, jnp.bfloat16),
            pltpu.VMEM((4,) + gu_block, jnp.bfloat16),
            pltpu.VMEM((4,) + dn_block, jnp.bfloat16),
            pltpu.VMEM(gu_block, jnp.bfloat16),
            pltpu.VMEM(dn_block, jnp.bfloat16),
            pltpu.SemaphoreType.DMA((2, TREE_DEVS - 1)),
        ]
        + scatter_sems(shards, 2, 4),
        cost_estimate=work(5e10, 7e8),
        compiler_params=pltpu.CompilerParams(
            collective_id=3, has_side_effects=True, vmem_limit_bytes=60 * 2**20
        ),
    )(slots, bias, inv, q, kv, o, do, lse, gate_up_grad, down_grad)[:4]


def finish_kernel(shards, arrays, pieces, *refs):
    refs = list(refs)

    def take(count):
        taken = refs[:count]
        del refs[:count]
        return taken

    grads = take(arrays)
    shares = take(pieces)
    outs = take(arrays)
    expert_outs = take(2)
    core_bufs = take(arrays)
    share_bufs = take(arrays)
    cross_bufs = take(arrays)
    temps = take(arrays)
    pair_bufs = take(arrays)
    line_bufs = take(arrays)
    stages = take(arrays)
    totals = take(arrays)
    core_sems, swap_sems, own_sems, cross, core, relay, pair, line, loads = refs
    rep = lax.axis_index("rep")
    near = rep + 1 - 2 * (rep % 2)
    far = lax.rem(rep + 2, 4)
    half = rep % 2
    greet(line_neighbours(shards) + rep_neighbours())
    sends = Sends()
    length = shards // 2
    order = []
    for step in range(length):
        for target in (length - 1 - step, step):
            if target not in order:
                order.append(target)
    side = lax.axis_index("shard") % 2

    def columns(n, ref, which):
        width = totals[n].shape[-1]
        if width == ref.shape[-1]:
            return ref
        return ref.at[:, :, pl.ds(pl.multiple_of(which * width, LANES), width)]

    for turn in (1 - side, side):
        for target in order:
            block = 2 * target + turn
            for n in range(arrays):
                sends.start(
                    None,
                    columns(n, grads[n].at[block], 1 - half),
                    core_bufs[n].at[block],
                    core_sems.at[0, block, n],
                    core_sems.at[1, block, n],
                    {"rep": near},
                )
    experts = pieces // 2
    size = shares[0].shape[0]

    def place(n, part, block):
        return expert_outs[n // experts].at[part, pl.ds(n % experts * size, size)]

    for n in range(pieces):
        sends.local(shares[n], place(n, rep, 0), own_sems.at[n])
    spread = RepSpread(tuple(range(pieces)), place, cross, core, relay)
    spread.sources = shares
    spread.arrived(None, 0, 0)

    def ready(block):
        for n in range(arrays):
            received(
                None, core_bufs[n].at[block], core_sems.at[0, block, n], core_sems.at[1, block, n], {"rep": near}
            )

    scatter = LineScatter(
        shards,
        arrays,
        lambda n, block: [columns(n, grads[n].at[block], half), core_bufs[n].at[block]],
        pair_bufs,
        line_bufs,
        temps,
        stages,
        totals,
        pair,
        line,
        loads,
        ready,
    )
    scatter.begin()
    for turn in range(scatter.length):
        scatter.step(turn)
    scatter.finish(share_bufs)
    for n in range(arrays):
        sends.start(
            None, share_bufs[n], cross_bufs[n], swap_sems.at[0, 0, n], swap_sems.at[1, 0, n], {"rep": far}
        )
    spread.end()
    for n in range(arrays):
        received(None, cross_bufs[n], swap_sems.at[0, 0, n], swap_sems.at[1, 0, n], {"rep": far})
        mine = columns(n, outs[n], half)
        scatter.add(n, [(None, share_bufs[n]), (None, cross_bufs[n])], mine)
        if outs[n].shape != totals[n].shape:
            sends.start(None, mine, mine, swap_sems.at[0, 1, n], swap_sems.at[1, 1, n], {"rep": near})
    for n in range(arrays):
        if outs[n].shape != totals[n].shape:
            theirs = columns(n, outs[n], 1 - half)
            received(None, theirs, swap_sems.at[0, 1, n], swap_sems.at[1, 1, n], {"rep": near})
    sends.drain()
    scatter.sends.drain()


def finish_grads(grads, halved, gate_up_shares, down_shares, reps):
    shards = grads[0].shape[0]
    arrays = len(grads)
    parts = len(gate_up_shares)
    wholes = [grad.shape[1:] for grad in grads]
    blocks = [
        whole[:-1] + (whole[-1] // 2 if halve else whole[-1],) for whole, halve in zip(wholes, halved)
    ]
    experts = parts * gate_up_shares[0].shape[0]
    shapes = list(wholes)
    shapes += [(reps, experts) + gate_up_shares[0].shape[1:], (reps, experts) + down_shares[0].shape[1:]]
    shapes += [(shards,) + block for block in blocks]
    shapes += blocks + blocks
    shapes += [(shards // 2,) + block for block in blocks]
    shapes += [(shards // 2,) + block for block in blocks]
    shapes += [(shards // 2 + 1,) + block for block in blocks]
    return pl.pallas_call(
        functools.partial(finish_kernel, shards, arrays, 2 * parts),
        out_shape=[jax.ShapeDtypeStruct(shape, jnp.bfloat16) for shape in shapes],
        in_specs=[ANY] * (arrays + 2 * parts),
        out_specs=[ANY] * len(shapes),
        scratch_shapes=[pltpu.VMEM((5,) + block, jnp.bfloat16) for block in blocks]
        + [pltpu.VMEM(block, jnp.bfloat16) for block in blocks]
        + [
            pltpu.SemaphoreType.DMA((2, shards, arrays)),
            pltpu.SemaphoreType.DMA((2, 2, arrays)),
            pltpu.SemaphoreType.DMA((2 * parts,)),
        ]
        + rep_sems(1, 2 * parts)
        + scatter_sems(shards, arrays, 5),
        cost_estimate=work(0, 4e8),
        compiler_params=pltpu.CompilerParams(
            collective_id=4, has_side_effects=True, vmem_limit_bytes=32 * 2**20
        ),
    )(*grads, *gate_up_shares, *down_shares)[: arrays + 2]


def norm_rows(values, gain):
    scale_rows = lax.rsqrt(jnp.mean(values * values, axis=-1, keepdims=True) + EPS)
    return (values * scale_rows * gain, scale_rows)


def norm_back(values, scale_rows, gain, upstream):
    scaled = upstream * gain
    inner = jnp.mean(scaled * values, axis=-1, keepdims=True)
    through = scale_rows * scaled - values * (scale_rows * scale_rows * scale_rows) * inner
    gain_grad = jnp.sum(upstream * values * scale_rows, axis=0)
    return (through, gain_grad)


def table_lookup(table, index):
    positions = jnp.arange(table.shape[0], dtype=jnp.int32)
    return jnp.sum(jnp.where(index[:, None] == positions[None, :], table[None, :], 0), axis=1)


def find_slot(group_ids, wanted):
    positions = jnp.arange(group_ids.shape[0], dtype=jnp.int32)
    return jnp.sum(jnp.where(group_ids[None, :] == wanted[:, None], positions[None, :], 0), axis=1)


def ancestor_slots(local_ids, group_ids, group_parents, depth):
    flat_parents = group_parents.reshape(-1)
    tree_index = local_ids // TREE_SEGS
    current = local_ids % TREE_SEGS
    alive = jnp.ones(local_ids.shape, dtype=bool)
    slot_list = []
    alive_list = []
    for level in range(depth):
        wanted = tree_index * TREE_SEGS + current
        slot_list.append(find_slot(group_ids, wanted))
        alive_list.append(alive)
        parent_seg = table_lookup(flat_parents, wanted)
        alive = alive & (parent_seg != current)
        current = parent_seg
    return (jnp.stack(slot_list, axis=1), jnp.stack(alive_list, axis=1))


def path_levels(path_slots, path_alive, slot_count):
    depth = path_slots.shape[1]
    slots = jnp.arange(slot_count, dtype=jnp.int32)
    hit = path_alive[None] & (path_slots[None] == slots[:, None, None])
    levels = jnp.arange(depth, dtype=jnp.int32)
    return depth - jnp.sum(jnp.where(hit, depth - levels, 0), axis=2)


def row_pieces(grad, shards):
    experts, rows, width = grad.shape
    return grad.astype(jnp.bfloat16).reshape(experts, shards, rows // shards, width).transpose(1, 0, 2, 3)


def expert_forward(rows, gates, w_gate_up, w_down, upstream):
    gate_up = jnp.einsum("td,edf->etf", rows, w_gate_up, preferred_element_type=jnp.float32)
    gate_part = gate_up[..., :FF]
    up_part = gate_up[..., FF:]
    sig_gate = jax.nn.sigmoid(gate_part)
    hidden = gate_part * sig_gate * up_part
    gated = (hidden * gates).astype(jnp.bfloat16)
    mix_part = jnp.einsum("etf,efd->td", gated, w_down, preferred_element_type=jnp.float32)
    raw_grad = jnp.einsum("td,efd->etf", upstream, w_down, preferred_element_type=jnp.float32)
    gate_grad = jnp.sum(hidden * raw_grad, axis=-1)
    hidden_grad = raw_grad * gates
    gate_grad_part = hidden_grad * up_part * sig_gate * (1.0 + gate_part * (1.0 - sig_gate))
    up_grad_part = hidden_grad * gate_part * sig_gate
    row_grads = jnp.concatenate([gate_grad_part, up_grad_part], axis=-1).astype(jnp.bfloat16)
    down_grad = jnp.einsum("etf,td->efd", gated, upstream, preferred_element_type=jnp.float32)
    gate_up_grad = jnp.einsum("td,etf->edf", rows, row_grads, preferred_element_type=jnp.float32)
    act_part = jnp.einsum("etf,edf->td", row_grads, w_gate_up, preferred_element_type=jnp.float32)
    return (mix_part, gate_grad, act_part, gate_up_grad, down_grad)


def shards(
    tokens,
    norm_gains,
    qkv_weight,
    out_weight,
    router_weight,
    gate_up_weight,
    down_weight,
    routes,
    placement,
    parents,
    cotangent,
):
    shard_index = lax.axis_index("shard")
    rep_index = lax.axis_index("rep")
    shard_count = lax.axis_size("shard")
    token_count = tokens.shape[0]
    seg_dev = token_count // SEG
    depth = TRUNK + 2
    width_q = H * HD
    width_kv = KVH * HD
    group_size = TREE_DEVS * seg_dev
    tree_count = group_size // TREE_SEGS
    member = shard_index % TREE_DEVS
    group = (rep_index * shard_count + shard_index) // TREE_DEVS
    group_ids = lax.dynamic_slice_in_dim(placement, group * group_size, group_size)
    group_parents = lax.dynamic_slice_in_dim(parents, group * tree_count, tree_count)
    local_ids = lax.dynamic_slice_in_dim(group_ids, member * seg_dev, seg_dev)
    path_slots, path_alive = ancestor_slots(local_ids, group_ids, group_parents, depth)
    rep_count = lax.axis_size("rep")
    own_experts = E // rep_count
    first_expert = rep_index * own_experts
    padding = jnp.zeros((norm_gains.shape[1], LANES - E - 2), jnp.bfloat16)
    small = jnp.concatenate([router_weight, norm_gains.T, padding], axis=1)
    w_qkv, small = gather_weights(qkv_weight, small, shard_count)
    w_qkv = w_qkv.reshape(D, -1)
    small = small.reshape(D, LANES)
    w_router = small[:, :E]
    gains = small[:, E : E + 2].T
    half = own_experts // 2
    gain_first = gains[0].astype(jnp.float32)
    gain_second = gains[1].astype(jnp.float32)
    token_values = tokens.astype(jnp.float32)
    normed_first, scale_first = norm_rows(token_values, gain_first)
    act_first = normed_first.astype(jnp.bfloat16)
    projected = jnp.dot(act_first, w_qkv, preferred_element_type=jnp.float32)
    queries = projected[:, :width_q].astype(jnp.bfloat16)
    own_kv = projected[:, width_q:].astype(jnp.bfloat16).reshape(seg_dev, SEG, 2 * width_kv)
    bias = jnp.where(path_alive, 0.0, NEG).astype(jnp.float32)
    attended, log_totals, group_kv, w_gate_up, w_down, w_out, cot_all = attend_gather(
        path_slots,
        bias,
        queries,
        own_kv,
        gate_up_weight,
        down_weight,
        out_weight,
        cotangent,
        depth,
        shard_count,
        rep_count,
        half,
    )
    gate_up_late, down_late, attended = lax.optimization_barrier(
        (
            lax.dynamic_slice_in_dim(gate_up_weight, first_expert + half, half),
            lax.dynamic_slice_in_dim(down_weight, first_expert + half, half),
            attended,
        )
    )
    w_gate_up_late = lax.all_gather(gate_up_late, "shard", axis=1, tiled=True)
    w_down_late = lax.all_gather(down_late, "shard", axis=1, tiled=True)
    w_gate_up = w_gate_up.reshape(half, D, -1)
    w_down = w_down.reshape(half, FF, D)
    w_out = w_out.reshape(H * HD, D)
    cot_all = cot_all.reshape(-1, D)
    residual = token_values + jnp.dot(attended, w_out, preferred_element_type=jnp.float32)
    normed_second, scale_second = norm_rows(residual, gain_second)
    act_second = normed_second.astype(jnp.bfloat16)
    logits = jnp.dot(act_second, w_router, preferred_element_type=jnp.float32)
    expert_ids = jnp.arange(E, dtype=jnp.int32)
    picks = routes[:, :, None] == expert_ids[None, None, :]
    chosen = jnp.sum(jnp.where(picks, logits[:, None, :], 0.0), axis=-1)
    gates = jax.nn.softmax(chosen, axis=-1)
    upstream = cotangent.astype(jnp.float32)
    gate_table = jnp.sum(jnp.where(picks, gates[:, :, None], 0.0), axis=1)
    act_all, gate_all = share_rows(act_second, gate_table.T, rep_count)
    act_all = act_all.reshape(-1, D)
    own_gate = lax.dynamic_slice_in_dim(gate_all, first_expert, own_experts, axis=1)
    own_gate = own_gate.transpose(1, 0, 2).reshape(own_experts, -1, 1)
    first_half = expert_forward(act_all, own_gate[:half], w_gate_up, w_down, cot_all)
    first_half = first_half[:3] + (
        row_pieces(first_half[3], shard_count),
        row_pieces(first_half[4], shard_count),
    )
    first_half, w_gate_up_late, w_down_late = lax.optimization_barrier(
        (first_half, w_gate_up_late, w_down_late)
    )
    second_half = expert_forward(act_all, own_gate[half:], w_gate_up_late, w_down_late, cot_all)
    mix_part = first_half[0] + second_half[0]
    gate_grad_own = jnp.concatenate([first_half[1], second_half[1]], axis=0)
    gate_up_early = lax.psum_scatter(first_half[3], "shard", scatter_dimension=0, tiled=False)
    down_early = lax.psum_scatter(first_half[4], "shard", scatter_dimension=0, tiled=False)
    down_grad = second_half[4]
    gate_up_grad = second_half[3]
    gate_grad_all = lax.all_gather(gate_grad_own, "rep", axis=0, tiled=True)
    gate_grad_table = lax.dynamic_slice_in_dim(
        gate_grad_all, rep_index * token_count, token_count, axis=1
    ).T
    inner_gate = jnp.sum(gate_table * gate_grad_table, axis=-1, keepdims=True)
    logit_grad = gate_table * (gate_grad_table - inner_gate)
    router_grad = jnp.dot(
        act_second.astype(jnp.float32).T,
        logit_grad,
        precision=lax.Precision.HIGHEST,
        preferred_element_type=jnp.float32,
    )
    act_part = (first_half[2] + second_half[2]).astype(jnp.bfloat16)
    act_second_grad = join_reps(act_part.reshape(rep_count, token_count, D))
    act_second_grad = act_second_grad + jnp.dot(
        logit_grad,
        w_router.astype(jnp.float32).T,
        precision=lax.Precision.HIGHEST,
        preferred_element_type=jnp.float32,
    )
    through_second, gain_grad_second = norm_back(
        residual, scale_second, gains[1].astype(jnp.float32), act_second_grad
    )
    residual_grad = upstream + through_second
    branch_grad = residual_grad.astype(jnp.bfloat16)
    out_grad = jnp.dot(attended.T, branch_grad, preferred_element_type=jnp.float32)
    attended_grad = lax.dot_general(
        branch_grad, w_out, (((1,), (1,)), ((), ())), preferred_element_type=jnp.float32
    ).astype(jnp.bfloat16)
    attended_grad, gate_up_early, down_early, mix_part = lax.optimization_barrier(
        (attended_grad, gate_up_early, down_early, mix_part.astype(jnp.bfloat16))
    )
    mixture = lax.psum_scatter(mix_part, "rep", scatter_dimension=0, tiled=True)
    block_out = (residual + mixture.astype(jnp.float32)).astype(jnp.bfloat16)
    query_grad, own_grad, gate_up_share, down_share = attend_back(
        path_slots,
        bias,
        path_levels(path_slots, path_alive, group_size),
        queries,
        group_kv,
        attended,
        attended_grad,
        log_totals,
        gate_up_grad.astype(jnp.bfloat16).reshape(half, shard_count, -1, 2 * FF),
        down_grad.astype(jnp.bfloat16).reshape(half, shard_count, -1, D),
        depth,
        shard_count,
    )
    projected_grad = jnp.concatenate(
        [query_grad, own_grad.reshape(token_count, 2 * width_kv)], axis=1
    )
    qkv_grad = jnp.dot(act_first.T, projected_grad, preferred_element_type=jnp.float32)
    act_first_grad = lax.dot_general(
        projected_grad, w_qkv, (((1,), (1,)), ((), ())), preferred_element_type=jnp.float32
    )
    through_first, gain_grad_first = norm_back(
        token_values, scale_first, gains[0].astype(jnp.float32), act_first_grad
    )
    token_grad = residual_grad + through_first
    small_grad = jnp.concatenate(
        [
            gain_grad_first[:, None],
            gain_grad_second[:, None],
            router_grad,
            jnp.zeros((D, LANES - E - 2), jnp.float32),
        ],
        axis=1,
    )
    grads = [
        grad.astype(jnp.bfloat16).reshape(shard_count, 1, D // shard_count, -1)
        for grad in (qkv_grad, out_grad, small_grad)
    ]
    qkv_grad, out_grad, small_grad, gate_up_grad, down_grad = finish_grads(
        grads, (True, True, False), (gate_up_early, gate_up_share), (down_early, down_share), rep_count
    )
    small_grad = small_grad[0].astype(jnp.float32)
    return (
        block_out,
        token_grad,
        small_grad[:, :2].T,
        qkv_grad[0].astype(jnp.float32),
        out_grad[0].astype(jnp.float32),
        small_grad[:, 2 : 2 + E],
        gate_up_grad.reshape((E,) + gate_up_grad.shape[2:]).astype(jnp.float32),
        down_grad.reshape((E,) + down_grad.shape[2:]).astype(jnp.float32),
    )


def solution(mesh):
    in_specs = (
        P(("rep", "shard"), None),
        P(None, "shard"),
        P("shard", None),
        P("shard", None),
        P("shard", None),
        P(None, "shard", None),
        P(None, "shard", None),
        P(("rep", "shard"), None),
        P(),
        P(),
        P(("rep", "shard"), None),
    )
    out_specs = (
        P(("rep", "shard"), None),
        P(("rep", "shard"), None),
        P(None, "shard"),
        P("shard", None),
        P("shard", None),
        P("shard", None),
        P(None, "shard", None),
        P(None, "shard", None),
    )
    return jax.shard_map(shards, mesh=mesh, in_specs=in_specs, out_specs=out_specs, check_vma=False)
```

```python
import functools

import jax
import jax.experimental.pallas as pl
import jax.experimental.pallas.tpu as pltpu
import jax.numpy as jnp
from jax import lax
from jax.sharding import PartitionSpec as P

D = 1536
H = 24
KVH = 8
HD = 64
FF = 512
TOP = 8
E = 16
SEG = 128
TRUNK = 8
TREE_DEVS = 4
TREE_SEGS = 20
CAP = 352


EPS = 1e-06


PAIRS = KVH // 2
LANES = 2 * HD
NEG=-1e30
def low_half(): return lax.broadcasted_iota(jnp.int32,(SEG,LANES),1)<HD
def stack_heads(ref, row, pair, factor=None):
    low=low_half()
    t=[ref[pl.ds(row,SEG), pl.ds(pl.multiple_of((3*pair+i)*LANES,LANES),LANES)].astype(jnp.float32) for i in range(3)]
    if factor is not None: t=[x*factor for x in t]
    z=jnp.zeros_like(t[0])
    r0=pltpu.roll(t[0],HD,1); r2=pltpu.roll(t[2],HD,1)
    parts=[jnp.where(low,t[0],z),jnp.where(low,r0,z),jnp.where(low,t[1],z),
           jnp.where(low,z,t[1]),jnp.where(low,z,r2),jnp.where(low,z,t[2])]
    return jnp.concatenate(parts,axis=0)
def unstack_heads(rows):
    low=low_half()
    a=[rows[i*SEG:(i+1)*SEG] for i in range(6)]
    return [jnp.where(low,a[0],pltpu.roll(a[1],HD,1)), jnp.where(low,a[2],a[3]), jnp.where(low,pltpu.roll(a[4],HD,1),a[5])]
def kv_path(kv_ref, slots, seg, depth, col):
    return jnp.concatenate([kv_ref[slots[seg,lev],:,pl.ds(pl.multiple_of(col,LANES),LANES)] for lev in range(depth)],axis=0)
NT=(((1,),(1,)),((),())); NN=(((1,),(0,)),((),())); TN=(((0,),(0,)),((),()))
def dot(a,b,dims): return lax.dot_general(a,b,dims,preferred_element_type=jnp.float32)
def causal_bias(width):
    key=lax.broadcasted_iota(jnp.int32,(SEG,width),0); qry=lax.broadcasted_iota(jnp.int32,(SEG,width),1)%SEG
    return jnp.where(key<=qry,0.0,NEG)
def fwd_step(depth, slots, bias, q_ref, kv_ref, o_ref, lse_ref, s_scr, p_scr, i, c):
    width=6*SEG
    seg=i//PAIRS; pair=i%PAIRS
    row=pl.multiple_of(seg*SEG,SEG)
    q6=stack_heads(q_ref,row,pair,HD**-0.5).astype(jnp.bfloat16)
    top=jnp.full((8,width),NEG,jnp.float32)
    for lev in range(depth):
        k=kv_ref[slots[seg,lev],:,pl.ds(pl.multiple_of(pair*LANES,LANES),LANES)]
        s=dot(k,q6,NT)
        s=s+(causal_bias(width) if lev==0 else bias[seg,lev])
        s_scr[lev*SEG:(lev+1)*SEG,:]=s
        top=jnp.maximum(top,jnp.max(s.reshape(SEG//8,8,width),axis=0))
    top=jnp.max(top,axis=0,keepdims=True)
    tot=jnp.zeros((8,width),jnp.float32)
    acc=jnp.zeros((LANES,width),jnp.float32)
    for lev in range(depth):
        p=jnp.exp(s_scr[lev*SEG:(lev+1)*SEG,:]-top)
        tot=tot+jnp.sum(p.reshape(SEG//8,8,width),axis=0)
        p_scr[lev*SEG:(lev+1)*SEG,:]=p.astype(jnp.bfloat16)
    v=kv_path(kv_ref,slots,seg,depth,KVH*HD+pair*LANES)
    acc=dot(v,p_scr[...],TN)
    tot=jnp.sum(tot,axis=0,keepdims=True)
    lse_ref[i]=jnp.broadcast_to(top+jnp.log(tot),(8,width))
    o6=(acc/tot).T
    for j,t in enumerate(unstack_heads(o6)):
        o_ref[pl.ds(row,SEG),pl.ds(pl.multiple_of((3*pair+j)*LANES,LANES),LANES)]=t.astype(o_ref.dtype)
    return c
def bwd_step(depth, slots, bias, q_ref, kv_ref, o_ref, do_ref, lse_ref, dq_ref, path, p_scr, d_scr, i, c):
    width=6*SEG
    seg=i//PAIRS; pair=i%PAIRS
    row=pl.multiple_of(seg*SEG,SEG)
    q6=stack_heads(q_ref,row,pair,HD**-0.5).astype(jnp.bfloat16)
    do6f=stack_heads(do_ref,row,pair)
    do6=do6f.astype(jnp.bfloat16)
    prod=do6f*stack_heads(o_ref,row,pair)
    hi=prod.astype(jnp.bfloat16); lo=(prod-hi.astype(jnp.float32)).astype(jnp.bfloat16)
    ones=jnp.ones((8,LANES),jnp.bfloat16)
    delta=(dot(ones,hi,NT)+dot(ones,lo,NT))[:1]
    lse=lse_ref[i][:1]
    kcol=pl.multiple_of(pair*LANES,LANES); vcol=pl.multiple_of(KVH*HD+pair*LANES,LANES)
    for lev in range(depth):
        k=kv_ref[slots[seg,lev],:,pl.ds(kcol,LANES)]
        v=kv_ref[slots[seg,lev],:,pl.ds(vcol,LANES)]
        s=dot(k,q6,NT)
        s=s+(causal_bias(width) if lev==0 else bias[seg,lev])
        p=jnp.exp(s-lse)
        dp=dot(v,do6,NT)
        ds=(p*(dp-delta)).astype(jnp.bfloat16)
        p_scr[lev*SEG:(lev+1)*SEG,:]=p.astype(jnp.bfloat16)
        d_scr[lev*SEG:(lev+1)*SEG,:]=ds
    dv=dot(p_scr[...],do6,NN)
    dk=dot(d_scr[...],q6,NN)
    for lev in range(depth):
        path[seg,lev,:,pl.ds(kcol,LANES)]=dk[lev*SEG:(lev+1)*SEG].astype(path.dtype)
        path[seg,lev,:,pl.ds(vcol,LANES)]=dv[lev*SEG:(lev+1)*SEG].astype(path.dtype)
    k=kv_path(kv_ref,slots,seg,depth,pair*LANES)
    dq6=(dot(k,d_scr[...],TN)*(HD**-0.5)).T
    for j,t in enumerate(unstack_heads(dq6)):
        dq_ref[pl.ds(row,SEG),pl.ds(pl.multiple_of((3*pair+j)*LANES,LANES),LANES)]=t.astype(dq_ref.dtype)
    return c
def bwd_collect(inv, path, group, slot, c):
    for col in range(0,2*KVH*HD,256):
        tot=path[0,inv[slot,0],:,col:col+256].astype(jnp.float32)
        for seg in range(1,path.shape[0]): tot=tot+path[seg,inv[slot,seg],:,col:col+256].astype(jnp.float32)
        group[slot,:,col:col+256]=tot.astype(group.dtype)
    return c
MESH = pl.DeviceIdType.MESH
ANY = pl.BlockSpec(memory_space=pl.ANY)
VMEM = pl.BlockSpec(memory_space=pltpu.VMEM)
SMEM = pl.BlockSpec(memory_space=pltpu.SMEM)


def work(flops, moved):
    return pl.CostEstimate(flops=int(flops), bytes_accessed=int(moved), transcendentals=0)


class Sends:
    def __init__(self):
        self.open = []

    def start(self, cond, src, dst, send_sem, recv_sem, device):
        copy = pltpu.make_async_remote_copy(
            src_ref=src, dst_ref=dst, send_sem=send_sem, recv_sem=recv_sem, device_id=device, device_id_type=MESH
        )
        when(cond, copy.start)
        self.open.append((cond, copy.wait_send))

    def local(self, src, dst, sem):
        copy = pltpu.make_async_copy(src, dst, sem)
        copy.start()
        self.open.append((None, copy.wait))

    def drain(self):
        for cond, wait in self.open:
            when(cond, wait)
        self.open = []


def when(cond, body):
    if cond is None:
        body()
    else:
        pl.when(cond)(body)


def received(cond, region, send_sem, recv_sem, device):
    copy = pltpu.make_async_remote_copy(
        src_ref=region, dst_ref=region, send_sem=send_sem, recv_sem=recv_sem, device_id=device, device_id_type=MESH
    )
    when(cond, copy.wait_recv)


def line_place(shards):
    me = lax.axis_index("shard")
    return me, me // 2, shards // 2


def greet(devices):
    barrier = pltpu.get_barrier_semaphore()
    count = 0
    for cond, device in devices:
        when(
            cond,
            lambda device=device: pl.semaphore_signal(barrier, inc=1, device_id=device, device_id_type=MESH),
        )
        count = count + (1 if cond is None else cond.astype(jnp.int32))
    pl.semaphore_wait(barrier, count)


def line_neighbours(shards):
    me, spot, length = line_place(shards)
    return [
        (None, {"shard": me + 1 - 2 * (me % 2)}),
        (spot > 0, {"shard": me - 2}),
        (spot + 1 < length, {"shard": me + 2}),
    ]


class LineGather:
    def __init__(self, shards, sources, region, up, down, pair, local_sem, arrived=None, order=None):
        self.shards, self.sources, self.region = shards, sources, region
        self.up, self.down, self.pair, self.local_sem = up, down, pair, local_sem
        self.arrived = arrived or (lambda cond, block, index: None)
        self.order = order or tuple(range(len(sources)))
        self.sends = Sends()
        self.me, self.spot, self.length = line_place(shards)
        self.twin = self.me + 1 - 2 * (self.me % 2)

    def forward(self, cond, block, step, rising, falling, src=None):
        place = step if rising else self.length - 1 + step
        for n in self.order:
            here = self.region(n, block)
            out = here if src is None else src[n]
            ways = []
            if rising:
                ways.append((both(cond, self.spot + 1 < self.length), self.up, step + 1, self.me + 2))
            if falling:
                ways.append((both(cond, self.spot > 0), self.down, step + 1, self.me - 2))
            for where, sems, index, device in ways:
                if index < self.length:
                    self.sends.start(where, out, here, sems.at[0, index, n], sems.at[1, index, n], {"shard": device})
            self.sends.start(
                cond, out, here, self.pair.at[0, place, n], self.pair.at[1, place, n], {"shard": self.twin}
            )

    def begin(self):
        for n, src in enumerate(self.sources):
            self.sends.local(src, self.region(n, self.me), self.local_sem.at[n])
        self.forward(None, self.me, 0, True, True, self.sources)

    def finish_local(self):
        for cond, wait in self.sends.open[: len(self.sources)]:
            wait()
        self.sends.open = self.sends.open[len(self.sources) :]

    def step(self, step):
        for sems, cond, block, rising in (
            (self.up, self.spot - step >= 0, self.me - 2 * step, True),
            (self.down, self.spot + step < self.length, self.me + 2 * step, False),
        ):
            for n in range(len(self.sources)):
                received(cond, self.region(n, block), sems.at[0, step, n], sems.at[1, step, n], {"shard": self.twin})
            self.forward(cond, block, step, rising, not rising)
            self.arrived(cond, block, step if rising else self.length - 1 + step)

    def pair_step(self, step):
        turns = [(None, self.twin, 0)] if step == 0 else [
            (self.spot - step >= 0, self.twin - 2 * step, step),
            (self.spot + step < self.length, self.twin + 2 * step, self.length - 1 + step),
        ]
        for cond, block, place in turns:
            for n in range(len(self.sources)):
                received(
                    cond, self.region(n, block), self.pair.at[0, place, n], self.pair.at[1, place, n], {"shard": self.twin}
                )
            self.arrived(cond, block, 2 * self.length - 1 + place)


def both(first, second):
    return second if first is None else jnp.logical_and(first, second)


def line_sems(shards, arrays):
    length = shards // 2
    return [
        pltpu.SemaphoreType.DMA((2, length, arrays)),
        pltpu.SemaphoreType.DMA((2, length, arrays)),
        pltpu.SemaphoreType.DMA((2, 2 * length - 1, arrays)),
        pltpu.SemaphoreType.DMA((arrays,)),
    ]


class RepSpread:
    def __init__(self, arrays, region, cross, core, relay):
        self.arrays, self.region = arrays, region
        self.cross, self.core, self.relay = cross, core, relay
        rep = lax.axis_index("rep")
        self.rep = rep
        self.near = rep + 1 - 2 * (rep % 2)
        self.far = lax.rem(rep + 2, 4)
        self.diagonal = lax.rem(self.near + 2, 4)
        self.sends = Sends()
        self.blocks = []
        self.passed = []
        self.sources = None

    def arrived(self, cond, block, index):
        for n in self.arrays:
            here = self.region(n, self.rep, block)
            src = here if self.sources is None else self.sources[n]
            self.sends.start(
                cond, src, here, self.cross.at[0, block, n], self.cross.at[1, block, n], {"rep": self.far}
            )
            self.sends.start(
                cond, src, here, self.core.at[0, block, n], self.core.at[1, block, n], {"rep": self.near}
            )
        self.blocks.append((cond, block))

    def pass_on(self):
        for cond, block in self.blocks:
            for n in self.arrays:
                here = self.region(n, self.far, block)
                received(cond, here, self.cross.at[0, block, n], self.cross.at[1, block, n], {"rep": self.far})
                self.sends.start(
                    cond, here, here, self.relay.at[0, block, n], self.relay.at[1, block, n], {"rep": self.near}
                )
        self.passed = self.passed + self.blocks
        self.blocks = []

    def end(self):
        self.pass_on()
        for cond, block in self.passed:
            for n in self.arrays:
                for sems, part in ((self.core, self.near), (self.relay, self.diagonal)):
                    here = self.region(n, part, block)
                    received(cond, here, sems.at[0, block, n], sems.at[1, block, n], {"rep": self.near})
        self.sends.drain()


def rep_neighbours():
    rep = lax.axis_index("rep")
    return [(None, {"rep": rep + 1 - 2 * (rep % 2)}), (None, {"rep": lax.rem(rep + 2, 4)})]


def rep_sems(shards, arrays):
    return [pltpu.SemaphoreType.DMA((2, shards, arrays)) for unused in range(3)]


def part_columns(ref, part, width):
    return ref.at[:, pl.ds(pl.multiple_of(part * width, LANES), width)]


def weights_kernel(shards, qkv, small, qkv_all, small_all, up, down, pair, local_sem, cross, core, relay):
    rep = lax.axis_index("rep")
    greet(line_neighbours(shards) + rep_neighbours())
    width = qkv.shape[1] // lax.axis_size("rep")

    def part(n, owner, block):
        return small_all.at[block] if n == 1 else part_columns(qkv_all.at[block], owner, width)

    spread = RepSpread((0,), part, cross, core, relay)
    spread.sources = None
    gather = LineGather(
        shards,
        (part_columns(qkv, rep, width), small),
        lambda n, block: part(n, rep, block),
        up,
        down,
        pair,
        local_sem,
        spread.arrived,
    )
    gather.begin()
    gather.finish_local()
    spread.arrived(None, gather.me, 0)
    for step in range(gather.length):
        if step:
            gather.step(step)
        spread.pass_on()
        gather.pair_step(step)
    spread.end()
    gather.sends.drain()


def gather_weights(qkv_weight, small, shards):
    shapes = [(shards,) + qkv_weight.shape, (shards,) + small.shape]
    return pl.pallas_call(
        functools.partial(weights_kernel, shards),
        out_shape=[jax.ShapeDtypeStruct(shape, jnp.bfloat16) for shape in shapes],
        in_specs=[ANY] * 2,
        out_specs=[ANY] * 2,
        scratch_shapes=line_sems(shards, 2) + rep_sems(shards, 1),
        cost_estimate=work(0, 2e8),
        compiler_params=pltpu.CompilerParams(collective_id=1, has_side_effects=True),
    )(qkv_weight, small)


def attend_gather_kernel(
    depth,
    shards,
    experts,
    slots,
    bias,
    q_ref,
    kv_ref,
    gu_ref,
    dn_ref,
    out_ref,
    cot_ref,
    o_ref,
    lse_ref,
    kv_all,
    gu_all,
    dn_all,
    out_all,
    cot_all,
    s_scr,
    p_scr,
    kv_sems,
    cot_sem,
    up,
    down,
    pair,
    local_sem,
    cross,
    core,
    relay,
    cot_cross,
    cot_core,
    cot_relay,
):
    me = lax.axis_index("shard")
    rep = lax.axis_index("rep")
    member = me % TREE_DEVS
    seg_dev = kv_ref.shape[0]
    twin = me + 1 - 2 * (member % 2)
    across = me + 2 - 4 * (member // 2)
    greet(line_neighbours(shards) + rep_neighbours() + [(None, {"shard": across})])
    sends = Sends()

    def kv_block(owner):
        return kv_all.at[pl.ds(owner % TREE_DEVS * seg_dev, seg_dev)]

    own = kv_block(me)
    sends.start(None, kv_ref, own, kv_sems.at[0, 0], kv_sems.at[1, 0], {"shard": twin})
    sends.start(None, kv_ref, own, kv_sems.at[0, 1], kv_sems.at[1, 1], {"shard": across})
    width = out_ref.shape[1] // lax.axis_size("rep")
    own_experts = gu_ref.shape[0] // lax.axis_size("rep")

    def part(n, owner, block):
        if n == 2:
            return part_columns(out_all.at[block], owner, width)
        return (gu_all, dn_all)[n].at[:, block]

    spread = RepSpread((2,), part, cross, core, relay)
    gather = LineGather(
        shards,
        (
            gu_ref.at[pl.ds(rep * own_experts + own_experts // 2 - experts, experts)],
            dn_ref.at[pl.ds(rep * own_experts, own_experts // 2)],
            part_columns(out_ref, rep, width),
        ),
        lambda n, block: part(n, rep, block),
        up,
        down,
        pair,
        local_sem,
        spread.arrived,
        (2, 0, 1),
    )
    gather.begin()
    sends.local(cot_ref, cot_all.at[rep], cot_sem)
    cot_spread = RepSpread((0,), lambda n, owner, block: cot_all.at[owner], cot_cross, cot_core, cot_relay)
    cot_spread.sources = (cot_ref,)
    cot_spread.arrived(None, 0, 0)
    gather.finish_local()
    spread.arrived(None, me, 0)
    kv_all[pl.ds(member * seg_dev, seg_dev)] = kv_ref[...]
    theirs = kv_block(twin)
    received(None, theirs, kv_sems.at[0, 0], kv_sems.at[1, 0], {"shard": twin})
    sends.start(None, theirs, theirs, kv_sems.at[0, 2], kv_sems.at[1, 2], {"shard": across})
    gather.step(1)
    gather.pair_step(0)
    received(None, kv_block(across), kv_sems.at[0, 1], kv_sems.at[1, 1], {"shard": across})
    diagonal = across + 1 - 2 * (member % 2)
    received(None, kv_block(diagonal), kv_sems.at[0, 2], kv_sems.at[1, 2], {"shard": across})
    count = seg_dev * PAIRS
    attend = functools.partial(fwd_step, depth, slots, bias, q_ref, kv_all, o_ref, lse_ref, s_scr, p_scr)
    done = 0
    for step in range(2, gather.length + 1):
        upto = count * (step - 1) // (gather.length - 1)
        lax.fori_loop(done, upto, attend, 0)
        done = upto
        if step < gather.length:
            gather.step(step)
            gather.pair_step(step - 1)
            spread.pass_on()
    cot_spread.end()
    gather.pair_step(gather.length - 1)
    spread.end()
    gather.sends.drain()
    sends.drain()


def attend_gather(slots, bias, q, kv, gate_up, down, out, cotangent, depth, shards, reps, experts):
    tokens = q.shape[0]
    count = tokens // SEG * PAIRS
    shapes = [
        q.shape,
        (TREE_DEVS * kv.shape[0],) + kv.shape[1:],
        (experts, shards) + gate_up.shape[1:],
        (down.shape[0] // reps // 2, shards) + down.shape[1:],
        (shards,) + out.shape,
        (reps,) + cotangent.shape,
    ]
    outs = [jax.ShapeDtypeStruct(shape, jnp.bfloat16) for shape in shapes]
    return pl.pallas_call(
        functools.partial(attend_gather_kernel, depth, shards, experts),
        out_shape=outs[:1] + [jax.ShapeDtypeStruct((count, 8, 6 * SEG), jnp.float32)] + outs[1:],
        in_specs=[SMEM, SMEM, VMEM, VMEM] + [ANY] * 4,
        out_specs=[VMEM] * 3 + [ANY] * 4,
        scratch_shapes=[
            pltpu.VMEM((depth * SEG, 6 * SEG), jnp.float32),
            pltpu.VMEM((depth * SEG, 6 * SEG), jnp.bfloat16),
            pltpu.SemaphoreType.DMA((2, TREE_DEVS - 1)),
            pltpu.SemaphoreType.DMA,
        ]
        + line_sems(shards, 3)
        + rep_sems(shards, 3)
        + rep_sems(1, 1),
        cost_estimate=work(2e10, 7e8),
        compiler_params=pltpu.CompilerParams(
            collective_id=2, has_side_effects=True, vmem_limit_bytes=48 * 2**20
        ),
    )(slots, bias, q, kv, gate_up, down, out, cotangent)


def share_kernel(chunks, rows_ref, gate_ref, rows_all, gate_all, own_sems, cross, core, relay):
    rep = lax.axis_index("rep")
    greet(rep_neighbours())
    size = rows_ref.shape[0] // chunks

    def piece(n, part, block):
        return gate_all.at[part] if n == chunks else rows_all.at[part, pl.ds(n * size, size)]

    spread = RepSpread(tuple(range(chunks + 1)), piece, cross, core, relay)
    spread.sources = [rows_ref.at[pl.ds(n * size, size)] for n in range(chunks)] + [gate_ref]
    spread.arrived(None, 0, 0)
    for n in range(chunks + 1):
        spread.sends.local(spread.sources[n], piece(n, rep, 0), own_sems.at[n])
    spread.end()


def share_rows(rows, gates, reps):
    chunks = 4
    return pl.pallas_call(
        functools.partial(share_kernel, chunks),
        out_shape=[
            jax.ShapeDtypeStruct((reps,) + rows.shape, rows.dtype),
            jax.ShapeDtypeStruct((reps,) + gates.shape, gates.dtype),
        ],
        in_specs=[ANY] * 2,
        out_specs=[ANY] * 2,
        scratch_shapes=[pltpu.SemaphoreType.DMA((chunks + 1,))] + rep_sems(1, chunks + 1),
        cost_estimate=work(0, 1.6e8),
        compiler_params=pltpu.CompilerParams(collective_id=6, has_side_effects=True),
    )(rows, gates)


def join_kernel(part, total, near_buf, cross_out, cross_buf, near_sems, cross_sems):
    rep = lax.axis_index("rep")
    near = rep + 1 - 2 * (rep % 2)
    far = lax.rem(rep + 2, 4)
    diagonal = lax.rem(near + 2, 4)
    greet(rep_neighbours())
    sends = Sends()
    chunks = near_sems.shape[2]
    size = total.shape[0] // chunks
    for slot, owner in ((1, diagonal), (0, near)):
        for c in range(chunks):
            rows = pl.ds(c * size, size)
            sends.start(
                None,
                part.at[owner, rows],
                near_buf.at[slot, rows],
                near_sems.at[0, slot, c],
                near_sems.at[1, slot, c],
                {"rep": near},
            )

    def got(slot, c):
        here = near_buf.at[slot, pl.ds(c * size, size)]
        received(None, here, near_sems.at[0, slot, c], near_sems.at[1, slot, c], {"rep": near})

    step = 32 if size % 32 == 0 else size
    for c in range(chunks):
        got(1, c)

        def first(i, carry, c=c):
            rows = pl.ds(pl.multiple_of(c * size + i * step, step), step)
            value = part[far, rows].astype(jnp.float32) + near_buf[1, rows].astype(jnp.float32)
            cross_out[rows] = value.astype(cross_out.dtype)
            return carry

        lax.fori_loop(0, size // step, first, 0)
        rows = pl.ds(c * size, size)
        sends.start(
            None, cross_out.at[rows], cross_buf.at[rows], cross_sems.at[0, c], cross_sems.at[1, c], {"rep": far}
        )
    for c in range(chunks):
        got(0, c)
        here = cross_buf.at[pl.ds(c * size, size)]
        received(None, here, cross_sems.at[0, c], cross_sems.at[1, c], {"rep": far})

        def second(i, carry, c=c):
            rows = pl.ds(pl.multiple_of(c * size + i * step, step), step)
            value = part[rep, rows].astype(jnp.float32) + near_buf[0, rows].astype(jnp.float32)
            total[rows] = value + cross_buf[rows].astype(jnp.float32)
            return carry

        lax.fori_loop(0, size // step, second, 0)
    sends.drain()


def join_reps(part):
    block = part.shape[1:]
    chunks = 4
    return pl.pallas_call(
        join_kernel,
        out_shape=jax.ShapeDtypeStruct(block, jnp.float32),
        in_specs=[VMEM],
        out_specs=VMEM,
        scratch_shapes=[
            pltpu.VMEM((2,) + block, jnp.bfloat16),
            pltpu.VMEM(block, jnp.bfloat16),
            pltpu.VMEM(block, jnp.bfloat16),
            pltpu.SemaphoreType.DMA((2, 2, chunks)),
            pltpu.SemaphoreType.DMA((2, chunks)),
        ],
        cost_estimate=work(0, 1.6e8),
        compiler_params=pltpu.CompilerParams(
            collective_id=5, has_side_effects=True, vmem_limit_bytes=40 * 2**20
        ),
    )(part)


class LineScatter:
    def __init__(self, shards, arrays, local, pair_buf, line_buf, temp, stages, outs, pair, line, loads, ready=None):
        self.shards, self.arrays, self.local = shards, arrays, local
        self.pair_buf, self.line_buf, self.temp = pair_buf, line_buf, temp
        self.stages, self.outs = stages, outs
        self.pair, self.line, self.loads = pair, line, loads
        self.ready = ready or (lambda block: None)
        self.sends = Sends()
        self.me, self.spot, self.length = line_place(shards)
        self.side = self.me % 2
        self.twin = self.me + 1 - 2 * self.side

    def add(self, n, sources, target):
        stage, out = self.stages[n], self.outs[n]
        copies = []
        for k, (cond, ref) in enumerate(sources):
            copy = pltpu.make_async_copy(ref, stage.at[k], self.loads.at[k])
            copies.append((cond, copy))
            when(cond, copy.start)
        outer, rows, width = out.shape
        chunk = 32 if rows % 32 == 0 else rows
        pieces = rows // chunk

        def clear(k):
            def one(i, c):
                row = pl.multiple_of(i % pieces * chunk, chunk)
                stage[k, i // pieces, pl.ds(row, chunk)] = jnp.zeros((chunk, width), stage.dtype)
                return c

            lax.fori_loop(0, outer * pieces, one, 0)

        for k, (cond, copy) in enumerate(copies):
            when(cond, copy.wait)
            if cond is not None:
                pl.when(jnp.logical_not(cond))(functools.partial(clear, k))

        def one(i, c):
            row = pl.multiple_of(i % pieces * chunk, chunk)
            total = stage[0, i // pieces, pl.ds(row, chunk)].astype(jnp.float32)
            for k in range(1, len(sources)):
                total = total + stage[k, i // pieces, pl.ds(row, chunk)].astype(jnp.float32)
            out[i // pieces, pl.ds(row, chunk)] = total.astype(out.dtype)
            return c

        lax.fori_loop(0, outer * pieces, one, 0)
        store = pltpu.make_async_copy(out, target, self.loads.at[self.loads.shape[0] - 1])
        store.start()
        store.wait()

    def pick(self, turn):
        spot, last = self.spot, self.length - 1
        low = jnp.where(turn < last - spot, last - turn, turn - last + spot)
        high = jnp.where(turn < spot, turn, last - turn + spot)
        return jnp.where(turn == last, spot, jnp.where(2 * spot < self.length, low, high))

    def offer(self, turn):
        if turn >= self.length:
            return
        target = self.pick(turn)
        block = 2 * target + 1 - self.side
        self.ready(block)
        for n in range(self.arrays):
            sources = self.local(n, block)
            src = sources[0]
            if len(sources) > 1:
                src = self.temp[n].at[target]
                self.add(n, [(None, ref) for ref in sources], src)
            self.sends.start(
                None,
                src,
                self.pair_buf[n].at[target],
                self.pair.at[0, target, n],
                self.pair.at[1, target, n],
                {"shard": self.twin},
            )

    def got_pair(self, target, n):
        received(
            None,
            self.pair_buf[n].at[target],
            self.pair.at[0, target, n],
            self.pair.at[1, target, n],
            {"shard": self.twin},
        )

    def got_line(self, cond, slot, n, device):
        received(cond, self.line_buf[n].at[slot], self.line.at[0, slot, n], self.line.at[1, slot, n], {"shard": device})

    def step(self, slot):
        below, above = self.spot > 0, self.spot + 1 < self.length
        mirrored = self.length - 1 - self.spot
        turns = (
            (self.spot <= slot, self.length - 1 - slot + self.spot, True, below, self.me - 2, self.me + 2),
            (mirrored <= slot, slot - mirrored, False, above, self.me + 2, self.me - 2),
        )
        for cond, target, rising, has, source, device in turns:
            block = 2 * target + self.side
            place = target if rising else jnp.where(self.spot == target + 1, self.length, target)
            for n in range(self.arrays):
                copy = pltpu.make_async_remote_copy(
                    src_ref=self.pair_buf[n].at[target],
                    dst_ref=self.line_buf[n].at[place],
                    send_sem=self.line.at[0, place, n],
                    recv_sem=self.line.at[1, place, n],
                    device_id={"shard": device},
                    device_id_type=MESH,
                )

                def body(n=n, copy=copy, target=target, has=has, source=source, block=block):
                    self.got_pair(target, n)
                    self.got_line(has, target, n, source)
                    if n == 0:
                        self.ready(block)
                    sources = [(None, ref) for ref in self.local(n, block)]
                    sources += [(None, self.pair_buf[n].at[target]), (has, self.line_buf[n].at[target])]
                    self.add(n, sources, self.pair_buf[n].at[target])
                    copy.start()

                pl.when(cond)(body)
                self.sends.open.append((cond, copy.wait_send))

    def finish(self, targets):
        below, above = self.spot > 0, self.spot + 1 < self.length
        self.ready(self.me)
        for n in range(self.arrays):
            self.got_pair(self.spot, n)
            self.got_line(below, self.spot, n, self.me - 2)
            self.got_line(above, self.length, n, self.me + 2)
            sources = [(None, ref) for ref in self.local(n, self.me)]
            sources += [
                (None, self.pair_buf[n].at[self.spot]),
                (below, self.line_buf[n].at[self.spot]),
                (above, self.line_buf[n].at[self.length]),
            ]
            self.add(n, sources, targets[n])


def scatter_sems(shards, arrays, loads):
    length = shards // 2
    return [
        pltpu.SemaphoreType.DMA((2, length, arrays)),
        pltpu.SemaphoreType.DMA((2, length + 1, arrays)),
        pltpu.SemaphoreType.DMA((loads + 1,)),
    ]


def scatter_buffers(shards, block):
    length = shards // 2
    return [
        jax.ShapeDtypeStruct((length,) + block, jnp.bfloat16),
        jax.ShapeDtypeStruct((length + 1,) + block, jnp.bfloat16),
    ]


def back_kernel(
    depth,
    shards,
    slots,
    bias,
    inv,
    q_ref,
    kv_ref,
    o_ref,
    do_ref,
    lse_ref,
    gu_ref,
    dn_ref,
    dq_ref,
    dkv_ref,
    gu_out,
    dn_out,
    gu_pair,
    gu_line,
    dn_pair,
    dn_line,
    path,
    p_scr,
    d_scr,
    group,
    guest,
    passing,
    landed,
    gu_stage,
    dn_stage,
    gu_sum,
    dn_sum,
    kv_sems,
    pair,
    line,
    loads,
):
    me = lax.axis_index("shard")
    member = me % TREE_DEVS
    segs = q_ref.shape[0] // SEG
    twin = me + 1 - 2 * (member % 2)
    across = me + 2 - 4 * (member // 2)
    greet(line_neighbours(shards) + [(None, {"shard": across})])
    scatter = LineScatter(
        shards,
        2,
        lambda n, block: [(gu_ref, dn_ref)[n].at[:, block]],
        (gu_pair, dn_pair),
        (gu_line, dn_line),
        None,
        (gu_stage, dn_stage),
        (gu_sum, dn_sum),
        pair,
        line,
        loads,
    )
    scatter.offer(0)
    path[:, depth] = jnp.zeros((segs,) + path.shape[2:], path.dtype)
    step = functools.partial(
        bwd_step, depth, slots, bias, q_ref, kv_ref, o_ref, do_ref, lse_ref, dq_ref, path, p_scr, d_scr
    )
    count = segs * PAIRS
    cuts = (0, count * 8 // 20, count * 14 // 20, count)
    scatter.offer(1)
    lax.fori_loop(cuts[0], cuts[1], step, 0)
    scatter.step(0)
    scatter.offer(2)
    lax.fori_loop(cuts[1], cuts[2], step, 0)
    if scatter.length > 2:
        scatter.step(1)
    scatter.offer(3)
    lax.fori_loop(cuts[2], cuts[3], step, 0)
    lax.fori_loop(0, group.shape[0], functools.partial(bwd_collect, inv, path, group), 0)
    sends = Sends()
    side = member % 2
    for turn, slot in ((0, 1 - side), (1, side)):
        owner = (across - side + slot) % TREE_DEVS
        sends.start(
            None,
            group.at[pl.ds(owner * segs, segs)],
            guest.at[slot],
            kv_sems.at[0, turn],
            kv_sems.at[1, turn],
            {"shard": across},
        )

    def join(mine, slot, extra, target):
        def one(seg, c):
            for col in range(0, 2 * KVH * HD, 256):
                total = group[mine * segs + seg, :, col : col + 256].astype(jnp.float32)
                total = total + guest[slot, seg, :, col : col + 256].astype(jnp.float32)
                if extra is not None:
                    total = total + extra[seg, :, col : col + 256].astype(jnp.float32)
                target[seg, :, col : col + 256] = total.astype(target.dtype)
            return c

        lax.fori_loop(0, segs, one, 0)

    received(None, guest.at[1 - side], kv_sems.at[0, 0], kv_sems.at[1, 0], {"shard": across})
    join(twin % TREE_DEVS, 1 - side, None, passing)
    sends.start(None, passing, landed, kv_sems.at[0, 2], kv_sems.at[1, 2], {"shard": twin})
    for turn in range(2, scatter.length - 1):
        scatter.offer(turn + 2)
        scatter.step(turn)
    received(None, guest.at[side], kv_sems.at[0, 1], kv_sems.at[1, 1], {"shard": across})
    received(None, landed, kv_sems.at[0, 2], kv_sems.at[1, 2], {"shard": twin})
    join(member, side, landed, dkv_ref)
    scatter.finish((gu_out, dn_out))
    sends.drain()
    scatter.sends.drain()


def attend_back(slots, bias, inv, q, kv, o, do, lse, gate_up_grad, down_grad, depth, shards):
    segs = q.shape[0] // SEG
    own_kv = (segs,) + kv.shape[1:]
    gu_block = (gate_up_grad.shape[0],) + gate_up_grad.shape[2:]
    dn_block = (down_grad.shape[0],) + down_grad.shape[2:]
    outs = [
        jax.ShapeDtypeStruct(q.shape, jnp.bfloat16),
        jax.ShapeDtypeStruct(own_kv, jnp.bfloat16),
        jax.ShapeDtypeStruct(gu_block, jnp.bfloat16),
        jax.ShapeDtypeStruct(dn_block, jnp.bfloat16),
    ]
    outs += scatter_buffers(shards, gu_block) + scatter_buffers(shards, dn_block)
    return pl.pallas_call(
        functools.partial(back_kernel, depth, shards),
        out_shape=outs,
        in_specs=[SMEM] * 3 + [VMEM] * 5 + [ANY] * 2,
        out_specs=[VMEM] * 2 + [ANY] * 6,
        scratch_shapes=[
            pltpu.VMEM((segs, depth + 1, SEG, 2 * KVH * HD), jnp.bfloat16),
            pltpu.VMEM((depth * SEG, 6 * SEG), jnp.bfloat16),
            pltpu.VMEM((depth * SEG, 6 * SEG), jnp.bfloat16),
            pltpu.VMEM(kv.shape, jnp.bfloat16),
            pltpu.VMEM((2,) + own_kv, jnp.bfloat16),
            pltpu.VMEM(own_kv, jnp.bfloat16),
            pltpu.VMEM(own_kv, jnp.bfloat16),
            pltpu.VMEM((4,) + gu_block, jnp.bfloat16),
            pltpu.VMEM((4,) + dn_block, jnp.bfloat16),
            pltpu.VMEM(gu_block, jnp.bfloat16),
            pltpu.VMEM(dn_block, jnp.bfloat16),
            pltpu.SemaphoreType.DMA((2, TREE_DEVS - 1)),
        ]
        + scatter_sems(shards, 2, 4),
        cost_estimate=work(5e10, 7e8),
        compiler_params=pltpu.CompilerParams(
            collective_id=3, has_side_effects=True, vmem_limit_bytes=60 * 2**20
        ),
    )(slots, bias, inv, q, kv, o, do, lse, gate_up_grad, down_grad)[:4]


def finish_kernel(shards, arrays, pieces, *refs):
    refs = list(refs)

    def take(count):
        taken = refs[:count]
        del refs[:count]
        return taken

    grads = take(arrays)
    shares = take(pieces)
    outs = take(arrays)
    expert_outs = take(2)
    core_bufs = take(arrays)
    share_bufs = take(arrays)
    cross_bufs = take(arrays)
    temps = take(arrays)
    pair_bufs = take(arrays)
    line_bufs = take(arrays)
    stages = take(arrays)
    totals = take(arrays)
    core_sems, swap_sems, own_sems, cross, core, relay, pair, line, loads = refs
    rep = lax.axis_index("rep")
    near = rep + 1 - 2 * (rep % 2)
    far = lax.rem(rep + 2, 4)
    half = rep % 2
    greet(line_neighbours(shards) + rep_neighbours())
    sends = Sends()
    length = shards // 2
    side = lax.axis_index("shard") % 2

    def columns(n, ref, which):
        width = totals[n].shape[-1]
        if width == ref.shape[-1]:
            return ref
        return ref.at[:, :, pl.ds(pl.multiple_of(which * width, LANES), width)]

    experts = pieces // 2
    size = shares[0].shape[0]

    def place(n, part, block):
        return expert_outs[n // experts].at[part, pl.ds(n % experts * size, size)]

    for n in range(pieces):
        sends.local(shares[n], place(n, rep, 0), own_sems.at[n])
    spread = RepSpread(tuple(range(pieces)), place, cross, core, relay)
    spread.sources = shares
    spread.arrived(None, 0, 0)

    def ready(block):
        for n in range(arrays):
            received(
                None, core_bufs[n].at[block], core_sems.at[0, block, n], core_sems.at[1, block, n], {"rep": near}
            )

    scatter = LineScatter(
        shards,
        arrays,
        lambda n, block: [columns(n, grads[n].at[block], half), core_bufs[n].at[block]],
        pair_bufs,
        line_bufs,
        temps,
        stages,
        totals,
        pair,
        line,
        loads,
        ready,
    )
    for turn in range(length):
        for which in (1 - side, side):
            block = 2 * scatter.pick(turn) + which
            for n in range(arrays):
                sends.start(
                    None,
                    columns(n, grads[n].at[block], 1 - half),
                    core_bufs[n].at[block],
                    core_sems.at[0, block, n],
                    core_sems.at[1, block, n],
                    {"rep": near},
                )
    scatter.offer(0)
    scatter.offer(1)
    for turn in range(scatter.length - 1):
        scatter.offer(turn + 2)
        scatter.step(turn)
    scatter.finish(share_bufs)
    for n in range(arrays):
        sends.start(
            None, share_bufs[n], cross_bufs[n], swap_sems.at[0, 0, n], swap_sems.at[1, 0, n], {"rep": far}
        )
    spread.end()
    for n in range(arrays):
        received(None, cross_bufs[n], swap_sems.at[0, 0, n], swap_sems.at[1, 0, n], {"rep": far})
        mine = columns(n, outs[n], half)
        scatter.add(n, [(None, share_bufs[n]), (None, cross_bufs[n])], mine)
        if outs[n].shape != totals[n].shape:
            sends.start(None, mine, mine, swap_sems.at[0, 1, n], swap_sems.at[1, 1, n], {"rep": near})
    for n in range(arrays):
        if outs[n].shape != totals[n].shape:
            theirs = columns(n, outs[n], 1 - half)
            received(None, theirs, swap_sems.at[0, 1, n], swap_sems.at[1, 1, n], {"rep": near})
    sends.drain()
    scatter.sends.drain()


def finish_grads(grads, halved, gate_up_shares, down_shares, reps):
    shards = grads[0].shape[0]
    arrays = len(grads)
    parts = len(gate_up_shares)
    wholes = [grad.shape[1:] for grad in grads]
    blocks = [
        whole[:-1] + (whole[-1] // 2 if halve else whole[-1],) for whole, halve in zip(wholes, halved)
    ]
    experts = parts * gate_up_shares[0].shape[0]
    shapes = list(wholes)
    shapes += [(reps, experts) + gate_up_shares[0].shape[1:], (reps, experts) + down_shares[0].shape[1:]]
    shapes += [(shards,) + block for block in blocks]
    shapes += blocks + blocks
    shapes += [(shards // 2,) + block for block in blocks]
    shapes += [(shards // 2,) + block for block in blocks]
    shapes += [(shards // 2 + 1,) + block for block in blocks]
    return pl.pallas_call(
        functools.partial(finish_kernel, shards, arrays, 2 * parts),
        out_shape=[jax.ShapeDtypeStruct(shape, jnp.bfloat16) for shape in shapes],
        in_specs=[ANY] * (arrays + 2 * parts),
        out_specs=[ANY] * len(shapes),
        scratch_shapes=[pltpu.VMEM((5,) + block, jnp.bfloat16) for block in blocks]
        + [pltpu.VMEM(block, jnp.bfloat16) for block in blocks]
        + [
            pltpu.SemaphoreType.DMA((2, shards, arrays)),
            pltpu.SemaphoreType.DMA((2, 2, arrays)),
            pltpu.SemaphoreType.DMA((2 * parts,)),
        ]
        + rep_sems(1, 2 * parts)
        + scatter_sems(shards, arrays, 5),
        cost_estimate=work(0, 4e8),
        compiler_params=pltpu.CompilerParams(
            collective_id=4, has_side_effects=True, vmem_limit_bytes=32 * 2**20
        ),
    )(*grads, *gate_up_shares, *down_shares)[: arrays + 2]


def norm_rows(values, gain):
    scale_rows = lax.rsqrt(jnp.mean(values * values, axis=-1, keepdims=True) + EPS)
    return (values * scale_rows * gain, scale_rows)


def norm_back(values, scale_rows, gain, upstream):
    scaled = upstream * gain
    inner = jnp.mean(scaled * values, axis=-1, keepdims=True)
    through = scale_rows * scaled - values * (scale_rows * scale_rows * scale_rows) * inner
    gain_grad = jnp.sum(upstream * values * scale_rows, axis=0)
    return (through, gain_grad)


def table_lookup(table, index):
    positions = jnp.arange(table.shape[0], dtype=jnp.int32)
    return jnp.sum(jnp.where(index[:, None] == positions[None, :], table[None, :], 0), axis=1)


def find_slot(group_ids, wanted):
    positions = jnp.arange(group_ids.shape[0], dtype=jnp.int32)
    return jnp.sum(jnp.where(group_ids[None, :] == wanted[:, None], positions[None, :], 0), axis=1)


def ancestor_slots(local_ids, group_ids, group_parents, depth):
    flat_parents = group_parents.reshape(-1)
    tree_index = local_ids // TREE_SEGS
    current = local_ids % TREE_SEGS
    alive = jnp.ones(local_ids.shape, dtype=bool)
    slot_list = []
    alive_list = []
    for level in range(depth):
        wanted = tree_index * TREE_SEGS + current
        slot_list.append(find_slot(group_ids, wanted))
        alive_list.append(alive)
        parent_seg = table_lookup(flat_parents, wanted)
        alive = alive & (parent_seg != current)
        current = parent_seg
    return (jnp.stack(slot_list, axis=1), jnp.stack(alive_list, axis=1))


def path_levels(path_slots, path_alive, slot_count):
    depth = path_slots.shape[1]
    slots = jnp.arange(slot_count, dtype=jnp.int32)
    hit = path_alive[None] & (path_slots[None] == slots[:, None, None])
    levels = jnp.arange(depth, dtype=jnp.int32)
    return depth - jnp.sum(jnp.where(hit, depth - levels, 0), axis=2)


def row_pieces(grad, shards):
    experts, rows, width = grad.shape
    return grad.astype(jnp.bfloat16).reshape(experts, shards, rows // shards, width).transpose(1, 0, 2, 3)


def expert_forward(rows, gates, w_gate_up, w_down, upstream):
    gate_up = jnp.einsum("td,edf->etf", rows, w_gate_up, preferred_element_type=jnp.bfloat16)
    gate_part = gate_up[..., :FF].astype(jnp.float32)
    up_part = gate_up[..., FF:].astype(jnp.float32)
    sig_gate = jax.nn.sigmoid(gate_part)
    hidden = gate_part * sig_gate * up_part
    gated = (hidden * gates).astype(jnp.bfloat16)
    mix_part = jnp.einsum("etf,efd->td", gated, w_down, preferred_element_type=jnp.float32)
    raw_grad = jnp.einsum("td,efd->etf", upstream, w_down, preferred_element_type=jnp.float32)
    gate_grad = jnp.sum(hidden * raw_grad, axis=-1)
    hidden_grad = raw_grad * gates
    gate_grad_part = hidden_grad * up_part * sig_gate * (1.0 + gate_part * (1.0 - sig_gate))
    up_grad_part = hidden_grad * gate_part * sig_gate
    row_grads = jnp.concatenate([gate_grad_part, up_grad_part], axis=-1).astype(jnp.bfloat16)
    down_grad = jnp.einsum("etf,td->efd", gated, upstream, preferred_element_type=jnp.float32)
    gate_up_grad = jnp.einsum("td,etf->edf", rows, row_grads, preferred_element_type=jnp.float32)
    act_part = jnp.einsum("etf,edf->td", row_grads, w_gate_up, preferred_element_type=jnp.float32)
    return (mix_part, gate_grad, act_part, gate_up_grad, down_grad)


def shards(
    tokens,
    norm_gains,
    qkv_weight,
    out_weight,
    router_weight,
    gate_up_weight,
    down_weight,
    routes,
    placement,
    parents,
    cotangent,
):
    shard_index = lax.axis_index("shard")
    rep_index = lax.axis_index("rep")
    shard_count = lax.axis_size("shard")
    token_count = tokens.shape[0]
    seg_dev = token_count // SEG
    depth = TRUNK + 2
    width_q = H * HD
    width_kv = KVH * HD
    group_size = TREE_DEVS * seg_dev
    tree_count = group_size // TREE_SEGS
    member = shard_index % TREE_DEVS
    group = (rep_index * shard_count + shard_index) // TREE_DEVS
    group_ids = lax.dynamic_slice_in_dim(placement, group * group_size, group_size)
    group_parents = lax.dynamic_slice_in_dim(parents, group * tree_count, tree_count)
    local_ids = lax.dynamic_slice_in_dim(group_ids, member * seg_dev, seg_dev)
    path_slots, path_alive = ancestor_slots(local_ids, group_ids, group_parents, depth)
    rep_count = lax.axis_size("rep")
    own_experts = E // rep_count
    first_expert = rep_index * own_experts
    half = own_experts // 2
    padding = jnp.zeros((norm_gains.shape[1], LANES - E - 2), jnp.bfloat16)
    small = jnp.concatenate([router_weight, norm_gains.T, padding], axis=1)
    w_qkv, small = gather_weights(qkv_weight, small, shard_count)
    w_qkv = w_qkv.reshape(D, -1)
    small = small.reshape(D, LANES)
    w_router = small[:, :E]
    gains = small[:, E : E + 2].T
    gain_first = gains[0].astype(jnp.float32)
    gain_second = gains[1].astype(jnp.float32)
    token_values = tokens.astype(jnp.float32)
    normed_first, scale_first = norm_rows(token_values, gain_first)
    act_first = normed_first.astype(jnp.bfloat16)
    projected = jnp.dot(act_first, w_qkv, preferred_element_type=jnp.float32)
    queries = projected[:, :width_q].astype(jnp.bfloat16)
    w_gate_up_early = lax.all_gather(
        lax.dynamic_slice_in_dim(gate_up_weight, first_expert, half - 1), "shard", axis=1, tiled=True
    )
    queries, w_gate_up_early = lax.optimization_barrier((queries, w_gate_up_early))
    own_kv = projected[:, width_q:].astype(jnp.bfloat16).reshape(seg_dev, SEG, 2 * width_kv)
    bias = jnp.where(path_alive, 0.0, NEG).astype(jnp.float32)
    attended, log_totals, group_kv, w_gate_up, w_down, w_out, cot_all = attend_gather(
        path_slots,
        bias,
        queries,
        own_kv,
        gate_up_weight,
        down_weight,
        out_weight,
        cotangent,
        depth,
        shard_count,
        rep_count,
        1,
    )
    gate_up_late, down_late, attended = lax.optimization_barrier(
        (
            lax.dynamic_slice_in_dim(gate_up_weight, first_expert + half, half),
            lax.dynamic_slice_in_dim(down_weight, first_expert + half, half),
            attended,
        )
    )
    w_gate_up_late = lax.all_gather(gate_up_late, "shard", axis=1, tiled=True)
    w_down_late = lax.all_gather(down_late, "shard", axis=1, tiled=True)
    w_gate_up = jnp.concatenate([w_gate_up_early, w_gate_up.reshape(1, D, -1)], axis=0)
    w_down = w_down.reshape(half, FF, D)
    w_out = w_out.reshape(H * HD, D)
    cot_all = cot_all.reshape(-1, D)
    residual = token_values + jnp.dot(attended, w_out, preferred_element_type=jnp.float32)
    normed_second, scale_second = norm_rows(residual, gain_second)
    act_second = normed_second.astype(jnp.bfloat16)
    logits = jnp.dot(act_second, w_router, preferred_element_type=jnp.float32)
    expert_ids = jnp.arange(E, dtype=jnp.int32)
    picks = routes[:, :, None] == expert_ids[None, None, :]
    chosen = jnp.sum(jnp.where(picks, logits[:, None, :], 0.0), axis=-1)
    gates = jax.nn.softmax(chosen, axis=-1)
    upstream = cotangent.astype(jnp.float32)
    gate_table = jnp.sum(jnp.where(picks, gates[:, :, None], 0.0), axis=1)
    act_all, gate_all = share_rows(act_second, gate_table.T, rep_count)
    act_all = act_all.reshape(-1, D)
    own_gate = lax.dynamic_slice_in_dim(gate_all, first_expert, own_experts, axis=1)
    own_gate = own_gate.transpose(1, 0, 2).reshape(own_experts, -1, 1)
    first_half = expert_forward(act_all, own_gate[:half], w_gate_up, w_down, cot_all)
    first_half = first_half[:3] + (
        row_pieces(first_half[3], shard_count),
        row_pieces(first_half[4], shard_count),
    )
    first_half, w_gate_up_late, w_down_late = lax.optimization_barrier(
        (first_half, w_gate_up_late, w_down_late)
    )
    second_half = expert_forward(act_all, own_gate[half:], w_gate_up_late, w_down_late, cot_all)
    mix_part = first_half[0] + second_half[0]
    gate_grad_own = jnp.concatenate([first_half[1], second_half[1]], axis=0)
    gate_up_early = lax.psum_scatter(first_half[3], "shard", scatter_dimension=0, tiled=False)
    down_early = lax.psum_scatter(first_half[4], "shard", scatter_dimension=0, tiled=False)
    down_grad = second_half[4]
    gate_up_grad = second_half[3]
    gate_grad_all = lax.all_gather(gate_grad_own, "rep", axis=0, tiled=True)
    gate_grad_table = lax.dynamic_slice_in_dim(
        gate_grad_all, rep_index * token_count, token_count, axis=1
    ).T
    inner_gate = jnp.sum(gate_table * gate_grad_table, axis=-1, keepdims=True)
    logit_grad = gate_table * (gate_grad_table - inner_gate)
    router_grad = jnp.dot(
        act_second.astype(jnp.float32).T,
        logit_grad,
        precision=lax.Precision.HIGHEST,
        preferred_element_type=jnp.float32,
    )
    act_part = (first_half[2] + second_half[2]).astype(jnp.bfloat16)
    act_second_grad = join_reps(act_part.reshape(rep_count, token_count, D))
    act_second_grad = act_second_grad + jnp.dot(
        logit_grad,
        w_router.astype(jnp.float32).T,
        precision=lax.Precision.HIGHEST,
        preferred_element_type=jnp.float32,
    )
    through_second, gain_grad_second = norm_back(
        residual, scale_second, gains[1].astype(jnp.float32), act_second_grad
    )
    residual_grad = upstream + through_second
    branch_grad = residual_grad.astype(jnp.bfloat16)
    out_grad = jnp.dot(attended.T, branch_grad, preferred_element_type=jnp.float32)
    attended_grad = lax.dot_general(
        branch_grad, w_out, (((1,), (1,)), ((), ())), preferred_element_type=jnp.float32
    ).astype(jnp.bfloat16)
    attended_grad, gate_up_early, down_early = lax.optimization_barrier(
        (attended_grad, gate_up_early, down_early)
    )
    query_grad, own_grad, gate_up_share, down_share = attend_back(
        path_slots,
        bias,
        path_levels(path_slots, path_alive, group_size),
        queries,
        group_kv,
        attended,
        attended_grad,
        log_totals,
        gate_up_grad.astype(jnp.bfloat16).reshape(half, shard_count, -1, 2 * FF),
        down_grad.astype(jnp.bfloat16).reshape(half, shard_count, -1, D),
        depth,
        shard_count,
    )
    mix_part, query_grad = lax.optimization_barrier((mix_part.astype(jnp.bfloat16), query_grad))
    mixture = lax.psum_scatter(mix_part, "rep", scatter_dimension=0, tiled=True)
    block_out = (residual + mixture.astype(jnp.float32)).astype(jnp.bfloat16)
    projected_grad = jnp.concatenate(
        [query_grad, own_grad.reshape(token_count, 2 * width_kv)], axis=1
    )
    qkv_grad = jnp.dot(act_first.T, projected_grad, preferred_element_type=jnp.float32)
    act_first_grad = lax.dot_general(
        projected_grad, w_qkv, (((1,), (1,)), ((), ())), preferred_element_type=jnp.float32
    )
    through_first, gain_grad_first = norm_back(
        token_values, scale_first, gains[0].astype(jnp.float32), act_first_grad
    )
    token_grad = residual_grad + through_first
    small_grad = jnp.concatenate(
        [
            gain_grad_first[:, None],
            gain_grad_second[:, None],
            router_grad,
            jnp.zeros((D, LANES - E - 2), jnp.float32),
        ],
        axis=1,
    )
    grads = [
        grad.astype(jnp.bfloat16).reshape(shard_count, 1, D // shard_count, -1)
        for grad in (qkv_grad, out_grad, small_grad)
    ]
    qkv_grad, out_grad, small_grad, gate_up_grad, down_grad = finish_grads(
        grads, (True, True, False), (gate_up_early, gate_up_share), (down_early, down_share), rep_count
    )
    small_grad = small_grad[0].astype(jnp.float32)
    return (
        block_out,
        token_grad,
        small_grad[:, :2].T,
        qkv_grad[0].astype(jnp.float32),
        out_grad[0].astype(jnp.float32),
        small_grad[:, 2 : 2 + E],
        gate_up_grad.reshape((E,) + gate_up_grad.shape[2:]).astype(jnp.float32),
        down_grad.reshape((E,) + down_grad.shape[2:]).astype(jnp.float32),
    )


def solution(mesh):
    in_specs = (
        P(("rep", "shard"), None),
        P(None, "shard"),
        P("shard", None),
        P("shard", None),
        P("shard", None),
        P(None, "shard", None),
        P(None, "shard", None),
        P(("rep", "shard"), None),
        P(),
        P(),
        P(("rep", "shard"), None),
    )
    out_specs = (
        P(("rep", "shard"), None),
        P(("rep", "shard"), None),
        P(None, "shard"),
        P("shard", None),
        P("shard", None),
        P("shard", None),
        P(None, "shard", None),
        P(None, "shard", None),
    )
    return jax.shard_map(shards, mesh=mesh, in_specs=in_specs, out_specs=out_specs, check_vma=False)
```

```python
import functools

import jax
import jax.experimental.pallas as pl
import jax.experimental.pallas.tpu as pltpu
import jax.numpy as jnp
from jax import lax
from jax.experimental.layout import Layout, with_layout_constraint
from jax.sharding import PartitionSpec as P

D = 1536
H = 24
KVH = 8
HD = 64
FF = 512
TOP = 8
E = 16
SEG = 128
TRUNK = 8
TREE_DEVS = 4
TREE_SEGS = 20
CAP = 352


EPS = 1e-06


PAIRS = KVH // 2
LANES = 2 * HD
NEG=-1e30
def low_half(): return lax.broadcasted_iota(jnp.int32,(SEG,LANES),1)<HD
def stack_heads(ref, row, pair, factor=None):
    low=low_half()
    t=[ref[pl.ds(row,SEG), pl.ds(pl.multiple_of((3*pair+i)*LANES,LANES),LANES)].astype(jnp.float32) for i in range(3)]
    if factor is not None: t=[x*factor for x in t]
    z=jnp.zeros_like(t[0])
    r0=pltpu.roll(t[0],HD,1); r2=pltpu.roll(t[2],HD,1)
    parts=[jnp.where(low,t[0],z),jnp.where(low,r0,z),jnp.where(low,t[1],z),
           jnp.where(low,z,t[1]),jnp.where(low,z,r2),jnp.where(low,z,t[2])]
    return jnp.concatenate(parts,axis=0)
def unstack_heads(rows):
    low=low_half()
    a=[rows[i*SEG:(i+1)*SEG] for i in range(6)]
    return [jnp.where(low,a[0],pltpu.roll(a[1],HD,1)), jnp.where(low,a[2],a[3]), jnp.where(low,pltpu.roll(a[4],HD,1),a[5])]
def kv_path(kv_ref, slots, seg, depth, col):
    return jnp.concatenate([kv_ref[slots[seg,lev],:,pl.ds(pl.multiple_of(col,LANES),LANES)] for lev in range(depth)],axis=0)
NT=(((1,),(1,)),((),())); NN=(((1,),(0,)),((),())); TN=(((0,),(0,)),((),()))
def dot(a,b,dims): return lax.dot_general(a,b,dims,preferred_element_type=jnp.float32)
def causal_bias(width):
    key=lax.broadcasted_iota(jnp.int32,(SEG,width),0); qry=lax.broadcasted_iota(jnp.int32,(SEG,width),1)%SEG
    return jnp.where(key<=qry,0.0,NEG)
def fwd_step(depth, slots, bias, q_ref, kv_ref, o_ref, lse_ref, s_scr, p_scr, i, c):
    width=6*SEG
    seg=i//PAIRS; pair=i%PAIRS
    row=pl.multiple_of(seg*SEG,SEG)
    q6=stack_heads(q_ref,row,pair,HD**-0.5).astype(jnp.bfloat16)
    top=jnp.full((8,width),NEG,jnp.float32)
    for lev in range(depth):
        k=kv_ref[slots[seg,lev],:,pl.ds(pl.multiple_of(pair*LANES,LANES),LANES)]
        s=dot(k,q6,NT)
        s=s+(causal_bias(width) if lev==0 else bias[seg,lev])
        s_scr[lev*SEG:(lev+1)*SEG,:]=s
        top=jnp.maximum(top,jnp.max(s.reshape(SEG//8,8,width),axis=0))
    top=jnp.max(top,axis=0,keepdims=True)
    tot=jnp.zeros((8,width),jnp.float32)
    acc=jnp.zeros((LANES,width),jnp.float32)
    for lev in range(depth):
        p=jnp.exp(s_scr[lev*SEG:(lev+1)*SEG,:]-top)
        tot=tot+jnp.sum(p.reshape(SEG//8,8,width),axis=0)
        p_scr[lev*SEG:(lev+1)*SEG,:]=p.astype(jnp.bfloat16)
    v=kv_path(kv_ref,slots,seg,depth,KVH*HD+pair*LANES)
    acc=dot(v,p_scr[...],TN)
    tot=jnp.sum(tot,axis=0,keepdims=True)
    lse_ref[i]=jnp.broadcast_to(top+jnp.log(tot),(8,width))
    o6=(acc/tot).T
    for j,t in enumerate(unstack_heads(o6)):
        o_ref[pl.ds(row,SEG),pl.ds(pl.multiple_of((3*pair+j)*LANES,LANES),LANES)]=t.astype(o_ref.dtype)
    return c
def bwd_step(depth, slots, bias, q_ref, kv_ref, o_ref, do_ref, lse_ref, dq_ref, path, p_scr, d_scr, i, c):
    width=6*SEG
    seg=i//PAIRS; pair=i%PAIRS
    row=pl.multiple_of(seg*SEG,SEG)
    q6=stack_heads(q_ref,row,pair,HD**-0.5).astype(jnp.bfloat16)
    do6f=stack_heads(do_ref,row,pair)
    do6=do6f.astype(jnp.bfloat16)
    prod=do6f*stack_heads(o_ref,row,pair)
    hi=prod.astype(jnp.bfloat16); lo=(prod-hi.astype(jnp.float32)).astype(jnp.bfloat16)
    ones=jnp.ones((8,LANES),jnp.bfloat16)
    delta=(dot(ones,hi,NT)+dot(ones,lo,NT))[:1]
    lse=lse_ref[i][:1]
    kcol=pl.multiple_of(pair*LANES,LANES); vcol=pl.multiple_of(KVH*HD+pair*LANES,LANES)
    for lev in range(depth):
        k=kv_ref[slots[seg,lev],:,pl.ds(kcol,LANES)]
        v=kv_ref[slots[seg,lev],:,pl.ds(vcol,LANES)]
        s=dot(k,q6,NT)
        s=s+(causal_bias(width) if lev==0 else bias[seg,lev])
        p=jnp.exp(s-lse)
        dp=dot(v,do6,NT)
        ds=(p*(dp-delta)).astype(jnp.bfloat16)
        p_scr[lev*SEG:(lev+1)*SEG,:]=p.astype(jnp.bfloat16)
        d_scr[lev*SEG:(lev+1)*SEG,:]=ds
    dv=dot(p_scr[...],do6,NN)
    dk=dot(d_scr[...],q6,NN)
    for lev in range(depth):
        path[seg,lev,:,pl.ds(kcol,LANES)]=dk[lev*SEG:(lev+1)*SEG].astype(path.dtype)
        path[seg,lev,:,pl.ds(vcol,LANES)]=dv[lev*SEG:(lev+1)*SEG].astype(path.dtype)
    k=kv_path(kv_ref,slots,seg,depth,pair*LANES)
    dq6=(dot(k,d_scr[...],TN)*(HD**-0.5)).T
    for j,t in enumerate(unstack_heads(dq6)):
        dq_ref[pl.ds(row,SEG),pl.ds(pl.multiple_of((3*pair+j)*LANES,LANES),LANES)]=t.astype(dq_ref.dtype)
    return c
def bwd_collect(inv, path, group, slot, c):
    for col in range(0,2*KVH*HD,256):
        tot=path[0,inv[slot,0],:,col:col+256].astype(jnp.float32)
        for seg in range(1,path.shape[0]): tot=tot+path[seg,inv[slot,seg],:,col:col+256].astype(jnp.float32)
        group[slot,:,col:col+256]=tot.astype(group.dtype)
    return c
MESH = pl.DeviceIdType.MESH
ANY = pl.BlockSpec(memory_space=pl.ANY)
VMEM = pl.BlockSpec(memory_space=pltpu.VMEM)
SMEM = pl.BlockSpec(memory_space=pltpu.SMEM)


def work(flops, moved):
    return pl.CostEstimate(flops=int(flops), bytes_accessed=int(moved), transcendentals=0)


class Sends:
    def __init__(self):
        self.open = []

    def start(self, cond, src, dst, send_sem, recv_sem, device):
        copy = pltpu.make_async_remote_copy(
            src_ref=src, dst_ref=dst, send_sem=send_sem, recv_sem=recv_sem, device_id=device, device_id_type=MESH
        )
        when(cond, copy.start)
        self.open.append((cond, copy.wait_send))

    def local(self, src, dst, sem):
        copy = pltpu.make_async_copy(src, dst, sem)
        copy.start()
        self.open.append((None, copy.wait))

    def drain(self):
        for cond, wait in self.open:
            when(cond, wait)
        self.open = []


def when(cond, body):
    if cond is None:
        body()
    else:
        pl.when(cond)(body)


def received(cond, region, send_sem, recv_sem, device):
    copy = pltpu.make_async_remote_copy(
        src_ref=region, dst_ref=region, send_sem=send_sem, recv_sem=recv_sem, device_id=device, device_id_type=MESH
    )
    when(cond, copy.wait_recv)


def line_place(shards):
    me = lax.axis_index("shard")
    return me, me // 2, shards // 2


def greet(devices):
    barrier = pltpu.get_barrier_semaphore()
    count = 0
    for cond, device in devices:
        when(
            cond,
            lambda device=device: pl.semaphore_signal(barrier, inc=1, device_id=device, device_id_type=MESH),
        )
        count = count + (1 if cond is None else cond.astype(jnp.int32))
    pl.semaphore_wait(barrier, count)


def line_neighbours(shards):
    me, spot, length = line_place(shards)
    return [
        (None, {"shard": me + 1 - 2 * (me % 2)}),
        (spot > 0, {"shard": me - 2}),
        (spot + 1 < length, {"shard": me + 2}),
    ]


class LineGather:
    def __init__(self, shards, sources, region, up, down, pair, local_sem, arrived=None, order=None):
        self.shards, self.sources, self.region = shards, sources, region
        self.up, self.down, self.pair, self.local_sem = up, down, pair, local_sem
        self.arrived = arrived or (lambda cond, block, index: None)
        self.order = order or tuple(range(len(sources)))
        self.sends = Sends()
        self.me, self.spot, self.length = line_place(shards)
        self.twin = self.me + 1 - 2 * (self.me % 2)

    def forward(self, cond, block, step, rising, falling, src=None):
        place = step if rising else self.length - 1 + step
        for n in self.order:
            here = self.region(n, block)
            out = here if src is None else src[n]
            ways = []
            if rising:
                ways.append((both(cond, self.spot + 1 < self.length), self.up, step + 1, self.me + 2))
            if falling:
                ways.append((both(cond, self.spot > 0), self.down, step + 1, self.me - 2))
            for where, sems, index, device in ways:
                if index < self.length:
                    self.sends.start(where, out, here, sems.at[0, index, n], sems.at[1, index, n], {"shard": device})
            self.sends.start(
                cond, out, here, self.pair.at[0, place, n], self.pair.at[1, place, n], {"shard": self.twin}
            )

    def begin(self):
        for n, src in enumerate(self.sources):
            self.sends.local(src, self.region(n, self.me), self.local_sem.at[n])
        self.forward(None, self.me, 0, True, True, self.sources)

    def step(self, step):
        for sems, cond, block, rising in (
            (self.up, self.spot - step >= 0, self.me - 2 * step, True),
            (self.down, self.spot + step < self.length, self.me + 2 * step, False),
        ):
            for n in range(len(self.sources)):
                received(cond, self.region(n, block), sems.at[0, step, n], sems.at[1, step, n], {"shard": self.twin})
            self.forward(cond, block, step, rising, not rising)
            self.arrived(cond, block, step if rising else self.length - 1 + step)

    def pair_step(self, step):
        turns = [(None, self.twin, 0)] if step == 0 else [
            (self.spot - step >= 0, self.twin - 2 * step, step),
            (self.spot + step < self.length, self.twin + 2 * step, self.length - 1 + step),
        ]
        for cond, block, place in turns:
            for n in range(len(self.sources)):
                received(
                    cond, self.region(n, block), self.pair.at[0, place, n], self.pair.at[1, place, n], {"shard": self.twin}
                )
            self.arrived(cond, block, 2 * self.length - 1 + place)


def both(first, second):
    return second if first is None else jnp.logical_and(first, second)


def line_sems(shards, arrays):
    length = shards // 2
    return [
        pltpu.SemaphoreType.DMA((2, length, arrays)),
        pltpu.SemaphoreType.DMA((2, length, arrays)),
        pltpu.SemaphoreType.DMA((2, 2 * length - 1, arrays)),
        pltpu.SemaphoreType.DMA((arrays,)),
    ]


class RepSpread:
    def __init__(self, arrays, region, cross, core, relay):
        self.arrays, self.region = arrays, region
        self.cross, self.core, self.relay = cross, core, relay
        rep = lax.axis_index("rep")
        self.rep = rep
        self.near = rep + 1 - 2 * (rep % 2)
        self.far = lax.rem(rep + 2, 4)
        self.diagonal = lax.rem(self.near + 2, 4)
        self.sends = Sends()
        self.blocks = []
        self.passed = []
        self.sources = None

    def arrived(self, cond, block, index):
        for n in self.arrays:
            here = self.region(n, self.rep, block)
            src = here if self.sources is None else self.sources[n]
            self.sends.start(
                cond, src, here, self.cross.at[0, block, n], self.cross.at[1, block, n], {"rep": self.far}
            )
            self.sends.start(
                cond, src, here, self.core.at[0, block, n], self.core.at[1, block, n], {"rep": self.near}
            )
        self.blocks.append((cond, block))

    def pass_on(self):
        for cond, block in self.blocks:
            for n in self.arrays:
                here = self.region(n, self.far, block)
                received(cond, here, self.cross.at[0, block, n], self.cross.at[1, block, n], {"rep": self.far})
                self.sends.start(
                    cond, here, here, self.relay.at[0, block, n], self.relay.at[1, block, n], {"rep": self.near}
                )
        self.passed = self.passed + self.blocks
        self.blocks = []

    def end(self):
        self.pass_on()
        for cond, block in self.passed:
            for n in self.arrays:
                for sems, part in ((self.core, self.near), (self.relay, self.diagonal)):
                    here = self.region(n, part, block)
                    received(cond, here, sems.at[0, block, n], sems.at[1, block, n], {"rep": self.near})
        self.sends.drain()


def rep_neighbours():
    rep = lax.axis_index("rep")
    return [(None, {"rep": rep + 1 - 2 * (rep % 2)}), (None, {"rep": lax.rem(rep + 2, 4)})]


def rep_sems(shards, arrays):
    return [pltpu.SemaphoreType.DMA((2, shards, arrays)) for unused in range(3)]


def part_columns(ref, part, width):
    return ref.at[:, pl.ds(pl.multiple_of(part * width, LANES), width)]


def weights_kernel(shards, qkv, small, qkv_all, small_all, up, down, pair, local_sem, cross, core, relay):
    rep = lax.axis_index("rep")
    greet(line_neighbours(shards) + rep_neighbours())
    width = qkv.shape[1] // lax.axis_size("rep")

    def part(n, owner, block):
        return small_all.at[block] if n == 1 else part_columns(qkv_all.at[block], owner, width)

    spread = RepSpread((0,), part, cross, core, relay)
    gather = LineGather(
        shards,
        (part_columns(qkv, rep, width), small),
        lambda n, block: part(n, rep, block),
        up,
        down,
        pair,
        local_sem,
        spread.arrived,
    )
    gather.begin()
    spread.sources = {0: part_columns(qkv, rep, width)}
    spread.arrived(None, gather.me, 0)
    spread.sources = None
    for step in range(gather.length):
        if step:
            gather.step(step)
        spread.pass_on()
        gather.pair_step(step)
    spread.end()
    gather.sends.drain()


def gather_weights(qkv_weight, small, shards):
    shapes = [(shards,) + qkv_weight.shape, (shards,) + small.shape]
    return pl.pallas_call(
        functools.partial(weights_kernel, shards),
        out_shape=[jax.ShapeDtypeStruct(shape, jnp.bfloat16) for shape in shapes],
        in_specs=[ANY] * 2,
        out_specs=[ANY] * 2,
        scratch_shapes=line_sems(shards, 2) + rep_sems(shards, 1),
        cost_estimate=work(0, 2e8),
        compiler_params=pltpu.CompilerParams(collective_id=1, has_side_effects=True),
    )(qkv_weight, small)


def attend_gather_kernel(
    depth,
    shards,
    experts,
    slots,
    bias,
    q_ref,
    kv_ref,
    gu_ref,
    dn_ref,
    out_ref,
    cot_ref,
    early_ref,
    o_ref,
    lse_ref,
    kv_all,
    gu_all,
    dn_all,
    out_all,
    cot_all,
    s_scr,
    p_scr,
    kv_sems,
    cot_sem,
    early_sem,
    up,
    down,
    pair,
    local_sem,
    cross,
    core,
    relay,
    cot_cross,
    cot_core,
    cot_relay,
):
    me = lax.axis_index("shard")
    rep = lax.axis_index("rep")
    member = me % TREE_DEVS
    seg_dev = kv_ref.shape[0]
    twin = me + 1 - 2 * (member % 2)
    across = me + 2 - 4 * (member // 2)
    greet(line_neighbours(shards) + rep_neighbours() + [(None, {"shard": across})])
    sends = Sends()

    def kv_block(owner):
        return kv_all.at[pl.ds(owner % TREE_DEVS * seg_dev, seg_dev)]

    own = kv_block(me)
    sends.start(None, kv_ref, own, kv_sems.at[0, 0], kv_sems.at[1, 0], {"shard": twin})
    sends.start(None, kv_ref, own, kv_sems.at[0, 1], kv_sems.at[1, 1], {"shard": across})
    width = out_ref.shape[1] // lax.axis_size("rep")
    own_experts = gu_ref.shape[0] // lax.axis_size("rep")
    early = early_ref.shape[0]

    def part(n, owner, block):
        if n == 2:
            return part_columns(out_all.at[block], owner, width)
        return dn_all.at[:, block] if n else gu_all.at[pl.ds(early, experts), block]

    spread = RepSpread((2,), part, cross, core, relay)
    gather = LineGather(
        shards,
        (
            gu_ref.at[pl.ds(rep * own_experts + own_experts // 2 - experts, experts)],
            dn_ref.at[pl.ds(rep * own_experts, own_experts // 2)],
            part_columns(out_ref, rep, width),
        ),
        lambda n, block: part(n, rep, block),
        up,
        down,
        pair,
        local_sem,
        spread.arrived,
        (2, 0, 1),
    )
    gather.begin()
    sends.local(cot_ref, cot_all.at[rep], cot_sem)
    sends.local(early_ref, gu_all.at[pl.ds(0, early)], early_sem)
    cot_spread = RepSpread((0,), lambda n, owner, block: cot_all.at[owner], cot_cross, cot_core, cot_relay)
    cot_spread.sources = (cot_ref,)
    cot_spread.arrived(None, 0, 0)
    spread.sources = {2: part_columns(out_ref, rep, width)}
    spread.arrived(None, me, 0)
    spread.sources = None
    kv_all[pl.ds(member * seg_dev, seg_dev)] = kv_ref[...]
    theirs = kv_block(twin)
    received(None, theirs, kv_sems.at[0, 0], kv_sems.at[1, 0], {"shard": twin})
    sends.start(None, theirs, theirs, kv_sems.at[0, 2], kv_sems.at[1, 2], {"shard": across})
    gather.step(1)
    gather.pair_step(0)
    received(None, kv_block(across), kv_sems.at[0, 1], kv_sems.at[1, 1], {"shard": across})
    diagonal = across + 1 - 2 * (member % 2)
    received(None, kv_block(diagonal), kv_sems.at[0, 2], kv_sems.at[1, 2], {"shard": across})
    count = seg_dev * PAIRS
    attend = functools.partial(fwd_step, depth, slots, bias, q_ref, kv_all, o_ref, lse_ref, s_scr, p_scr)
    done = 0
    for step in range(2, gather.length + 1):
        upto = count * (step - 1) // (gather.length - 1)
        lax.fori_loop(done, upto, attend, 0)
        done = upto
        if step < gather.length:
            gather.step(step)
            gather.pair_step(step - 1)
            spread.pass_on()
    cot_spread.end()
    gather.pair_step(gather.length - 1)
    spread.end()
    gather.sends.drain()
    sends.drain()


def attend_gather(slots, bias, q, kv, gate_up, down, out, cotangent, early, depth, shards, reps, experts):
    tokens = q.shape[0]
    count = tokens // SEG * PAIRS
    shapes = [
        q.shape,
        (TREE_DEVS * kv.shape[0],) + kv.shape[1:],
        (early.shape[0] + experts, shards) + gate_up.shape[1:],
        (down.shape[0] // reps // 2, shards) + down.shape[1:],
        (shards,) + out.shape,
        (reps,) + cotangent.shape,
    ]
    outs = [jax.ShapeDtypeStruct(shape, jnp.bfloat16) for shape in shapes]
    return pl.pallas_call(
        functools.partial(attend_gather_kernel, depth, shards, experts),
        out_shape=outs[:1] + [jax.ShapeDtypeStruct((count, 8, 6 * SEG), jnp.float32)] + outs[1:],
        in_specs=[SMEM, SMEM, VMEM, VMEM] + [ANY] * 3 + [VMEM] * 2,
        out_specs=[VMEM] * 3 + [ANY] * 4,
        scratch_shapes=[
            pltpu.VMEM((depth * SEG, 6 * SEG), jnp.float32),
            pltpu.VMEM((depth * SEG, 6 * SEG), jnp.bfloat16),
            pltpu.SemaphoreType.DMA((2, TREE_DEVS - 1)),
            pltpu.SemaphoreType.DMA,
            pltpu.SemaphoreType.DMA,
        ]
        + line_sems(shards, 3)
        + rep_sems(shards, 3)
        + rep_sems(1, 1),
        cost_estimate=work(2e10, 7e8),
        compiler_params=pltpu.CompilerParams(
            collective_id=2, has_side_effects=True, vmem_limit_bytes=48 * 2**20
        ),
    )(slots, bias, q, kv, gate_up, down, out, cotangent, early)


def share_kernel(chunks, rows_ref, gate_ref, rows_all, gate_all, own_sems, cross, core, relay):
    rep = lax.axis_index("rep")
    greet(rep_neighbours())
    size = rows_ref.shape[0] // chunks

    def piece(n, part, block):
        return gate_all.at[part] if n == chunks else rows_all.at[part, pl.ds(n * size, size)]

    spread = RepSpread(tuple(range(chunks + 1)), piece, cross, core, relay)
    spread.sources = [rows_ref.at[pl.ds(n * size, size)] for n in range(chunks)] + [gate_ref]
    spread.arrived(None, 0, 0)
    for n in range(chunks + 1):
        spread.sends.local(spread.sources[n], piece(n, rep, 0), own_sems.at[n])
    spread.end()


def share_rows(rows, gates, reps):
    chunks = 4
    return pl.pallas_call(
        functools.partial(share_kernel, chunks),
        out_shape=[
            jax.ShapeDtypeStruct((reps,) + rows.shape, rows.dtype),
            jax.ShapeDtypeStruct((reps,) + gates.shape, gates.dtype),
        ],
        in_specs=[VMEM] * 2,
        out_specs=[VMEM] * 2,
        scratch_shapes=[pltpu.SemaphoreType.DMA((chunks + 1,))] + rep_sems(1, chunks + 1),
        cost_estimate=work(0, 1.6e8),
        compiler_params=pltpu.CompilerParams(
            collective_id=6, has_side_effects=True, vmem_limit_bytes=32 * 2**20
        ),
    )(rows, gates)


def join_kernel(part, total, near_buf, cross_out, cross_buf, near_sems, cross_sems):
    rep = lax.axis_index("rep")
    near = rep + 1 - 2 * (rep % 2)
    far = lax.rem(rep + 2, 4)
    diagonal = lax.rem(near + 2, 4)
    greet(rep_neighbours())
    sends = Sends()
    chunks = near_sems.shape[2]
    size = total.shape[0] // chunks
    for slot, owner in ((1, diagonal), (0, near)):
        for c in range(chunks):
            rows = pl.ds(c * size, size)
            sends.start(
                None,
                part.at[owner, rows],
                near_buf.at[slot, rows],
                near_sems.at[0, slot, c],
                near_sems.at[1, slot, c],
                {"rep": near},
            )

    def got(slot, c):
        here = near_buf.at[slot, pl.ds(c * size, size)]
        received(None, here, near_sems.at[0, slot, c], near_sems.at[1, slot, c], {"rep": near})

    step = 32 if size % 32 == 0 else size
    for c in range(chunks):
        got(1, c)

        def first(i, carry, c=c):
            rows = pl.ds(pl.multiple_of(c * size + i * step, step), step)
            value = part[far, rows].astype(jnp.float32) + near_buf[1, rows].astype(jnp.float32)
            cross_out[rows] = value.astype(cross_out.dtype)
            return carry

        lax.fori_loop(0, size // step, first, 0)
        rows = pl.ds(c * size, size)
        sends.start(
            None, cross_out.at[rows], cross_buf.at[rows], cross_sems.at[0, c], cross_sems.at[1, c], {"rep": far}
        )
    for c in range(chunks):
        got(0, c)
        here = cross_buf.at[pl.ds(c * size, size)]
        received(None, here, cross_sems.at[0, c], cross_sems.at[1, c], {"rep": far})

        def second(i, carry, c=c):
            rows = pl.ds(pl.multiple_of(c * size + i * step, step), step)
            value = part[rep, rows].astype(jnp.float32) + near_buf[0, rows].astype(jnp.float32)
            total[rows] = value + cross_buf[rows].astype(jnp.float32)
            return carry

        lax.fori_loop(0, size // step, second, 0)
    sends.drain()


def join_reps(part):
    block = part.shape[1:]
    chunks = 4
    return pl.pallas_call(
        join_kernel,
        out_shape=jax.ShapeDtypeStruct(block, jnp.float32),
        in_specs=[VMEM],
        out_specs=VMEM,
        scratch_shapes=[
            pltpu.VMEM((2,) + block, jnp.bfloat16),
            pltpu.VMEM(block, jnp.bfloat16),
            pltpu.VMEM(block, jnp.bfloat16),
            pltpu.SemaphoreType.DMA((2, 2, chunks)),
            pltpu.SemaphoreType.DMA((2, chunks)),
        ],
        cost_estimate=work(0, 1.6e8),
        compiler_params=pltpu.CompilerParams(
            collective_id=5, has_side_effects=True, vmem_limit_bytes=40 * 2**20
        ),
    )(part)


class LineScatter:
    def __init__(self, shards, arrays, local, pair_buf, line_buf, temp, stages, outs, pair, line, loads, ready=None):
        self.shards, self.arrays, self.local = shards, arrays, local
        self.pair_buf, self.line_buf, self.temp = pair_buf, line_buf, temp
        self.stages, self.outs = stages, outs
        self.pair, self.line, self.loads = pair, line, loads
        self.ready = ready or (lambda block: None)
        self.sends = Sends()
        self.me, self.spot, self.length = line_place(shards)
        self.side = self.me % 2
        self.twin = self.me + 1 - 2 * self.side

    def add(self, n, sources, target):
        stage, out = self.stages[n], self.outs[n]
        copies = []
        for k, (cond, ref) in enumerate(sources):
            copy = pltpu.make_async_copy(ref, stage.at[k], self.loads.at[k])
            copies.append((cond, copy))
            when(cond, copy.start)
        outer, rows, width = out.shape
        chunk = 32 if rows % 32 == 0 else rows
        pieces = rows // chunk

        def clear(k):
            def one(i, c):
                row = pl.multiple_of(i % pieces * chunk, chunk)
                stage[k, i // pieces, pl.ds(row, chunk)] = jnp.zeros((chunk, width), stage.dtype)
                return c

            lax.fori_loop(0, outer * pieces, one, 0)

        for k, (cond, copy) in enumerate(copies):
            when(cond, copy.wait)
            if cond is not None:
                pl.when(jnp.logical_not(cond))(functools.partial(clear, k))

        def one(i, c):
            row = pl.multiple_of(i % pieces * chunk, chunk)
            total = stage[0, i // pieces, pl.ds(row, chunk)].astype(jnp.float32)
            for k in range(1, len(sources)):
                total = total + stage[k, i // pieces, pl.ds(row, chunk)].astype(jnp.float32)
            out[i // pieces, pl.ds(row, chunk)] = total.astype(out.dtype)
            return c

        lax.fori_loop(0, outer * pieces, one, 0)
        store = pltpu.make_async_copy(out, target, self.loads.at[self.loads.shape[0] - 1])
        store.start()
        store.wait()

    def pick(self, turn):
        spot, last = self.spot, self.length - 1
        low = jnp.where(turn < last - spot, last - turn, turn - last + spot)
        high = jnp.where(turn < spot, turn, last - turn + spot)
        return jnp.where(turn == last, spot, jnp.where(2 * spot < self.length, low, high))

    def offer(self, turn):
        if turn >= self.length:
            return
        target = self.pick(turn)
        block = 2 * target + 1 - self.side
        self.ready(block)
        for n in range(self.arrays):
            sources = self.local(n, block)
            src = sources[0]
            if len(sources) > 1:
                src = self.temp[n].at[target]
                self.add(n, [(None, ref) for ref in sources], src)
            self.sends.start(
                None,
                src,
                self.pair_buf[n].at[target],
                self.pair.at[0, target, n],
                self.pair.at[1, target, n],
                {"shard": self.twin},
            )

    def got_pair(self, target, n):
        received(
            None,
            self.pair_buf[n].at[target],
            self.pair.at[0, target, n],
            self.pair.at[1, target, n],
            {"shard": self.twin},
        )

    def got_line(self, cond, slot, n, device):
        received(cond, self.line_buf[n].at[slot], self.line.at[0, slot, n], self.line.at[1, slot, n], {"shard": device})

    def step(self, slot):
        below, above = self.spot > 0, self.spot + 1 < self.length
        mirrored = self.length - 1 - self.spot
        turns = (
            (self.spot <= slot, self.length - 1 - slot + self.spot, True, below, self.me - 2, self.me + 2),
            (mirrored <= slot, slot - mirrored, False, above, self.me + 2, self.me - 2),
        )
        for cond, target, rising, has, source, device in turns:
            block = 2 * target + self.side
            place = target if rising else jnp.where(self.spot == target + 1, self.length, target)
            for n in range(self.arrays):
                copy = pltpu.make_async_remote_copy(
                    src_ref=self.pair_buf[n].at[target],
                    dst_ref=self.line_buf[n].at[place],
                    send_sem=self.line.at[0, place, n],
                    recv_sem=self.line.at[1, place, n],
                    device_id={"shard": device},
                    device_id_type=MESH,
                )

                def body(n=n, copy=copy, target=target, has=has, source=source, block=block):
                    self.got_pair(target, n)
                    self.got_line(has, target, n, source)
                    if n == 0:
                        self.ready(block)
                    sources = [(None, ref) for ref in self.local(n, block)]
                    sources += [(None, self.pair_buf[n].at[target]), (has, self.line_buf[n].at[target])]
                    self.add(n, sources, self.pair_buf[n].at[target])
                    copy.start()

                pl.when(cond)(body)
                self.sends.open.append((cond, copy.wait_send))

    def finish(self, targets):
        below, above = self.spot > 0, self.spot + 1 < self.length
        self.ready(self.me)
        for n in range(self.arrays):
            self.got_pair(self.spot, n)
            self.got_line(below, self.spot, n, self.me - 2)
            self.got_line(above, self.length, n, self.me + 2)
            sources = [(None, ref) for ref in self.local(n, self.me)]
            sources += [
                (None, self.pair_buf[n].at[self.spot]),
                (below, self.line_buf[n].at[self.spot]),
                (above, self.line_buf[n].at[self.length]),
            ]
            self.add(n, sources, targets[n])


def scatter_sems(shards, arrays, loads):
    length = shards // 2
    return [
        pltpu.SemaphoreType.DMA((2, length, arrays)),
        pltpu.SemaphoreType.DMA((2, length + 1, arrays)),
        pltpu.SemaphoreType.DMA((loads + 1,)),
    ]


def scatter_buffers(shards, block):
    length = shards // 2
    return [
        jax.ShapeDtypeStruct((length,) + block, jnp.bfloat16),
        jax.ShapeDtypeStruct((length + 1,) + block, jnp.bfloat16),
    ]


def back_kernel(
    depth,
    shards,
    slots,
    bias,
    inv,
    q_ref,
    kv_ref,
    o_ref,
    do_ref,
    lse_ref,
    gu_ref,
    dn_ref,
    dq_ref,
    dkv_ref,
    gu_out,
    dn_out,
    gu_pair,
    gu_line,
    dn_pair,
    dn_line,
    path,
    p_scr,
    d_scr,
    group,
    guest,
    passing,
    landed,
    gu_stage,
    dn_stage,
    gu_sum,
    dn_sum,
    kv_sems,
    pair,
    line,
    loads,
):
    me = lax.axis_index("shard")
    member = me % TREE_DEVS
    segs = q_ref.shape[0] // SEG
    twin = me + 1 - 2 * (member % 2)
    across = me + 2 - 4 * (member // 2)
    greet(line_neighbours(shards) + [(None, {"shard": across})])
    scatter = LineScatter(
        shards,
        2,
        lambda n, block: [(gu_ref, dn_ref)[n].at[:, block]],
        (gu_pair, dn_pair),
        (gu_line, dn_line),
        None,
        (gu_stage, dn_stage),
        (gu_sum, dn_sum),
        pair,
        line,
        loads,
    )
    scatter.offer(0)
    path[:, depth] = jnp.zeros((segs,) + path.shape[2:], path.dtype)
    step = functools.partial(
        bwd_step, depth, slots, bias, q_ref, kv_ref, o_ref, do_ref, lse_ref, dq_ref, path, p_scr, d_scr
    )
    count = segs * PAIRS
    cuts = (0, count * 8 // 20, count * 14 // 20, count)
    scatter.offer(1)
    lax.fori_loop(cuts[0], cuts[1], step, 0)
    scatter.step(0)
    scatter.offer(2)
    lax.fori_loop(cuts[1], cuts[2], step, 0)
    if scatter.length > 2:
        scatter.step(1)
    scatter.offer(3)
    lax.fori_loop(cuts[2], cuts[3], step, 0)
    lax.fori_loop(0, group.shape[0], functools.partial(bwd_collect, inv, path, group), 0)
    sends = Sends()
    side = member % 2
    for turn, slot in ((0, 1 - side), (1, side)):
        owner = (across - side + slot) % TREE_DEVS
        sends.start(
            None,
            group.at[pl.ds(owner * segs, segs)],
            guest.at[slot],
            kv_sems.at[0, turn],
            kv_sems.at[1, turn],
            {"shard": across},
        )

    def join(mine, slot, extra, target):
        def one(seg, c):
            for col in range(0, 2 * KVH * HD, 256):
                total = group[mine * segs + seg, :, col : col + 256].astype(jnp.float32)
                total = total + guest[slot, seg, :, col : col + 256].astype(jnp.float32)
                if extra is not None:
                    total = total + extra[seg, :, col : col + 256].astype(jnp.float32)
                target[seg, :, col : col + 256] = total.astype(target.dtype)
            return c

        lax.fori_loop(0, segs, one, 0)

    received(None, guest.at[1 - side], kv_sems.at[0, 0], kv_sems.at[1, 0], {"shard": across})
    join(twin % TREE_DEVS, 1 - side, None, passing)
    sends.start(None, passing, landed, kv_sems.at[0, 2], kv_sems.at[1, 2], {"shard": twin})
    for turn in range(2, scatter.length - 1):
        scatter.offer(turn + 2)
        scatter.step(turn)
    received(None, guest.at[side], kv_sems.at[0, 1], kv_sems.at[1, 1], {"shard": across})
    received(None, landed, kv_sems.at[0, 2], kv_sems.at[1, 2], {"shard": twin})
    join(member, side, landed, dkv_ref)
    scatter.finish((gu_out, dn_out))
    sends.drain()
    scatter.sends.drain()


def attend_back(slots, bias, inv, q, kv, o, do, lse, gate_up_grad, down_grad, depth, shards):
    segs = q.shape[0] // SEG
    own_kv = (segs,) + kv.shape[1:]
    gu_block = (gate_up_grad.shape[0],) + gate_up_grad.shape[2:]
    dn_block = (down_grad.shape[0],) + down_grad.shape[2:]
    outs = [
        jax.ShapeDtypeStruct(q.shape, jnp.bfloat16),
        jax.ShapeDtypeStruct(own_kv, jnp.bfloat16),
        jax.ShapeDtypeStruct(gu_block, jnp.bfloat16),
        jax.ShapeDtypeStruct(dn_block, jnp.bfloat16),
    ]
    outs += scatter_buffers(shards, gu_block) + scatter_buffers(shards, dn_block)
    return pl.pallas_call(
        functools.partial(back_kernel, depth, shards),
        out_shape=outs,
        in_specs=[SMEM] * 3 + [VMEM] * 5 + [ANY] * 2,
        out_specs=[VMEM] * 2 + [ANY] * 6,
        scratch_shapes=[
            pltpu.VMEM((segs, depth + 1, SEG, 2 * KVH * HD), jnp.bfloat16),
            pltpu.VMEM((depth * SEG, 6 * SEG), jnp.bfloat16),
            pltpu.VMEM((depth * SEG, 6 * SEG), jnp.bfloat16),
            pltpu.VMEM(kv.shape, jnp.bfloat16),
            pltpu.VMEM((2,) + own_kv, jnp.bfloat16),
            pltpu.VMEM(own_kv, jnp.bfloat16),
            pltpu.VMEM(own_kv, jnp.bfloat16),
            pltpu.VMEM((4,) + gu_block, jnp.bfloat16),
            pltpu.VMEM((4,) + dn_block, jnp.bfloat16),
            pltpu.VMEM(gu_block, jnp.bfloat16),
            pltpu.VMEM(dn_block, jnp.bfloat16),
            pltpu.SemaphoreType.DMA((2, TREE_DEVS - 1)),
        ]
        + scatter_sems(shards, 2, 4),
        cost_estimate=work(5e10, 7e8),
        compiler_params=pltpu.CompilerParams(
            collective_id=3, has_side_effects=True, vmem_limit_bytes=60 * 2**20
        ),
    )(slots, bias, inv, q, kv, o, do, lse, gate_up_grad, down_grad)[:4]


def finish_kernel(shards, arrays, pieces, *refs):
    refs = list(refs)

    def take(count):
        taken = refs[:count]
        del refs[:count]
        return taken

    grads = take(arrays)
    shares = take(pieces)
    outs = take(arrays)
    expert_outs = take(2)
    core_bufs = take(arrays)
    share_bufs = take(arrays)
    cross_bufs = take(arrays)
    temps = take(arrays)
    pair_bufs = take(arrays)
    line_bufs = take(arrays)
    stages = take(arrays)
    totals = take(arrays)
    core_sems, swap_sems, own_sems, cross, core, relay, pair, line, loads = refs
    rep = lax.axis_index("rep")
    near = rep + 1 - 2 * (rep % 2)
    far = lax.rem(rep + 2, 4)
    half = rep % 2
    greet(line_neighbours(shards) + rep_neighbours())
    sends = Sends()
    length = shards // 2
    side = lax.axis_index("shard") % 2

    def columns(n, ref, which):
        width = totals[n].shape[-1]
        if width == ref.shape[-1]:
            return ref
        return ref.at[:, :, pl.ds(pl.multiple_of(which * width, LANES), width)]

    experts = pieces // 2
    size = shares[0].shape[0]

    def place(n, part, block):
        return expert_outs[n // experts].at[part, pl.ds(n % experts * size, size)]

    for n in range(pieces):
        sends.local(shares[n], place(n, rep, 0), own_sems.at[n])
    spread = RepSpread(tuple(range(pieces)), place, cross, core, relay)
    spread.sources = shares
    spread.arrived(None, 0, 0)

    def ready(block):
        for n in range(arrays):
            received(
                None, core_bufs[n].at[block], core_sems.at[0, block, n], core_sems.at[1, block, n], {"rep": near}
            )

    scatter = LineScatter(
        shards,
        arrays,
        lambda n, block: [columns(n, grads[n].at[block], half), core_bufs[n].at[block]],
        pair_bufs,
        line_bufs,
        temps,
        stages,
        totals,
        pair,
        line,
        loads,
        ready,
    )
    for turn in range(length):
        for which in (1 - side, side):
            block = 2 * scatter.pick(turn) + which
            for n in range(arrays):
                sends.start(
                    None,
                    columns(n, grads[n].at[block], 1 - half),
                    core_bufs[n].at[block],
                    core_sems.at[0, block, n],
                    core_sems.at[1, block, n],
                    {"rep": near},
                )
    scatter.offer(0)
    scatter.offer(1)
    for turn in range(scatter.length - 1):
        scatter.offer(turn + 2)
        scatter.step(turn)
    scatter.finish(share_bufs)
    for n in range(arrays):
        sends.start(
            None, share_bufs[n], cross_bufs[n], swap_sems.at[0, 0, n], swap_sems.at[1, 0, n], {"rep": far}
        )
    spread.end()
    for n in range(arrays):
        received(None, cross_bufs[n], swap_sems.at[0, 0, n], swap_sems.at[1, 0, n], {"rep": far})
        mine = columns(n, outs[n], half)
        scatter.add(n, [(None, share_bufs[n]), (None, cross_bufs[n])], mine)
        if outs[n].shape != totals[n].shape:
            sends.start(None, mine, mine, swap_sems.at[0, 1, n], swap_sems.at[1, 1, n], {"rep": near})
    for n in range(arrays):
        if outs[n].shape != totals[n].shape:
            theirs = columns(n, outs[n], 1 - half)
            received(None, theirs, swap_sems.at[0, 1, n], swap_sems.at[1, 1, n], {"rep": near})
    sends.drain()
    scatter.sends.drain()


def finish_grads(grads, halved, gate_up_shares, down_shares, reps):
    shards = grads[0].shape[0]
    arrays = len(grads)
    parts = len(gate_up_shares)
    wholes = [grad.shape[1:] for grad in grads]
    blocks = [
        whole[:-1] + (whole[-1] // 2 if halve else whole[-1],) for whole, halve in zip(wholes, halved)
    ]
    experts = parts * gate_up_shares[0].shape[0]
    shapes = list(wholes)
    shapes += [(reps, experts) + gate_up_shares[0].shape[1:], (reps, experts) + down_shares[0].shape[1:]]
    shapes += [(shards,) + block for block in blocks]
    shapes += blocks + blocks
    shapes += [(shards // 2,) + block for block in blocks]
    shapes += [(shards // 2,) + block for block in blocks]
    shapes += [(shards // 2 + 1,) + block for block in blocks]
    return pl.pallas_call(
        functools.partial(finish_kernel, shards, arrays, 2 * parts),
        out_shape=[jax.ShapeDtypeStruct(shape, jnp.bfloat16) for shape in shapes],
        in_specs=[ANY] * (arrays + 2 * parts),
        out_specs=[ANY] * len(shapes),
        scratch_shapes=[pltpu.VMEM((5,) + block, jnp.bfloat16) for block in blocks]
        + [pltpu.VMEM(block, jnp.bfloat16) for block in blocks]
        + [
            pltpu.SemaphoreType.DMA((2, shards, arrays)),
            pltpu.SemaphoreType.DMA((2, 2, arrays)),
            pltpu.SemaphoreType.DMA((2 * parts,)),
        ]
        + rep_sems(1, 2 * parts)
        + scatter_sems(shards, arrays, 5),
        cost_estimate=work(0, 4e8),
        compiler_params=pltpu.CompilerParams(
            collective_id=4, has_side_effects=True, vmem_limit_bytes=32 * 2**20
        ),
    )(*grads, *gate_up_shares, *down_shares)[: arrays + 2]


def norm_rows(values, gain):
    scale_rows = lax.rsqrt(jnp.mean(values * values, axis=-1, keepdims=True) + EPS)
    return (values * scale_rows * gain, scale_rows)


def norm_back(values, scale_rows, gain, upstream):
    scaled = upstream * gain
    inner = jnp.mean(scaled * values, axis=-1, keepdims=True)
    through = scale_rows * scaled - values * (scale_rows * scale_rows * scale_rows) * inner
    gain_grad = jnp.sum(upstream * values * scale_rows, axis=0)
    return (through, gain_grad)


def table_lookup(table, index):
    positions = jnp.arange(table.shape[0], dtype=jnp.int32)
    return jnp.sum(jnp.where(index[:, None] == positions[None, :], table[None, :], 0), axis=1)


def find_slot(group_ids, wanted):
    positions = jnp.arange(group_ids.shape[0], dtype=jnp.int32)
    return jnp.sum(jnp.where(group_ids[None, :] == wanted[:, None], positions[None, :], 0), axis=1)


def ancestor_slots(local_ids, group_ids, group_parents, depth):
    flat_parents = group_parents.reshape(-1)
    tree_index = local_ids // TREE_SEGS
    current = local_ids % TREE_SEGS
    alive = jnp.ones(local_ids.shape, dtype=bool)
    slot_list = []
    alive_list = []
    for level in range(depth):
        wanted = tree_index * TREE_SEGS + current
        slot_list.append(find_slot(group_ids, wanted))
        alive_list.append(alive)
        parent_seg = table_lookup(flat_parents, wanted)
        alive = alive & (parent_seg != current)
        current = parent_seg
    return (jnp.stack(slot_list, axis=1), jnp.stack(alive_list, axis=1))


def path_levels(path_slots, path_alive, slot_count):
    depth = path_slots.shape[1]
    slots = jnp.arange(slot_count, dtype=jnp.int32)
    hit = path_alive[None] & (path_slots[None] == slots[:, None, None])
    levels = jnp.arange(depth, dtype=jnp.int32)
    return depth - jnp.sum(jnp.where(hit, depth - levels, 0), axis=2)


def row_pieces(grad, shards):
    experts, rows, width = grad.shape
    return grad.astype(jnp.bfloat16).reshape(experts, shards, rows // shards, width).transpose(1, 0, 2, 3)


def expert_forward(rows, gates, w_gate_up, w_down, upstream):
    gate_up = jnp.einsum("td,edf->etf", rows, w_gate_up, preferred_element_type=jnp.bfloat16)
    gate_part = gate_up[..., :FF].astype(jnp.float32)
    up_part = gate_up[..., FF:].astype(jnp.float32)
    sig_gate = jax.nn.sigmoid(gate_part)
    hidden = gate_part * sig_gate * up_part
    gated = (hidden * gates).astype(jnp.bfloat16)
    mix_part = jnp.einsum("etf,efd->td", gated, w_down, preferred_element_type=jnp.float32)
    raw_grad = jnp.einsum("td,efd->etf", upstream, w_down, preferred_element_type=jnp.float32)
    gate_grad = jnp.sum(hidden * raw_grad, axis=-1)
    hidden_grad = raw_grad * gates
    gate_grad_part = hidden_grad * up_part * sig_gate * (1.0 + gate_part * (1.0 - sig_gate))
    up_grad_part = hidden_grad * gate_part * sig_gate
    row_grads = jnp.concatenate([gate_grad_part, up_grad_part], axis=-1).astype(jnp.bfloat16)
    down_grad = jnp.einsum("etf,td->efd", gated, upstream, preferred_element_type=jnp.float32)
    gate_up_grad = jnp.einsum("td,etf->edf", rows, row_grads, preferred_element_type=jnp.float32)
    gate_up_grad = with_layout_constraint(gate_up_grad.astype(jnp.bfloat16), Layout((0, 1, 2)))
    act_part = jnp.einsum("etf,edf->td", row_grads, w_gate_up, preferred_element_type=jnp.float32)
    return (mix_part, gate_grad, act_part, gate_up_grad, down_grad)


def shards(
    tokens,
    norm_gains,
    qkv_weight,
    out_weight,
    router_weight,
    gate_up_weight,
    down_weight,
    routes,
    placement,
    parents,
    cotangent,
):
    shard_index = lax.axis_index("shard")
    rep_index = lax.axis_index("rep")
    shard_count = lax.axis_size("shard")
    token_count = tokens.shape[0]
    seg_dev = token_count // SEG
    depth = TRUNK + 2
    width_q = H * HD
    width_kv = KVH * HD
    group_size = TREE_DEVS * seg_dev
    tree_count = group_size // TREE_SEGS
    member = shard_index % TREE_DEVS
    group = (rep_index * shard_count + shard_index) // TREE_DEVS
    group_ids = lax.dynamic_slice_in_dim(placement, group * group_size, group_size)
    group_parents = lax.dynamic_slice_in_dim(parents, group * tree_count, tree_count)
    local_ids = lax.dynamic_slice_in_dim(group_ids, member * seg_dev, seg_dev)
    path_slots, path_alive = ancestor_slots(local_ids, group_ids, group_parents, depth)
    rep_count = lax.axis_size("rep")
    own_experts = E // rep_count
    first_expert = rep_index * own_experts
    half = own_experts // 2
    padding = jnp.zeros((norm_gains.shape[1], LANES - E - 2), jnp.bfloat16)
    small = jnp.concatenate([router_weight, norm_gains.T, padding], axis=1)
    w_qkv, small = gather_weights(qkv_weight, small, shard_count)
    w_qkv = w_qkv.reshape(D, -1)
    small = small.reshape(D, LANES)
    w_router = small[:, :E]
    gains = small[:, E : E + 2].T
    gain_first = gains[0].astype(jnp.float32)
    gain_second = gains[1].astype(jnp.float32)
    token_values = tokens.astype(jnp.float32)
    normed_first, scale_first = norm_rows(token_values, gain_first)
    act_first = normed_first.astype(jnp.bfloat16)
    projected = jnp.dot(act_first, w_qkv, preferred_element_type=jnp.float32)
    queries = projected[:, :width_q].astype(jnp.bfloat16)
    w_gate_up_early = lax.all_gather(
        lax.dynamic_slice_in_dim(gate_up_weight, first_expert, half - 1), "shard", axis=1, tiled=True
    )
    own_kv = projected[:, width_q:].astype(jnp.bfloat16).reshape(seg_dev, SEG, 2 * width_kv)
    bias = jnp.where(path_alive, 0.0, NEG).astype(jnp.float32)
    attended, log_totals, group_kv, w_gate_up, w_down, w_out, cot_all = attend_gather(
        path_slots,
        bias,
        queries,
        own_kv,
        gate_up_weight,
        down_weight,
        out_weight,
        cotangent,
        w_gate_up_early.reshape(half - 1, shard_count, -1, 2 * FF),
        depth,
        shard_count,
        rep_count,
        1,
    )
    gate_up_late, down_late, attended = lax.optimization_barrier(
        (
            lax.dynamic_slice_in_dim(gate_up_weight, first_expert + half, half),
            lax.dynamic_slice_in_dim(down_weight, first_expert + half, half),
            attended,
        )
    )
    w_gate_up_late = lax.all_gather(gate_up_late, "shard", axis=1, tiled=True)
    w_down_late = lax.all_gather(down_late, "shard", axis=1, tiled=True)
    w_gate_up = w_gate_up.reshape(half, D, -1)
    w_down = w_down.reshape(half, FF, D)
    w_out = w_out.reshape(H * HD, D)
    cot_all = cot_all.reshape(-1, D)
    residual = token_values + jnp.dot(attended, w_out, preferred_element_type=jnp.float32)
    normed_second, scale_second = norm_rows(residual, gain_second)
    act_second = normed_second.astype(jnp.bfloat16)
    logits = jnp.dot(act_second, w_router, preferred_element_type=jnp.float32)
    expert_ids = jnp.arange(E, dtype=jnp.int32)
    picks = routes[:, :, None] == expert_ids[None, None, :]
    chosen = jnp.sum(jnp.where(picks, logits[:, None, :], 0.0), axis=-1)
    gates = jax.nn.softmax(chosen, axis=-1)
    upstream = cotangent.astype(jnp.float32)
    gate_table = jnp.sum(jnp.where(picks, gates[:, :, None], 0.0), axis=1)
    act_all, gate_all = share_rows(act_second, gate_table.T, rep_count)
    act_all = act_all.reshape(-1, D)
    own_gate = lax.dynamic_slice_in_dim(gate_all, first_expert, own_experts, axis=1)
    own_gate = own_gate.transpose(1, 0, 2).reshape(own_experts, -1, 1)
    first_half = expert_forward(act_all, own_gate[:half], w_gate_up, w_down, cot_all)
    first_half = (
        first_half[0].astype(jnp.bfloat16),
        first_half[1],
        first_half[2].astype(jnp.bfloat16),
        row_pieces(first_half[3], shard_count),
        row_pieces(first_half[4], shard_count),
    )
    first_half, w_gate_up_late, w_down_late = lax.optimization_barrier(
        (first_half, w_gate_up_late, w_down_late)
    )
    second_half = expert_forward(act_all, own_gate[half:], w_gate_up_late, w_down_late, cot_all)
    mix_part = first_half[0].astype(jnp.float32) + second_half[0]
    gate_grad_own = jnp.concatenate([first_half[1], second_half[1]], axis=0)
    gate_up_early = lax.psum_scatter(first_half[3], "shard", scatter_dimension=0, tiled=False)
    down_early = lax.psum_scatter(first_half[4], "shard", scatter_dimension=0, tiled=False)
    down_grad = second_half[4]
    gate_up_grad = second_half[3]
    gate_grad_all = lax.all_gather(gate_grad_own, "rep", axis=0, tiled=True)
    gate_grad_table = lax.dynamic_slice_in_dim(
        gate_grad_all, rep_index * token_count, token_count, axis=1
    ).T
    inner_gate = jnp.sum(gate_table * gate_grad_table, axis=-1, keepdims=True)
    logit_grad = gate_table * (gate_grad_table - inner_gate)
    router_grad = jnp.dot(
        act_second.astype(jnp.float32).T,
        logit_grad,
        precision=lax.Precision.HIGHEST,
        preferred_element_type=jnp.float32,
    )
    act_part = (first_half[2].astype(jnp.float32) + second_half[2]).astype(jnp.bfloat16)
    act_second_grad = join_reps(act_part.reshape(rep_count, token_count, D))
    act_second_grad = act_second_grad + jnp.dot(
        logit_grad,
        w_router.astype(jnp.float32).T,
        precision=lax.Precision.HIGHEST,
        preferred_element_type=jnp.float32,
    )
    through_second, gain_grad_second = norm_back(
        residual, scale_second, gains[1].astype(jnp.float32), act_second_grad
    )
    residual_grad = upstream + through_second
    branch_grad = residual_grad.astype(jnp.bfloat16)
    out_grad = jnp.dot(attended.T, branch_grad, preferred_element_type=jnp.float32)
    attended_grad = lax.dot_general(
        branch_grad, w_out, (((1,), (1,)), ((), ())), preferred_element_type=jnp.float32
    ).astype(jnp.bfloat16)
    attended_grad, gate_up_early, down_early = lax.optimization_barrier(
        (attended_grad, gate_up_early, down_early)
    )
    query_grad, own_grad, gate_up_share, down_share = attend_back(
        path_slots,
        bias,
        path_levels(path_slots, path_alive, group_size),
        queries,
        group_kv,
        attended,
        attended_grad,
        log_totals,
        gate_up_grad.astype(jnp.bfloat16).reshape(half, shard_count, -1, 2 * FF),
        down_grad.astype(jnp.bfloat16).reshape(half, shard_count, -1, D),
        depth,
        shard_count,
    )
    mix_part, query_grad = lax.optimization_barrier((mix_part.astype(jnp.bfloat16), query_grad))
    mixture = lax.psum_scatter(mix_part, "rep", scatter_dimension=0, tiled=True)
    block_out = (residual + mixture.astype(jnp.float32)).astype(jnp.bfloat16)
    projected_grad = jnp.concatenate(
        [query_grad, own_grad.reshape(token_count, 2 * width_kv)], axis=1
    )
    qkv_grad = jnp.dot(act_first.T, projected_grad, preferred_element_type=jnp.float32)
    act_first_grad = lax.dot_general(
        projected_grad, w_qkv, (((1,), (1,)), ((), ())), preferred_element_type=jnp.float32
    )
    through_first, gain_grad_first = norm_back(
        token_values, scale_first, gains[0].astype(jnp.float32), act_first_grad
    )
    token_grad = residual_grad + through_first
    small_grad = jnp.concatenate(
        [
            gain_grad_first[:, None],
            gain_grad_second[:, None],
            router_grad,
            jnp.zeros((D, LANES - E - 2), jnp.float32),
        ],
        axis=1,
    )
    grads = [
        grad.astype(jnp.bfloat16).reshape(shard_count, 1, D // shard_count, -1)
        for grad in (qkv_grad, out_grad, small_grad)
    ]
    qkv_grad, out_grad, small_grad, gate_up_grad, down_grad = finish_grads(
        grads, (True, True, False), (gate_up_early, gate_up_share), (down_early, down_share), rep_count
    )
    small_grad = small_grad[0].astype(jnp.float32)
    return (
        block_out,
        token_grad,
        small_grad[:, :2].T,
        qkv_grad[0].astype(jnp.float32),
        out_grad[0].astype(jnp.float32),
        small_grad[:, 2 : 2 + E],
        gate_up_grad.reshape((E,) + gate_up_grad.shape[2:]).astype(jnp.float32),
        down_grad.reshape((E,) + down_grad.shape[2:]).astype(jnp.float32),
    )


def solution(mesh):
    in_specs = (
        P(("rep", "shard"), None),
        P(None, "shard"),
        P("shard", None),
        P("shard", None),
        P("shard", None),
        P(None, "shard", None),
        P(None, "shard", None),
        P(("rep", "shard"), None),
        P(),
        P(),
        P(("rep", "shard"), None),
    )
    out_specs = (
        P(("rep", "shard"), None),
        P(("rep", "shard"), None),
        P(None, "shard"),
        P("shard", None),
        P("shard", None),
        P("shard", None),
        P(None, "shard", None),
        P(None, "shard", None),
    )
    return jax.shard_map(shards, mesh=mesh, in_specs=in_specs, out_specs=out_specs, check_vma=False)
```

```python
import functools

import jax
import jax.experimental.pallas as pl
import jax.experimental.pallas.tpu as pltpu
import jax.numpy as jnp
from jax import lax
from jax.experimental.layout import Layout, with_layout_constraint
from jax.sharding import PartitionSpec as P

D = 1536
H = 24
KVH = 8
HD = 64
FF = 512
TOP = 8
E = 16
SEG = 128
TRUNK = 8
TREE_DEVS = 4
TREE_SEGS = 20
CAP = 352


EPS = 1e-06


PAIRS = KVH // 2
LANES = 2 * HD
NEG=-1e30
def low_half(): return lax.broadcasted_iota(jnp.int32,(SEG,LANES),1)<HD
def stack_heads(ref, row, pair, factor=None):
    low=low_half()
    t=[ref[pl.ds(row,SEG), pl.ds(pl.multiple_of((3*pair+i)*LANES,LANES),LANES)].astype(jnp.float32) for i in range(3)]
    if factor is not None: t=[x*factor for x in t]
    z=jnp.zeros_like(t[0])
    r0=pltpu.roll(t[0],HD,1); r2=pltpu.roll(t[2],HD,1)
    parts=[jnp.where(low,t[0],z),jnp.where(low,r0,z),jnp.where(low,t[1],z),
           jnp.where(low,z,t[1]),jnp.where(low,z,r2),jnp.where(low,z,t[2])]
    return jnp.concatenate(parts,axis=0)
def unstack_heads(rows):
    low=low_half()
    a=[rows[i*SEG:(i+1)*SEG] for i in range(6)]
    return [jnp.where(low,a[0],pltpu.roll(a[1],HD,1)), jnp.where(low,a[2],a[3]), jnp.where(low,pltpu.roll(a[4],HD,1),a[5])]
def kv_path(kv_ref, slots, seg, depth, col):
    return jnp.concatenate([kv_ref[slots[seg,lev],:,pl.ds(pl.multiple_of(col,LANES),LANES)] for lev in range(depth)],axis=0)
NT=(((1,),(1,)),((),())); NN=(((1,),(0,)),((),())); TN=(((0,),(0,)),((),()))
def dot(a,b,dims): return lax.dot_general(a,b,dims,preferred_element_type=jnp.float32)
def causal_bias(width):
    key=lax.broadcasted_iota(jnp.int32,(SEG,width),0); qry=lax.broadcasted_iota(jnp.int32,(SEG,width),1)%SEG
    return jnp.where(key<=qry,0.0,NEG)
def fwd_step(depth, slots, bias, q_ref, kv_ref, o_ref, lse_ref, s_scr, p_scr, i, c):
    width=6*SEG
    seg=i//PAIRS; pair=i%PAIRS
    row=pl.multiple_of(seg*SEG,SEG)
    q6=stack_heads(q_ref,row,pair,HD**-0.5).astype(jnp.bfloat16)
    top=jnp.full((8,width),NEG,jnp.float32)
    for lev in range(depth):
        k=kv_ref[slots[seg,lev],:,pl.ds(pl.multiple_of(pair*LANES,LANES),LANES)]
        s=dot(k,q6,NT)
        s=s+(causal_bias(width) if lev==0 else bias[seg,lev])
        s_scr[lev*SEG:(lev+1)*SEG,:]=s
        top=jnp.maximum(top,jnp.max(s.reshape(SEG//8,8,width),axis=0))
    top=jnp.max(top,axis=0,keepdims=True)
    tot=jnp.zeros((8,width),jnp.float32)
    acc=jnp.zeros((LANES,width),jnp.float32)
    for lev in range(depth):
        p=jnp.exp(s_scr[lev*SEG:(lev+1)*SEG,:]-top)
        tot=tot+jnp.sum(p.reshape(SEG//8,8,width),axis=0)
        p_scr[lev*SEG:(lev+1)*SEG,:]=p.astype(jnp.bfloat16)
    v=kv_path(kv_ref,slots,seg,depth,KVH*HD+pair*LANES)
    acc=dot(v,p_scr[...],TN)
    tot=jnp.sum(tot,axis=0,keepdims=True)
    lse_ref[i]=jnp.broadcast_to(top+jnp.log(tot),(8,width))
    o6=(acc/tot).T
    for j,t in enumerate(unstack_heads(o6)):
        o_ref[pl.ds(row,SEG),pl.ds(pl.multiple_of((3*pair+j)*LANES,LANES),LANES)]=t.astype(o_ref.dtype)
    return c
def bwd_step(depth, slots, bias, q_ref, kv_ref, o_ref, do_ref, lse_ref, dq_ref, path, p_scr, d_scr, i, c):
    width=6*SEG
    seg=i//PAIRS; pair=i%PAIRS
    row=pl.multiple_of(seg*SEG,SEG)
    q6=stack_heads(q_ref,row,pair,HD**-0.5).astype(jnp.bfloat16)
    do6f=stack_heads(do_ref,row,pair)
    do6=do6f.astype(jnp.bfloat16)
    prod=do6f*stack_heads(o_ref,row,pair)
    hi=prod.astype(jnp.bfloat16); lo=(prod-hi.astype(jnp.float32)).astype(jnp.bfloat16)
    ones=jnp.ones((8,LANES),jnp.bfloat16)
    delta=(dot(ones,hi,NT)+dot(ones,lo,NT))[:1]
    lse=lse_ref[i][:1]
    kcol=pl.multiple_of(pair*LANES,LANES); vcol=pl.multiple_of(KVH*HD+pair*LANES,LANES)
    for lev in range(depth):
        k=kv_ref[slots[seg,lev],:,pl.ds(kcol,LANES)]
        v=kv_ref[slots[seg,lev],:,pl.ds(vcol,LANES)]
        s=dot(k,q6,NT)
        s=s+(causal_bias(width) if lev==0 else bias[seg,lev])
        p=jnp.exp(s-lse)
        dp=dot(v,do6,NT)
        ds=(p*(dp-delta)).astype(jnp.bfloat16)
        p_scr[lev*SEG:(lev+1)*SEG,:]=p.astype(jnp.bfloat16)
        d_scr[lev*SEG:(lev+1)*SEG,:]=ds
    dv=dot(p_scr[...],do6,NN)
    dk=dot(d_scr[...],q6,NN)
    for lev in range(depth):
        path[seg,lev,:,pl.ds(kcol,LANES)]=dk[lev*SEG:(lev+1)*SEG].astype(path.dtype)
        path[seg,lev,:,pl.ds(vcol,LANES)]=dv[lev*SEG:(lev+1)*SEG].astype(path.dtype)
    k=kv_path(kv_ref,slots,seg,depth,pair*LANES)
    dq6=(dot(k,d_scr[...],TN)*(HD**-0.5)).T
    for j,t in enumerate(unstack_heads(dq6)):
        dq_ref[pl.ds(row,SEG),pl.ds(pl.multiple_of((3*pair+j)*LANES,LANES),LANES)]=t.astype(dq_ref.dtype)
    return c
def bwd_collect(inv, path, group, slot, c):
    for col in range(0,2*KVH*HD,256):
        tot=path[0,inv[slot,0],:,col:col+256].astype(jnp.float32)
        for seg in range(1,path.shape[0]): tot=tot+path[seg,inv[slot,seg],:,col:col+256].astype(jnp.float32)
        group[slot,:,col:col+256]=tot.astype(group.dtype)
    return c
MESH = pl.DeviceIdType.MESH
ANY = pl.BlockSpec(memory_space=pl.ANY)
VMEM = pl.BlockSpec(memory_space=pltpu.VMEM)
SMEM = pl.BlockSpec(memory_space=pltpu.SMEM)


def work(flops, moved):
    return pl.CostEstimate(flops=int(flops), bytes_accessed=int(moved), transcendentals=0)


class Sends:
    def __init__(self):
        self.open = []

    def start(self, cond, src, dst, send_sem, recv_sem, device):
        copy = pltpu.make_async_remote_copy(
            src_ref=src, dst_ref=dst, send_sem=send_sem, recv_sem=recv_sem, device_id=device, device_id_type=MESH
        )
        when(cond, copy.start)
        self.open.append((cond, copy.wait_send))

    def local(self, src, dst, sem):
        copy = pltpu.make_async_copy(src, dst, sem)
        copy.start()
        self.open.append((None, copy.wait))

    def drain(self):
        for cond, wait in self.open:
            when(cond, wait)
        self.open = []


def when(cond, body):
    if cond is None:
        body()
    else:
        pl.when(cond)(body)


def received(cond, region, send_sem, recv_sem, device):
    copy = pltpu.make_async_remote_copy(
        src_ref=region, dst_ref=region, send_sem=send_sem, recv_sem=recv_sem, device_id=device, device_id_type=MESH
    )
    when(cond, copy.wait_recv)


def line_place(shards):
    me = lax.axis_index("shard")
    return me, me // 2, shards // 2


def greet(devices):
    barrier = pltpu.get_barrier_semaphore()
    count = 0
    for cond, device in devices:
        when(
            cond,
            lambda device=device: pl.semaphore_signal(barrier, inc=1, device_id=device, device_id_type=MESH),
        )
        count = count + (1 if cond is None else cond.astype(jnp.int32))
    pl.semaphore_wait(barrier, count)


def line_neighbours(shards):
    me, spot, length = line_place(shards)
    return [
        (None, {"shard": me + 1 - 2 * (me % 2)}),
        (spot > 0, {"shard": me - 2}),
        (spot + 1 < length, {"shard": me + 2}),
    ]


class LineGather:
    def __init__(self, shards, sources, region, up, down, pair, local_sem, arrived=None, order=None):
        self.shards, self.sources, self.region = shards, sources, region
        self.up, self.down, self.pair, self.local_sem = up, down, pair, local_sem
        self.arrived = arrived or (lambda cond, block, index: None)
        self.order = order or tuple(range(len(sources)))
        self.sends = Sends()
        self.me, self.spot, self.length = line_place(shards)
        self.twin = self.me + 1 - 2 * (self.me % 2)

    def forward(self, cond, block, step, rising, falling, src=None):
        place = step if rising else self.length - 1 + step
        for n in self.order:
            here = self.region(n, block)
            out = here if src is None else src[n]
            ways = []
            if rising:
                ways.append((both(cond, self.spot + 1 < self.length), self.up, step + 1, self.me + 2))
            if falling:
                ways.append((both(cond, self.spot > 0), self.down, step + 1, self.me - 2))
            for where, sems, index, device in ways:
                if index < self.length:
                    self.sends.start(where, out, here, sems.at[0, index, n], sems.at[1, index, n], {"shard": device})
            self.sends.start(
                cond, out, here, self.pair.at[0, place, n], self.pair.at[1, place, n], {"shard": self.twin}
            )

    def begin(self):
        for n, src in enumerate(self.sources):
            self.sends.local(src, self.region(n, self.me), self.local_sem.at[n])
        self.forward(None, self.me, 0, True, True, self.sources)

    def step(self, step):
        for sems, cond, block, rising in (
            (self.up, self.spot - step >= 0, self.me - 2 * step, True),
            (self.down, self.spot + step < self.length, self.me + 2 * step, False),
        ):
            for n in range(len(self.sources)):
                received(cond, self.region(n, block), sems.at[0, step, n], sems.at[1, step, n], {"shard": self.twin})
            self.forward(cond, block, step, rising, not rising)
            self.arrived(cond, block, step if rising else self.length - 1 + step)

    def pair_step(self, step):
        turns = [(None, self.twin, 0)] if step == 0 else [
            (self.spot - step >= 0, self.twin - 2 * step, step),
            (self.spot + step < self.length, self.twin + 2 * step, self.length - 1 + step),
        ]
        for cond, block, place in turns:
            for n in range(len(self.sources)):
                received(
                    cond, self.region(n, block), self.pair.at[0, place, n], self.pair.at[1, place, n], {"shard": self.twin}
                )
            self.arrived(cond, block, 2 * self.length - 1 + place)


def both(first, second):
    return second if first is None else jnp.logical_and(first, second)


def line_sems(shards, arrays):
    length = shards // 2
    return [
        pltpu.SemaphoreType.DMA((2, length, arrays)),
        pltpu.SemaphoreType.DMA((2, length, arrays)),
        pltpu.SemaphoreType.DMA((2, 2 * length - 1, arrays)),
        pltpu.SemaphoreType.DMA((arrays,)),
    ]


class RepSpread:
    def __init__(self, arrays, region, cross, core, relay):
        self.arrays, self.region = arrays, region
        self.cross, self.core, self.relay = cross, core, relay
        rep = lax.axis_index("rep")
        self.rep = rep
        self.near = rep + 1 - 2 * (rep % 2)
        self.far = lax.rem(rep + 2, 4)
        self.diagonal = lax.rem(self.near + 2, 4)
        self.sends = Sends()
        self.blocks = []
        self.passed = []
        self.sources = None

    def arrived(self, cond, block, index):
        for n in self.arrays:
            here = self.region(n, self.rep, block)
            src = here if self.sources is None else self.sources[n]
            self.sends.start(
                cond, src, here, self.cross.at[0, block, n], self.cross.at[1, block, n], {"rep": self.far}
            )
            self.sends.start(
                cond, src, here, self.core.at[0, block, n], self.core.at[1, block, n], {"rep": self.near}
            )
        self.blocks.append((cond, block))

    def pass_on(self):
        for cond, block in self.blocks:
            for n in self.arrays:
                here = self.region(n, self.far, block)
                received(cond, here, self.cross.at[0, block, n], self.cross.at[1, block, n], {"rep": self.far})
                self.sends.start(
                    cond, here, here, self.relay.at[0, block, n], self.relay.at[1, block, n], {"rep": self.near}
                )
        self.passed = self.passed + self.blocks
        self.blocks = []

    def end(self):
        self.pass_on()
        for cond, block in self.passed:
            for n in self.arrays:
                for sems, part in ((self.core, self.near), (self.relay, self.diagonal)):
                    here = self.region(n, part, block)
                    received(cond, here, sems.at[0, block, n], sems.at[1, block, n], {"rep": self.near})
        self.sends.drain()


def rep_neighbours():
    rep = lax.axis_index("rep")
    return [(None, {"rep": rep + 1 - 2 * (rep % 2)}), (None, {"rep": lax.rem(rep + 2, 4)})]


def rep_sems(shards, arrays):
    return [pltpu.SemaphoreType.DMA((2, shards, arrays)) for unused in range(3)]


def part_columns(ref, part, width):
    return ref.at[:, pl.ds(pl.multiple_of(part * width, LANES), width)]


def weights_kernel(shards, qkv, small, qkv_all, small_all, up, down, pair, local_sem, cross, core, relay):
    rep = lax.axis_index("rep")
    greet(line_neighbours(shards) + rep_neighbours())
    width = qkv.shape[1] // lax.axis_size("rep")

    def part(n, owner, block):
        return small_all.at[block] if n == 1 else part_columns(qkv_all.at[block], owner, width)

    spread = RepSpread((0,), part, cross, core, relay)
    gather = LineGather(
        shards,
        (part_columns(qkv, rep, width), small),
        lambda n, block: part(n, rep, block),
        up,
        down,
        pair,
        local_sem,
        spread.arrived,
    )
    gather.begin()
    spread.sources = {0: part_columns(qkv, rep, width)}
    spread.arrived(None, gather.me, 0)
    spread.sources = None
    for step in range(gather.length):
        if step:
            gather.step(step)
        spread.pass_on()
        gather.pair_step(step)
    spread.end()
    gather.sends.drain()


def gather_weights(qkv_weight, small, shards):
    shapes = [(shards,) + qkv_weight.shape, (shards,) + small.shape]
    return pl.pallas_call(
        functools.partial(weights_kernel, shards),
        out_shape=[jax.ShapeDtypeStruct(shape, jnp.bfloat16) for shape in shapes],
        in_specs=[ANY] * 2,
        out_specs=[ANY] * 2,
        scratch_shapes=line_sems(shards, 2) + rep_sems(shards, 1),
        cost_estimate=work(0, 2e8),
        compiler_params=pltpu.CompilerParams(collective_id=1, has_side_effects=True),
    )(qkv_weight, small)


def attend_gather_kernel(
    depth,
    shards,
    experts,
    slots,
    bias,
    q_ref,
    kv_ref,
    gu_ref,
    dn_ref,
    out_ref,
    cot_ref,
    early_ref,
    o_ref,
    lse_ref,
    kv_all,
    gu_all,
    dn_all,
    out_all,
    cot_all,
    s_scr,
    p_scr,
    kv_sems,
    cot_sem,
    early_sem,
    up,
    down,
    pair,
    local_sem,
    cross,
    core,
    relay,
    cot_cross,
    cot_core,
    cot_relay,
):
    me = lax.axis_index("shard")
    rep = lax.axis_index("rep")
    member = me % TREE_DEVS
    seg_dev = kv_ref.shape[0]
    twin = me + 1 - 2 * (member % 2)
    across = me + 2 - 4 * (member // 2)
    greet(line_neighbours(shards) + rep_neighbours() + [(None, {"shard": across})])
    sends = Sends()

    def kv_block(owner):
        return kv_all.at[pl.ds(owner % TREE_DEVS * seg_dev, seg_dev)]

    own = kv_block(me)
    sends.start(None, kv_ref, own, kv_sems.at[0, 0], kv_sems.at[1, 0], {"shard": twin})
    sends.start(None, kv_ref, own, kv_sems.at[0, 1], kv_sems.at[1, 1], {"shard": across})
    width = out_ref.shape[1] // lax.axis_size("rep")
    own_experts = gu_ref.shape[0] // lax.axis_size("rep")
    early = early_ref.shape[0]

    def part(n, owner, block):
        if n == 2:
            return part_columns(out_all.at[block], owner, width)
        return dn_all.at[:, block] if n else gu_all.at[pl.ds(early, experts), block]

    spread = RepSpread((2,), part, cross, core, relay)
    gather = LineGather(
        shards,
        (
            gu_ref.at[pl.ds(rep * own_experts + own_experts // 2 - experts, experts)],
            dn_ref.at[pl.ds(rep * own_experts, own_experts // 2)],
            part_columns(out_ref, rep, width),
        ),
        lambda n, block: part(n, rep, block),
        up,
        down,
        pair,
        local_sem,
        spread.arrived,
        (2, 0, 1),
    )
    gather.begin()
    sends.local(cot_ref, cot_all.at[rep], cot_sem)
    sends.local(early_ref, gu_all.at[pl.ds(0, early)], early_sem)
    cot_spread = RepSpread((0,), lambda n, owner, block: cot_all.at[owner], cot_cross, cot_core, cot_relay)
    cot_spread.sources = (cot_ref,)
    cot_spread.arrived(None, 0, 0)
    spread.sources = {2: part_columns(out_ref, rep, width)}
    spread.arrived(None, me, 0)
    spread.sources = None
    kv_all[pl.ds(member * seg_dev, seg_dev)] = kv_ref[...]
    theirs = kv_block(twin)
    received(None, theirs, kv_sems.at[0, 0], kv_sems.at[1, 0], {"shard": twin})
    sends.start(None, theirs, theirs, kv_sems.at[0, 2], kv_sems.at[1, 2], {"shard": across})
    gather.step(1)
    gather.pair_step(0)
    received(None, kv_block(across), kv_sems.at[0, 1], kv_sems.at[1, 1], {"shard": across})
    diagonal = across + 1 - 2 * (member % 2)
    received(None, kv_block(diagonal), kv_sems.at[0, 2], kv_sems.at[1, 2], {"shard": across})
    count = seg_dev * PAIRS
    attend = functools.partial(fwd_step, depth, slots, bias, q_ref, kv_all, o_ref, lse_ref, s_scr, p_scr)
    done = 0
    for step in range(2, gather.length + 1):
        upto = count * (step - 1) // (gather.length - 1)
        lax.fori_loop(done, upto, attend, 0)
        done = upto
        if step < gather.length:
            gather.step(step)
            gather.pair_step(step - 1)
            spread.pass_on()
    cot_spread.end()
    gather.pair_step(gather.length - 1)
    spread.end()
    gather.sends.drain()
    sends.drain()


def attend_gather(slots, bias, q, kv, gate_up, down, out, cotangent, early, depth, shards, reps, experts):
    tokens = q.shape[0]
    count = tokens // SEG * PAIRS
    shapes = [
        q.shape,
        (TREE_DEVS * kv.shape[0],) + kv.shape[1:],
        (early.shape[0] + experts, shards) + gate_up.shape[1:],
        (down.shape[0] // reps // 2, shards) + down.shape[1:],
        (shards,) + out.shape,
        (reps,) + cotangent.shape,
    ]
    outs = [jax.ShapeDtypeStruct(shape, jnp.bfloat16) for shape in shapes]
    return pl.pallas_call(
        functools.partial(attend_gather_kernel, depth, shards, experts),
        out_shape=outs[:1] + [jax.ShapeDtypeStruct((count, 8, 6 * SEG), jnp.float32)] + outs[1:],
        in_specs=[SMEM, SMEM, VMEM, VMEM] + [ANY] * 3 + [VMEM] * 2,
        out_specs=[VMEM] * 3 + [ANY] * 4,
        scratch_shapes=[
            pltpu.VMEM((depth * SEG, 6 * SEG), jnp.float32),
            pltpu.VMEM((depth * SEG, 6 * SEG), jnp.bfloat16),
            pltpu.SemaphoreType.DMA((2, TREE_DEVS - 1)),
            pltpu.SemaphoreType.DMA,
            pltpu.SemaphoreType.DMA,
        ]
        + line_sems(shards, 3)
        + rep_sems(shards, 3)
        + rep_sems(1, 1),
        cost_estimate=work(2e10, 7e8),
        compiler_params=pltpu.CompilerParams(
            collective_id=2, has_side_effects=True, vmem_limit_bytes=48 * 2**20
        ),
    )(slots, bias, q, kv, gate_up, down, out, cotangent, early)


def share_kernel(chunks, rows_ref, gate_ref, rows_all, gate_all, own_sems, cross, core, relay):
    rep = lax.axis_index("rep")
    greet(rep_neighbours())
    size = rows_ref.shape[0] // chunks

    def piece(n, part, block):
        return gate_all.at[part] if n == chunks else rows_all.at[part, pl.ds(n * size, size)]

    spread = RepSpread(tuple(range(chunks + 1)), piece, cross, core, relay)
    spread.sources = [rows_ref.at[pl.ds(n * size, size)] for n in range(chunks)] + [gate_ref]
    spread.arrived(None, 0, 0)
    for n in range(chunks + 1):
        spread.sends.local(spread.sources[n], piece(n, rep, 0), own_sems.at[n])
    spread.end()


def share_rows(rows, gates, reps):
    chunks = 4
    return pl.pallas_call(
        functools.partial(share_kernel, chunks),
        out_shape=[
            jax.ShapeDtypeStruct((reps,) + rows.shape, rows.dtype),
            jax.ShapeDtypeStruct((reps,) + gates.shape, gates.dtype),
        ],
        in_specs=[VMEM] * 2,
        out_specs=[VMEM] * 2,
        scratch_shapes=[pltpu.SemaphoreType.DMA((chunks + 1,))] + rep_sems(1, chunks + 1),
        cost_estimate=work(0, 1.6e8),
        compiler_params=pltpu.CompilerParams(
            collective_id=6, has_side_effects=True, vmem_limit_bytes=32 * 2**20
        ),
    )(rows, gates)


def swap_reps(part, flip):
    return lax.ppermute(part, "rep", [(i, i ^ flip) for i in range(4)])


class LineScatter:
    def __init__(self, shards, arrays, local, pair_buf, line_buf, temp, stages, outs, pair, line, loads, ready=None):
        self.shards, self.arrays, self.local = shards, arrays, local
        self.pair_buf, self.line_buf, self.temp = pair_buf, line_buf, temp
        self.stages, self.outs = stages, outs
        self.pair, self.line, self.loads = pair, line, loads
        self.ready = ready or (lambda block: None)
        self.sends = Sends()
        self.me, self.spot, self.length = line_place(shards)
        self.side = self.me % 2
        self.twin = self.me + 1 - 2 * self.side

    def add(self, n, sources, target):
        stage, out = self.stages[n], self.outs[n]
        copies = []
        for k, (cond, ref) in enumerate(sources):
            copy = pltpu.make_async_copy(ref, stage.at[k], self.loads.at[k])
            copies.append((cond, copy))
            when(cond, copy.start)
        outer, rows, width = out.shape
        chunk = 32 if rows % 32 == 0 else rows
        pieces = rows // chunk

        def clear(k):
            def one(i, c):
                row = pl.multiple_of(i % pieces * chunk, chunk)
                stage[k, i // pieces, pl.ds(row, chunk)] = jnp.zeros((chunk, width), stage.dtype)
                return c

            lax.fori_loop(0, outer * pieces, one, 0)

        for k, (cond, copy) in enumerate(copies):
            when(cond, copy.wait)
            if cond is not None:
                pl.when(jnp.logical_not(cond))(functools.partial(clear, k))

        def one(i, c):
            row = pl.multiple_of(i % pieces * chunk, chunk)
            total = stage[0, i // pieces, pl.ds(row, chunk)].astype(jnp.float32)
            for k in range(1, len(sources)):
                total = total + stage[k, i // pieces, pl.ds(row, chunk)].astype(jnp.float32)
            out[i // pieces, pl.ds(row, chunk)] = total.astype(out.dtype)
            return c

        lax.fori_loop(0, outer * pieces, one, 0)
        store = pltpu.make_async_copy(out, target, self.loads.at[self.loads.shape[0] - 1])
        store.start()
        store.wait()

    def pick(self, turn):
        spot, last = self.spot, self.length - 1
        low = jnp.where(turn < last - spot, last - turn, turn - last + spot)
        high = jnp.where(turn < spot, turn, last - turn + spot)
        return jnp.where(turn == last, spot, jnp.where(2 * spot < self.length, low, high))

    def offer(self, turn):
        if turn >= self.length:
            return
        target = self.pick(turn)
        block = 2 * target + 1 - self.side
        self.ready(block)
        for n in range(self.arrays):
            sources = self.local(n, block)
            src = sources[0]
            if len(sources) > 1:
                src = self.temp[n].at[target]
                self.add(n, [(None, ref) for ref in sources], src)
            self.sends.start(
                None,
                src,
                self.pair_buf[n].at[target],
                self.pair.at[0, target, n],
                self.pair.at[1, target, n],
                {"shard": self.twin},
            )

    def got_pair(self, target, n):
        received(
            None,
            self.pair_buf[n].at[target],
            self.pair.at[0, target, n],
            self.pair.at[1, target, n],
            {"shard": self.twin},
        )

    def got_line(self, cond, slot, n, device):
        received(cond, self.line_buf[n].at[slot], self.line.at[0, slot, n], self.line.at[1, slot, n], {"shard": device})

    def step(self, slot):
        below, above = self.spot > 0, self.spot + 1 < self.length
        mirrored = self.length - 1 - self.spot
        turns = (
            (self.spot <= slot, self.length - 1 - slot + self.spot, True, below, self.me - 2, self.me + 2),
            (mirrored <= slot, slot - mirrored, False, above, self.me + 2, self.me - 2),
        )
        for cond, target, rising, has, source, device in turns:
            block = 2 * target + self.side
            place = target if rising else jnp.where(self.spot == target + 1, self.length, target)
            for n in range(self.arrays):
                copy = pltpu.make_async_remote_copy(
                    src_ref=self.pair_buf[n].at[target],
                    dst_ref=self.line_buf[n].at[place],
                    send_sem=self.line.at[0, place, n],
                    recv_sem=self.line.at[1, place, n],
                    device_id={"shard": device},
                    device_id_type=MESH,
                )

                def body(n=n, copy=copy, target=target, has=has, source=source, block=block):
                    self.got_pair(target, n)
                    self.got_line(has, target, n, source)
                    if n == 0:
                        self.ready(block)
                    sources = [(None, ref) for ref in self.local(n, block)]
                    sources += [(None, self.pair_buf[n].at[target]), (has, self.line_buf[n].at[target])]
                    self.add(n, sources, self.pair_buf[n].at[target])
                    copy.start()

                pl.when(cond)(body)
                self.sends.open.append((cond, copy.wait_send))

    def finish(self, targets):
        below, above = self.spot > 0, self.spot + 1 < self.length
        self.ready(self.me)
        for n in range(self.arrays):
            self.got_pair(self.spot, n)
            self.got_line(below, self.spot, n, self.me - 2)
            self.got_line(above, self.length, n, self.me + 2)
            sources = [(None, ref) for ref in self.local(n, self.me)]
            sources += [
                (None, self.pair_buf[n].at[self.spot]),
                (below, self.line_buf[n].at[self.spot]),
                (above, self.line_buf[n].at[self.length]),
            ]
            self.add(n, sources, targets[n])


def scatter_sems(shards, arrays, loads):
    length = shards // 2
    return [
        pltpu.SemaphoreType.DMA((2, length, arrays)),
        pltpu.SemaphoreType.DMA((2, length + 1, arrays)),
        pltpu.SemaphoreType.DMA((loads + 1,)),
    ]


def scatter_buffers(shards, block):
    length = shards // 2
    return [
        jax.ShapeDtypeStruct((length,) + block, jnp.bfloat16),
        jax.ShapeDtypeStruct((length + 1,) + block, jnp.bfloat16),
    ]


def back_kernel(
    depth,
    shards,
    slots,
    bias,
    inv,
    q_ref,
    kv_ref,
    o_ref,
    do_ref,
    lse_ref,
    gu_ref,
    dn_ref,
    dq_ref,
    dkv_ref,
    gu_out,
    dn_out,
    gu_pair,
    gu_line,
    dn_pair,
    dn_line,
    path,
    p_scr,
    d_scr,
    group,
    guest,
    passing,
    landed,
    gu_stage,
    dn_stage,
    gu_sum,
    dn_sum,
    kv_sems,
    pair,
    line,
    loads,
):
    me = lax.axis_index("shard")
    member = me % TREE_DEVS
    segs = q_ref.shape[0] // SEG
    twin = me + 1 - 2 * (member % 2)
    across = me + 2 - 4 * (member // 2)
    greet(line_neighbours(shards) + [(None, {"shard": across})])
    scatter = LineScatter(
        shards,
        2,
        lambda n, block: [(gu_ref, dn_ref)[n].at[:, block]],
        (gu_pair, dn_pair),
        (gu_line, dn_line),
        None,
        (gu_stage, dn_stage),
        (gu_sum, dn_sum),
        pair,
        line,
        loads,
    )
    scatter.offer(0)
    path[:, depth] = jnp.zeros((segs,) + path.shape[2:], path.dtype)
    step = functools.partial(
        bwd_step, depth, slots, bias, q_ref, kv_ref, o_ref, do_ref, lse_ref, dq_ref, path, p_scr, d_scr
    )
    count = segs * PAIRS
    cuts = (0, count * 8 // 20, count * 14 // 20, count)
    scatter.offer(1)
    lax.fori_loop(cuts[0], cuts[1], step, 0)
    scatter.step(0)
    scatter.offer(2)
    lax.fori_loop(cuts[1], cuts[2], step, 0)
    if scatter.length > 2:
        scatter.step(1)
    scatter.offer(3)
    lax.fori_loop(cuts[2], cuts[3], step, 0)
    lax.fori_loop(0, group.shape[0], functools.partial(bwd_collect, inv, path, group), 0)
    sends = Sends()
    side = member % 2
    for turn, slot in ((0, 1 - side), (1, side)):
        owner = (across - side + slot) % TREE_DEVS
        sends.start(
            None,
            group.at[pl.ds(owner * segs, segs)],
            guest.at[slot],
            kv_sems.at[0, turn],
            kv_sems.at[1, turn],
            {"shard": across},
        )

    def join(mine, slot, extra, target):
        def one(seg, c):
            for col in range(0, 2 * KVH * HD, 256):
                total = group[mine * segs + seg, :, col : col + 256].astype(jnp.float32)
                total = total + guest[slot, seg, :, col : col + 256].astype(jnp.float32)
                if extra is not None:
                    total = total + extra[seg, :, col : col + 256].astype(jnp.float32)
                target[seg, :, col : col + 256] = total.astype(target.dtype)
            return c

        lax.fori_loop(0, segs, one, 0)

    received(None, guest.at[1 - side], kv_sems.at[0, 0], kv_sems.at[1, 0], {"shard": across})
    join(twin % TREE_DEVS, 1 - side, None, passing)
    sends.start(None, passing, landed, kv_sems.at[0, 2], kv_sems.at[1, 2], {"shard": twin})
    for turn in range(2, scatter.length - 1):
        scatter.offer(turn + 2)
        scatter.step(turn)
    received(None, guest.at[side], kv_sems.at[0, 1], kv_sems.at[1, 1], {"shard": across})
    received(None, landed, kv_sems.at[0, 2], kv_sems.at[1, 2], {"shard": twin})
    join(member, side, landed, dkv_ref)
    scatter.finish((gu_out, dn_out))
    sends.drain()
    scatter.sends.drain()


def attend_back(slots, bias, inv, q, kv, o, do, lse, gate_up_grad, down_grad, depth, shards):
    segs = q.shape[0] // SEG
    own_kv = (segs,) + kv.shape[1:]
    gu_block = (gate_up_grad.shape[0],) + gate_up_grad.shape[2:]
    dn_block = (down_grad.shape[0],) + down_grad.shape[2:]
    outs = [
        jax.ShapeDtypeStruct(q.shape, jnp.bfloat16),
        jax.ShapeDtypeStruct(own_kv, jnp.bfloat16),
        jax.ShapeDtypeStruct(gu_block, jnp.bfloat16),
        jax.ShapeDtypeStruct(dn_block, jnp.bfloat16),
    ]
    outs += scatter_buffers(shards, gu_block) + scatter_buffers(shards, dn_block)
    return pl.pallas_call(
        functools.partial(back_kernel, depth, shards),
        out_shape=outs,
        in_specs=[SMEM] * 3 + [VMEM] * 5 + [ANY] * 2,
        out_specs=[VMEM] * 2 + [ANY] * 6,
        scratch_shapes=[
            pltpu.VMEM((segs, depth + 1, SEG, 2 * KVH * HD), jnp.bfloat16),
            pltpu.VMEM((depth * SEG, 6 * SEG), jnp.bfloat16),
            pltpu.VMEM((depth * SEG, 6 * SEG), jnp.bfloat16),
            pltpu.VMEM(kv.shape, jnp.bfloat16),
            pltpu.VMEM((2,) + own_kv, jnp.bfloat16),
            pltpu.VMEM(own_kv, jnp.bfloat16),
            pltpu.VMEM(own_kv, jnp.bfloat16),
            pltpu.VMEM((4,) + gu_block, jnp.bfloat16),
            pltpu.VMEM((4,) + dn_block, jnp.bfloat16),
            pltpu.VMEM(gu_block, jnp.bfloat16),
            pltpu.VMEM(dn_block, jnp.bfloat16),
            pltpu.SemaphoreType.DMA((2, TREE_DEVS - 1)),
        ]
        + scatter_sems(shards, 2, 4),
        cost_estimate=work(5e10, 7e8),
        compiler_params=pltpu.CompilerParams(
            collective_id=3, has_side_effects=True, vmem_limit_bytes=60 * 2**20
        ),
    )(slots, bias, inv, q, kv, o, do, lse, gate_up_grad, down_grad)[:4]


def finish_kernel(shards, arrays, pieces, *refs):
    refs = list(refs)

    def take(count):
        taken = refs[:count]
        del refs[:count]
        return taken

    grads = take(arrays)
    shares = take(pieces)
    outs = take(arrays)
    expert_outs = take(2)
    core_bufs = take(arrays)
    share_bufs = take(arrays)
    cross_bufs = take(arrays)
    temps = take(arrays)
    pair_bufs = take(arrays)
    line_bufs = take(arrays)
    stages = take(arrays)
    totals = take(arrays)
    core_sems, swap_sems, own_sems, cross, core, relay, pair, line, loads = refs
    rep = lax.axis_index("rep")
    near = rep + 1 - 2 * (rep % 2)
    far = lax.rem(rep + 2, 4)
    half = rep % 2
    greet(line_neighbours(shards) + rep_neighbours())
    sends = Sends()
    length = shards // 2
    side = lax.axis_index("shard") % 2

    def columns(n, ref, which):
        width = totals[n].shape[-1]
        if width == ref.shape[-1]:
            return ref
        return ref.at[:, :, pl.ds(pl.multiple_of(which * width, LANES), width)]

    experts = pieces // 2
    size = shares[0].shape[0]

    def place(n, part, block):
        return expert_outs[n // experts].at[part, pl.ds(n % experts * size, size)]

    for n in range(pieces):
        sends.local(shares[n], place(n, rep, 0), own_sems.at[n])
    spread = RepSpread(tuple(range(pieces)), place, cross, core, relay)
    spread.sources = shares
    spread.arrived(None, 0, 0)

    def ready(block):
        for n in range(arrays):
            received(
                None, core_bufs[n].at[block], core_sems.at[0, block, n], core_sems.at[1, block, n], {"rep": near}
            )

    scatter = LineScatter(
        shards,
        arrays,
        lambda n, block: [columns(n, grads[n].at[block], half), core_bufs[n].at[block]],
        pair_bufs,
        line_bufs,
        temps,
        stages,
        totals,
        pair,
        line,
        loads,
        ready,
    )
    for turn in range(length):
        for which in (1 - side, side):
            block = 2 * scatter.pick(turn) + which
            for n in range(arrays):
                sends.start(
                    None,
                    columns(n, grads[n].at[block], 1 - half),
                    core_bufs[n].at[block],
                    core_sems.at[0, block, n],
                    core_sems.at[1, block, n],
                    {"rep": near},
                )
    scatter.offer(0)
    scatter.offer(1)
    for turn in range(scatter.length - 1):
        scatter.offer(turn + 2)
        scatter.step(turn)
    scatter.finish(share_bufs)
    for n in range(arrays):
        sends.start(
            None, share_bufs[n], cross_bufs[n], swap_sems.at[0, 0, n], swap_sems.at[1, 0, n], {"rep": far}
        )
    spread.end()
    for n in range(arrays):
        received(None, cross_bufs[n], swap_sems.at[0, 0, n], swap_sems.at[1, 0, n], {"rep": far})
        mine = columns(n, outs[n], half)
        scatter.add(n, [(None, share_bufs[n]), (None, cross_bufs[n])], mine)
        if outs[n].shape != totals[n].shape:
            sends.start(None, mine, mine, swap_sems.at[0, 1, n], swap_sems.at[1, 1, n], {"rep": near})
    for n in range(arrays):
        if outs[n].shape != totals[n].shape:
            theirs = columns(n, outs[n], 1 - half)
            received(None, theirs, swap_sems.at[0, 1, n], swap_sems.at[1, 1, n], {"rep": near})
    sends.drain()
    scatter.sends.drain()


def finish_grads(grads, halved, gate_up_shares, down_shares, reps):
    shards = grads[0].shape[0]
    arrays = len(grads)
    parts = len(gate_up_shares)
    wholes = [grad.shape[1:] for grad in grads]
    blocks = [
        whole[:-1] + (whole[-1] // 2 if halve else whole[-1],) for whole, halve in zip(wholes, halved)
    ]
    experts = parts * gate_up_shares[0].shape[0]
    shapes = list(wholes)
    shapes += [(reps, experts) + gate_up_shares[0].shape[1:], (reps, experts) + down_shares[0].shape[1:]]
    shapes += [(shards,) + block for block in blocks]
    shapes += blocks + blocks
    shapes += [(shards // 2,) + block for block in blocks]
    shapes += [(shards // 2,) + block for block in blocks]
    shapes += [(shards // 2 + 1,) + block for block in blocks]
    return pl.pallas_call(
        functools.partial(finish_kernel, shards, arrays, 2 * parts),
        out_shape=[jax.ShapeDtypeStruct(shape, jnp.bfloat16) for shape in shapes],
        in_specs=[ANY] * (arrays + 2 * parts),
        out_specs=[ANY] * len(shapes),
        scratch_shapes=[pltpu.VMEM((5,) + block, jnp.bfloat16) for block in blocks]
        + [pltpu.VMEM(block, jnp.bfloat16) for block in blocks]
        + [
            pltpu.SemaphoreType.DMA((2, shards, arrays)),
            pltpu.SemaphoreType.DMA((2, 2, arrays)),
            pltpu.SemaphoreType.DMA((2 * parts,)),
        ]
        + rep_sems(1, 2 * parts)
        + scatter_sems(shards, arrays, 5),
        cost_estimate=work(0, 4e8),
        compiler_params=pltpu.CompilerParams(
            collective_id=4, has_side_effects=True, vmem_limit_bytes=32 * 2**20
        ),
    )(*grads, *gate_up_shares, *down_shares)[: arrays + 2]


def norm_rows(values, gain):
    scale_rows = lax.rsqrt(jnp.mean(values * values, axis=-1, keepdims=True) + EPS)
    return (values * scale_rows * gain, scale_rows)


def norm_back(values, scale_rows, gain, upstream):
    scaled = upstream * gain
    inner = jnp.mean(scaled * values, axis=-1, keepdims=True)
    through = scale_rows * scaled - values * (scale_rows * scale_rows * scale_rows) * inner
    gain_grad = jnp.sum(upstream * values * scale_rows, axis=0)
    return (through, gain_grad)


def table_lookup(table, index):
    positions = jnp.arange(table.shape[0], dtype=jnp.int32)
    return jnp.sum(jnp.where(index[:, None] == positions[None, :], table[None, :], 0), axis=1)


def find_slot(group_ids, wanted):
    positions = jnp.arange(group_ids.shape[0], dtype=jnp.int32)
    return jnp.sum(jnp.where(group_ids[None, :] == wanted[:, None], positions[None, :], 0), axis=1)


def ancestor_slots(local_ids, group_ids, group_parents, depth):
    flat_parents = group_parents.reshape(-1)
    tree_index = local_ids // TREE_SEGS
    current = local_ids % TREE_SEGS
    alive = jnp.ones(local_ids.shape, dtype=bool)
    slot_list = []
    alive_list = []
    for level in range(depth):
        wanted = tree_index * TREE_SEGS + current
        slot_list.append(find_slot(group_ids, wanted))
        alive_list.append(alive)
        parent_seg = table_lookup(flat_parents, wanted)
        alive = alive & (parent_seg != current)
        current = parent_seg
    return (jnp.stack(slot_list, axis=1), jnp.stack(alive_list, axis=1))


def path_levels(path_slots, path_alive, slot_count):
    depth = path_slots.shape[1]
    slots = jnp.arange(slot_count, dtype=jnp.int32)
    hit = path_alive[None] & (path_slots[None] == slots[:, None, None])
    levels = jnp.arange(depth, dtype=jnp.int32)
    return depth - jnp.sum(jnp.where(hit, depth - levels, 0), axis=2)


def row_pieces(grad, shards):
    experts, rows, width = grad.shape
    return grad.astype(jnp.bfloat16).reshape(experts, shards, rows // shards, width).transpose(1, 0, 2, 3)


def expert_grads(rows, gated, row_parts, upstream):
    row_grads = jnp.concatenate(row_parts, axis=-1)
    down_grad = jnp.einsum("etf,td->efd", gated, upstream, preferred_element_type=jnp.float32)
    gate_up_grad = jnp.einsum("td,etf->edf", rows, row_grads, preferred_element_type=jnp.float32)
    gate_up_grad = with_layout_constraint(gate_up_grad.astype(jnp.bfloat16), Layout((0, 1, 2)))
    return (gate_up_grad, down_grad)


def expert_forward(rows, gates, w_gate_up, w_down, upstream):
    gate_up = jnp.einsum("td,edf->etf", rows, w_gate_up, preferred_element_type=jnp.bfloat16)
    gate_part = gate_up[..., :FF].astype(jnp.float32)
    up_part = gate_up[..., FF:].astype(jnp.float32)
    sig_gate = jax.nn.sigmoid(gate_part)
    hidden = gate_part * sig_gate * up_part
    gated = (hidden * gates).astype(jnp.bfloat16)
    mix_part = jnp.einsum("etf,efd->td", gated, w_down, preferred_element_type=jnp.float32)
    raw_grad = jnp.einsum("td,efd->etf", upstream, w_down, preferred_element_type=jnp.float32)
    gate_grad = jnp.sum(hidden * raw_grad, axis=-1)
    hidden_grad = raw_grad * gates
    gate_grad_part = hidden_grad * up_part * sig_gate * (1.0 + gate_part * (1.0 - sig_gate))
    up_grad_part = hidden_grad * gate_part * sig_gate
    row_parts = (gate_grad_part.astype(jnp.bfloat16), up_grad_part.astype(jnp.bfloat16))
    row_grads = jnp.concatenate(row_parts, axis=-1)
    gate_up_grad, down_grad = expert_grads(rows, gated, row_parts, upstream)
    act_part = jnp.einsum("etf,edf->td", row_grads, w_gate_up, preferred_element_type=jnp.float32)
    return (mix_part, gate_grad, act_part, gate_up_grad, down_grad, gated, row_parts)


def shards(
    tokens,
    norm_gains,
    qkv_weight,
    out_weight,
    router_weight,
    gate_up_weight,
    down_weight,
    routes,
    placement,
    parents,
    cotangent,
):
    shard_index = lax.axis_index("shard")
    rep_index = lax.axis_index("rep")
    shard_count = lax.axis_size("shard")
    token_count = tokens.shape[0]
    seg_dev = token_count // SEG
    depth = TRUNK + 2
    width_q = H * HD
    width_kv = KVH * HD
    group_size = TREE_DEVS * seg_dev
    tree_count = group_size // TREE_SEGS
    member = shard_index % TREE_DEVS
    group = (rep_index * shard_count + shard_index) // TREE_DEVS
    group_ids = lax.dynamic_slice_in_dim(placement, group * group_size, group_size)
    group_parents = lax.dynamic_slice_in_dim(parents, group * tree_count, tree_count)
    local_ids = lax.dynamic_slice_in_dim(group_ids, member * seg_dev, seg_dev)
    path_slots, path_alive = ancestor_slots(local_ids, group_ids, group_parents, depth)
    rep_count = lax.axis_size("rep")
    own_experts = E // rep_count
    first_expert = rep_index * own_experts
    half = own_experts // 2
    padding = jnp.zeros((norm_gains.shape[1], LANES - E - 2), jnp.bfloat16)
    small = jnp.concatenate([router_weight, norm_gains.T, padding], axis=1)
    w_qkv, small = gather_weights(qkv_weight, small, shard_count)
    w_qkv = w_qkv.reshape(D, -1)
    small = small.reshape(D, LANES)
    w_router = small[:, :E]
    gains = small[:, E : E + 2].T
    gain_first = gains[0].astype(jnp.float32)
    gain_second = gains[1].astype(jnp.float32)
    token_values = tokens.astype(jnp.float32)
    normed_first, scale_first = norm_rows(token_values, gain_first)
    act_first = normed_first.astype(jnp.bfloat16)
    projected = jnp.dot(act_first, w_qkv, preferred_element_type=jnp.float32)
    queries = projected[:, :width_q].astype(jnp.bfloat16)
    w_gate_up_early = lax.all_gather(
        lax.dynamic_slice_in_dim(gate_up_weight, first_expert, half - 1), "shard", axis=1, tiled=True
    )
    own_kv = projected[:, width_q:].astype(jnp.bfloat16).reshape(seg_dev, SEG, 2 * width_kv)
    bias = jnp.where(path_alive, 0.0, NEG).astype(jnp.float32)
    attended, log_totals, group_kv, w_gate_up, w_down, w_out, cot_all = attend_gather(
        path_slots,
        bias,
        queries,
        own_kv,
        gate_up_weight,
        down_weight,
        out_weight,
        cotangent,
        w_gate_up_early.reshape(half - 1, shard_count, -1, 2 * FF),
        depth,
        shard_count,
        rep_count,
        1,
    )
    gate_up_late, down_late, attended = lax.optimization_barrier(
        (
            lax.dynamic_slice_in_dim(gate_up_weight, first_expert + half, half),
            lax.dynamic_slice_in_dim(down_weight, first_expert + half, half),
            attended,
        )
    )
    w_gate_up_late = lax.all_gather(gate_up_late, "shard", axis=1, tiled=True)
    w_down_late = lax.all_gather(down_late, "shard", axis=1, tiled=True)
    w_gate_up = w_gate_up.reshape(half, D, -1)
    w_down = w_down.reshape(half, FF, D)
    w_out = w_out.reshape(H * HD, D)
    cot_all = cot_all.reshape(-1, D)
    residual = token_values + jnp.dot(attended, w_out, preferred_element_type=jnp.float32)
    normed_second, scale_second = norm_rows(residual, gain_second)
    act_second = normed_second.astype(jnp.bfloat16)
    logits = jnp.dot(act_second, w_router, preferred_element_type=jnp.float32)
    expert_ids = jnp.arange(E, dtype=jnp.int32)
    picks = routes[:, :, None] == expert_ids[None, None, :]
    chosen = jnp.sum(jnp.where(picks, logits[:, None, :], 0.0), axis=-1)
    gates = jax.nn.softmax(chosen, axis=-1)
    upstream = cotangent.astype(jnp.float32)
    gate_table = jnp.sum(jnp.where(picks, gates[:, :, None], 0.0), axis=1)
    act_all, gate_all = share_rows(act_second, gate_table.T, rep_count)
    act_all = act_all.reshape(-1, D)
    own_gate = lax.dynamic_slice_in_dim(gate_all, first_expert, own_experts, axis=1)
    own_gate = own_gate.transpose(1, 0, 2).reshape(own_experts, -1, 1)
    first_half = expert_forward(act_all, own_gate[:half], w_gate_up, w_down, cot_all)
    first_half = (
        first_half[0].astype(jnp.bfloat16),
        first_half[1],
        first_half[2].astype(jnp.bfloat16),
        row_pieces(first_half[3], shard_count),
        row_pieces(first_half[4], shard_count),
    )
    first_half, w_gate_up_late, w_down_late = lax.optimization_barrier(
        (first_half, w_gate_up_late, w_down_late)
    )
    second_half = expert_forward(act_all, own_gate[half:], w_gate_up_late, w_down_late, cot_all)
    mix_part = first_half[0].astype(jnp.float32) + second_half[0]
    gate_grad_own = jnp.concatenate([first_half[1], second_half[1]], axis=0)
    gate_up_early = lax.psum_scatter(first_half[3], "shard", scatter_dimension=0, tiled=False)
    down_early = lax.psum_scatter(first_half[4], "shard", scatter_dimension=0, tiled=False)
    gate_grad_all = lax.all_gather(gate_grad_own, "rep", axis=0, tiled=True)
    gate_grad_table = lax.dynamic_slice_in_dim(
        gate_grad_all, rep_index * token_count, token_count, axis=1
    ).T
    inner_gate = jnp.sum(gate_table * gate_grad_table, axis=-1, keepdims=True)
    logit_grad = gate_table * (gate_grad_table - inner_gate)
    router_grad = jnp.dot(
        act_second.astype(jnp.float32).T,
        logit_grad,
        precision=lax.Precision.HIGHEST,
        preferred_element_type=jnp.float32,
    )
    act_part = (first_half[2].astype(jnp.float32) + second_half[2]).astype(jnp.bfloat16)
    part_at = functools.partial(
        lax.dynamic_index_in_dim, act_part.reshape(rep_count, token_count, D), axis=0, keepdims=False
    )
    near = rep_index + 1 - 2 * (rep_index % 2)
    far = lax.rem(rep_index + 2, 4)
    far_near = swap_reps(part_at(lax.rem(near + 2, 4)), 1)
    far_sum = (part_at(far).astype(jnp.float32) + far_near.astype(jnp.float32)).astype(jnp.bfloat16)
    far_sum, late_gated, late_rows = lax.optimization_barrier((far_sum, second_half[5], second_half[6]))
    far_got = swap_reps(far_sum, 2)
    gate_up_grad, down_grad = expert_grads(act_all, late_gated, late_rows, cot_all)
    own_near = swap_reps(part_at(near), 1)
    own_sum = part_at(rep_index).astype(jnp.float32) + own_near.astype(jnp.float32)
    act_second_grad = own_sum + far_got.astype(jnp.float32)
    act_second_grad = act_second_grad + jnp.dot(
        logit_grad,
        w_router.astype(jnp.float32).T,
        precision=lax.Precision.HIGHEST,
        preferred_element_type=jnp.float32,
    )
    through_second, gain_grad_second = norm_back(
        residual, scale_second, gains[1].astype(jnp.float32), act_second_grad
    )
    residual_grad = upstream + through_second
    branch_grad = residual_grad.astype(jnp.bfloat16)
    out_grad = jnp.dot(attended.T, branch_grad, preferred_element_type=jnp.float32)
    attended_grad = lax.dot_general(
        branch_grad, w_out, (((1,), (1,)), ((), ())), preferred_element_type=jnp.float32
    ).astype(jnp.bfloat16)
    attended_grad, gate_up_early, down_early = lax.optimization_barrier(
        (attended_grad, gate_up_early, down_early)
    )
    query_grad, own_grad, gate_up_share, down_share = attend_back(
        path_slots,
        bias,
        path_levels(path_slots, path_alive, group_size),
        queries,
        group_kv,
        attended,
        attended_grad,
        log_totals,
        gate_up_grad.astype(jnp.bfloat16).reshape(half, shard_count, -1, 2 * FF),
        down_grad.astype(jnp.bfloat16).reshape(half, shard_count, -1, D),
        depth,
        shard_count,
    )
    mix_part, query_grad = lax.optimization_barrier((mix_part.astype(jnp.bfloat16), query_grad))
    mixture = lax.psum_scatter(mix_part, "rep", scatter_dimension=0, tiled=True)
    block_out = (residual + mixture.astype(jnp.float32)).astype(jnp.bfloat16)
    projected_grad = jnp.concatenate(
        [query_grad, own_grad.reshape(token_count, 2 * width_kv)], axis=1
    )
    qkv_grad = jnp.dot(act_first.T, projected_grad, preferred_element_type=jnp.float32)
    act_first_grad = lax.dot_general(
        projected_grad, w_qkv, (((1,), (1,)), ((), ())), preferred_element_type=jnp.float32
    )
    through_first, gain_grad_first = norm_back(
        token_values, scale_first, gains[0].astype(jnp.float32), act_first_grad
    )
    token_grad = residual_grad + through_first
    small_grad = jnp.concatenate(
        [
            gain_grad_first[:, None],
            gain_grad_second[:, None],
            router_grad,
            jnp.zeros((D, LANES - E - 2), jnp.float32),
        ],
        axis=1,
    )
    grads = [
        grad.astype(jnp.bfloat16).reshape(shard_count, 1, D // shard_count, -1)
        for grad in (qkv_grad, out_grad, small_grad)
    ]
    qkv_grad, out_grad, small_grad, gate_up_grad, down_grad = finish_grads(
        grads, (True, True, False), (gate_up_early, gate_up_share), (down_early, down_share), rep_count
    )
    small_grad = small_grad[0].astype(jnp.float32)
    return (
        block_out,
        token_grad,
        small_grad[:, :2].T,
        qkv_grad[0].astype(jnp.float32),
        out_grad[0].astype(jnp.float32),
        small_grad[:, 2 : 2 + E],
        gate_up_grad.reshape((E,) + gate_up_grad.shape[2:]).astype(jnp.float32),
        down_grad.reshape((E,) + down_grad.shape[2:]).astype(jnp.float32),
    )


def solution(mesh):
    in_specs = (
        P(("rep", "shard"), None),
        P(None, "shard"),
        P("shard", None),
        P("shard", None),
        P("shard", None),
        P(None, "shard", None),
        P(None, "shard", None),
        P(("rep", "shard"), None),
        P(),
        P(),
        P(("rep", "shard"), None),
    )
    out_specs = (
        P(("rep", "shard"), None),
        P(("rep", "shard"), None),
        P(None, "shard"),
        P("shard", None),
        P("shard", None),
        P("shard", None),
        P(None, "shard", None),
        P(None, "shard", None),
    )
    return jax.shard_map(shards, mesh=mesh, in_specs=in_specs, out_specs=out_specs, check_vma=False)
```
